256 devices in a mesh: chrom: 128 (over z, x_lo, y, core), chan: 2 (over x_hi).
Axes of the slice: x: 4 (x_hi: 2, x_lo: 2; x = x_hi * 2 + x_lo), y: 4, z: 8, core: 2. Of those that a mesh axis runs over, the one named last changes fastest.
Arguments:
- embeddings: bfloat16 [8192, 512], P('chrom', 'chan'), may hold values from -6 to 6
- w_left: bfloat16 [512, 32], P(None, 'chan'), may hold values from -0.25 to 0.25
- w_right: bfloat16 [512, 32], P(None, 'chan'), may hold values from -0.25 to 0.25
- first_conv_weight: bfloat16 [32, 3, 3, 16], P('chan'), may hold values from -0.5 to 0.5
- second_conv_weight: bfloat16 [32, 3, 3, 16], P('chan'), may hold values from -0.5 to 0.5
- head_weight: float32 [32], P('chan'), may hold values from -1 to 1
- cotangent: bfloat16 [8192, 512], P('chrom'), may hold values from -6 to 6
- dilations: int32 [2], replicated, may hold values from 1 to 8, as said below
- chrom_ends: int32 [8], replicated, may hold values from 1 to 8192, as said below
Outputs:
- contacts: float32 [8192, 512], P('chrom')
- emb_grad: bfloat16 [8192, 512], P('chrom', 'chan')
- left_weight_grad: float32 [512, 32], P(None, 'chan')
- right_weight_grad: float32 [512, 32], P(None, 'chan')
- first_conv_grad: float32 [32, 3, 3, 16], P('chan')
- second_conv_grad: float32 [32, 3, 3, 16], P('chan')
- head_grad: float32 [32], P('chan')
The draws below stay inside these ranges and needn't reach their ends.
Inputs may be any that keep to these rules, and one draw needn't show every extreme that they name: `dilations`: one of the two convolutions has dilation 8, the other a smaller one. `chrom_ends`: strictly increasing; the last entry equals 8192.
All inputs are finite; a program needn't handle non-finite values.
Results may differ from the reference program's by a relative error of at most 0.015.
Values may be sent and summed in bfloat16 or wider, within the bound.
A program may use at most 64 MiB of HBM per device.

```python
import math
import jax
import jax.numpy as jnp
from jax import lax

D = 512
C = 32
GROUPS = 2
CG = 16
OFF = 512
LARGEST_DILATION = 8
NCHROM = 8
BINS = 8192


def draw_dilations(key, part):
    key = jax.random.fold_in(key, 4099)
    small_key = jax.random.fold_in(key, 7)
    order_key = jax.random.fold_in(key, 13)
    smaller = jax.random.randint(small_key, (), 1, LARGEST_DILATION).astype(jnp.int32)
    largest = jnp.int32(LARGEST_DILATION)
    first_big = jax.random.randint(order_key, (), 0, 2)
    return jnp.where(first_big == 1, jnp.stack([largest, smaller]), jnp.stack([smaller, largest])).astype(jnp.int32)


def draw_chrom_ends(key, part):
    key = jax.random.fold_in(key, 23)
    cut_points = jax.random.permutation(key, BINS - 1)[:NCHROM - 1] + 1
    return jnp.concatenate([jnp.sort(cut_points), jnp.array([BINS])]).astype(jnp.int32)


def levels(rng, shape, cuts, low, high):
    factor_of = 1.0
    for dim, parts in cuts:
        steps = jax.random.uniform(jax.random.fold_in(jax.random.fold_in(rng, 6), dim), (parts,), jnp.float32, low / len(cuts), high / len(cuts))
        factor_of = factor_of * jnp.repeat(jnp.exp(steps), shape[dim] // parts).reshape((-1,) + (1,) * (len(shape) - 1 - dim))
    return factor_of


def centred(stream_key, dims, deviation, bound, cuts=(), kind=jnp.bfloat16):
    values = deviation * jax.random.normal(stream_key, dims, jnp.float32)
    if cuts:
        values = values * levels(stream_key, dims, cuts, -0.22, 0.18)
    return jnp.clip(values, -bound, bound).astype(kind)


def setup_inputs(seed: int = 0) -> dict:
    keys = jax.random.split(jax.random.key(seed), 10)
    return {
        "embeddings": centred(keys[0], (BINS, D), 1.0, 6.0, ((0, 128), (1, 2))),
        "w_left": centred(keys[1], (D, C), D ** -0.5, 0.25, ((1, 2),)),
        "w_right": centred(keys[2], (D, C), D ** -0.5, 0.25, ((1, 2),)),
        "first_conv_weight": centred(keys[3], (C, 3, 3, CG), (9 * CG) ** -0.5, 0.5, ((0, 2),)),
        "second_conv_weight": centred(keys[4], (C, 3, 3, CG), (9 * CG) ** -0.5, 0.5, ((0, 2),)),
        "head_weight": centred(keys[5], (C,), C ** -0.5, 1.0, ((0, 2),), jnp.float32),
        "cotangent": centred(keys[6], (BINS, OFF), 1.0, 6.0, ((0, 128),)),
        "dilations": draw_dilations(jax.random.fold_in(keys[9], 71), 0),
        "chrom_ends": draw_chrom_ends(jax.random.fold_in(keys[9], 71), 0),
    }


INV_ROOT_TWO = 0.7071067811865476
INV_ROOT_TWO_PI = 0.3989422804014327

def gelu_value(values):
    return values * 0.5 * (1.0 + lax.erf(values * INV_ROOT_TWO))

def gelu_slope(values):
    return 0.5 * (1.0 + lax.erf(values * INV_ROOT_TWO)) + values * jnp.exp(-0.5 * values * values) * INV_ROOT_TWO_PI

def chrom_index(position, chrom_ends):
    return lax.optimization_barrier(jnp.sum((chrom_ends <= position[..., None]).astype(jnp.int32), axis=-1))

def band_valid(first_row, row_count, chrom_ends, bin_total):
    row_pos = first_row + jnp.arange(row_count, dtype=jnp.int32)[:, None]
    col_pos = row_pos + jnp.arange(OFF, dtype=jnp.int32)[None, :]
    same = chrom_index(row_pos, chrom_ends) == chrom_index(col_pos, chrom_ends)
    valid_mask = (row_pos >= 0) & (col_pos < bin_total) & same
    return valid_mask.astype(jnp.float32)

def window(padded, top_row, side_col, row_count):
    starts = (jnp.int32(0), jnp.asarray(top_row).astype(jnp.int32), jnp.asarray(side_col).astype(jnp.int32))
    return lax.dynamic_slice(padded, starts, (padded.shape[0], row_count, OFF))

def pad_field(field):
    return jnp.pad(field.astype(jnp.float32), ((0, 0), (LARGEST_DILATION, LARGEST_DILATION), (2 * LARGEST_DILATION, 2 * LARGEST_DILATION)))

def apply_convolution(weight, field, dilation):
    padded = pad_field(field)
    row_count = field.shape[1]
    result = jnp.zeros((weight.shape[0], row_count, OFF), jnp.float32)
    for row_tap, a in enumerate((-1, 0, 1)):
        for col_tap, b in enumerate((-1, 0, 1)):
            part_view = window(padded, LARGEST_DILATION + a * dilation, 2 * LARGEST_DILATION + (b - a) * dilation, row_count)
            result = result + jnp.einsum('oc,cik->oik', weight[:, row_tap, col_tap, :].astype(jnp.float32), part_view)
    return result

def convolution_transpose(weight, grad_out, dilation):
    padded = pad_field(grad_out)
    row_count = grad_out.shape[1]
    result = jnp.zeros((weight.shape[3], row_count, OFF), jnp.float32)
    for row_tap, a in enumerate((-1, 0, 1)):
        for col_tap, b in enumerate((-1, 0, 1)):
            part_view = window(padded, LARGEST_DILATION - a * dilation, 2 * LARGEST_DILATION - (b - a) * dilation, row_count)
            result = result + jnp.einsum('oc,oik->cik', weight[:, row_tap, col_tap, :].astype(jnp.float32), part_view)
    return result

def convolution_weight_gradient(grad_out, field, dilation):
    padded = pad_field(field)
    row_count = field.shape[1]
    grad_values = grad_out.astype(jnp.float32)
    rows_out = []
    for a in (-1, 0, 1):
        cols_out = []
        for b in (-1, 0, 1):
            part_view = window(padded, LARGEST_DILATION + a * dilation, 2 * LARGEST_DILATION + (b - a) * dilation, row_count)
            cols_out.append(jnp.einsum('oik,cik->oc', grad_values, part_view))
        rows_out.append(jnp.stack(cols_out, axis=1))
    return jnp.stack(rows_out, axis=1)

def reference(embeddings, w_left, w_right, first_conv_weight, second_conv_weight, head_weight, cotangent, dilations, chrom_ends):
    group_width = C // GROUPS
    first_dilation = dilations[0]
    second_dilation = dilations[1]
    left_proj = jnp.dot(embeddings, w_left, preferred_element_type=jnp.float32)
    right_proj = jnp.dot(embeddings, w_right, preferred_element_type=jnp.float32)
    valid_mask = band_valid(0, BINS, chrom_ends, BINS)
    col_index = (jnp.arange(BINS, dtype=jnp.int32)[:, None] + jnp.arange(OFF, dtype=jnp.int32)[None, :]).astype(jnp.int32)
    input_gradient = cotangent.astype(jnp.float32)

    def per_group(group_items):
        left_group, right_group, first_weight, second_weight, grouped_head = group_items
        right_pad = jnp.concatenate([right_group, jnp.zeros((OFF, group_width), jnp.float32)], axis=0)
        right_band = jnp.transpose(right_pad[col_index], (2, 0, 1))
        left_cols = left_group.T[:, :, None]
        pair_feature_map = (valid_mask * left_cols * right_band).astype(jnp.bfloat16)
        first_output_field = valid_mask * apply_convolution(first_weight, pair_feature_map, first_dilation)
        hidden_state = gelu_value(first_output_field).astype(jnp.bfloat16)
        second_output_field = valid_mask * apply_convolution(second_weight, hidden_state, second_dilation)
        field = pair_feature_map.astype(jnp.float32) + second_output_field
        contact_part = jnp.einsum('c,cik->ik', grouped_head, field)
        second_output_gradient = (valid_mask * grouped_head[:, None, None] * input_gradient).astype(jnp.bfloat16)
        hidden_gradient = convolution_transpose(second_weight, second_output_gradient, second_dilation)
        first_output_gradient = (valid_mask * gelu_slope(first_output_field) * hidden_gradient).astype(jnp.bfloat16)
        pair_gradient = grouped_head[:, None, None] * input_gradient + convolution_transpose(first_weight, first_output_gradient, first_dilation)
        second_weight_gradient = convolution_weight_gradient(second_output_gradient, hidden_state, second_dilation)
        first_weight_gradient = convolution_weight_gradient(first_output_gradient, pair_feature_map, first_dilation)
        head_part = lax.optimization_barrier(jnp.sum(field * input_gradient, axis=(1, 2)))
        left_grad = lax.optimization_barrier(jnp.sum(valid_mask * right_band * pair_gradient, axis=2)).T
        spread = valid_mask * left_cols * pair_gradient
        right_ext = jnp.zeros((group_width, BINS + OFF), jnp.float32).at[:, col_index].add(spread)
        right_grad = right_ext[:, :BINS].T
        return (contact_part, left_grad, right_grad, first_weight_gradient, second_weight_gradient, head_part)
    group_items = (jnp.transpose(left_proj.reshape(BINS, GROUPS, group_width), (1, 0, 2)), jnp.transpose(right_proj.reshape(BINS, GROUPS, group_width), (1, 0, 2)), first_conv_weight.reshape(GROUPS, group_width, 3, 3, group_width), second_conv_weight.reshape(GROUPS, group_width, 3, 3, group_width), head_weight.reshape(GROUPS, group_width))
    outputs = lax.map(per_group, group_items)
    contacts = lax.optimization_barrier(jnp.sum(outputs[0], axis=0))
    left_grad = jnp.transpose(outputs[1], (1, 0, 2)).reshape(BINS, C).astype(jnp.bfloat16)
    right_grad = jnp.transpose(outputs[2], (1, 0, 2)).reshape(BINS, C).astype(jnp.bfloat16)
    emb_grad = (jnp.dot(left_grad, w_left.T, preferred_element_type=jnp.float32) + jnp.dot(right_grad, w_right.T, preferred_element_type=jnp.float32)).astype(jnp.bfloat16)
    scale = 1.0 / math.sqrt(BINS * OFF)
    left_weight_grad = jnp.dot(embeddings.T, left_grad, preferred_element_type=jnp.float32) * scale
    right_weight_grad = jnp.dot(embeddings.T, right_grad, preferred_element_type=jnp.float32) * scale
    first_conv_grad = outputs[3].reshape(C, 3, 3, group_width) * scale
    second_conv_grad = outputs[4].reshape(C, 3, 3, group_width) * scale
    head_grad = outputs[5].reshape(C) * scale
    return (contacts, emb_grad, left_weight_grad, right_weight_grad, first_conv_grad, second_conv_grad, head_grad)
```

```python
import functools
import math

import jax
import jax.numpy as jnp
from jax import lax
from jax.experimental import pallas as pl
from jax.experimental.pallas import tpu as pltpu
from jax.sharding import PartitionSpec as P

MESH = pl.DeviceIdType.MESH
ROWS = 64
BEHIND = 9

OFF = 512
LANES = 128
TILES = OFF // LANES
TAPS = (-1, 0, 1)
INV_ROOT_TWO = 0.7071067811865476
INV_ROOT_TWO_PI = 0.3989422804014327


def lane_ids(rows):
    return lax.broadcasted_iota(jnp.int32, (rows, LANES), 1)


def shift_tiles(tiles, count, dist):
    if count == 0:
        return tiles
    lane = lane_ids(tiles[0].shape[0])
    zero = jnp.zeros_like(tiles[0])
    if count > 0:
        amount = count * dist
        rolled = [pltpu.roll(t, amount, 1) for t in tiles]
        before = [zero] + rolled[:-1]
        return [jnp.where(lane < amount, b, r) for b, r in zip(before, rolled)]
    amount = LANES + count * dist
    rolled = [pltpu.roll(t, amount, 1) for t in tiles]
    after = rolled[1:] + [zero]
    return [jnp.where(lane < amount, r, a) for r, a in zip(rolled, after)]


def local_kernel(
    ends, dil, rb, lb, cot, w1, w1t, vm, zw, head,
    contact, lg, rg, gconv, acc,
    px, gy, band, vga, z, reach,
    *, unroll,
):
    row0 = lax.axis_index("chrom") * 64 - 16
    d1 = dil[0]
    d2 = dil[1]
    big = jnp.int32(1 << 30)

    ids = lax.broadcasted_iota(jnp.int32, (96, LANES), 0) + row0
    nxt = jnp.full((96, LANES), big)
    for j in range(8):
        nxt = jnp.minimum(nxt, jnp.where(ends[j] > ids, ends[j], big))
    width = jnp.where((ids >= 0) & (nxt < big), nxt - ids, 0)
    lane96 = lane_ids(96)
    vg = [
        jnp.where(
            lane96 + t * LANES < width, cot[:, t * LANES : (t + 1) * LANES].astype(jnp.float32), 0.0
        )
        for t in range(TILES)
    ]
    for e in range(-2, 3):
        for t, tile in enumerate(shift_tiles(vg, e, d2)):
            vga[t, pl.ds(e + 2, 96, stride=8), :] = tile
    for e in range(5, 8):
        for t in range(TILES):
            vga[t, pl.ds(e, 96, stride=8), :] = jnp.zeros((96, LANES), jnp.float32)

    lane = lane_ids(16)

    def pair_row(q):
        i = row0 + q
        m = big
        for j in range(8):
            m = jnp.minimum(m, jnp.where(ends[j] > i, ends[j], big))
        n = jnp.where((i >= 0) & (m < big), m - i, 0)
        reach[q] = n
        back = lax.rem(LANES - q, LANES)
        rolled = [pltpu.roll(rb[:, t * LANES : (t + 1) * LANES], back, 1) for t in range(TILES + 1)]
        left = pltpu.roll(lb[...], back, 1)[:, 0:1]
        tiles = []
        for t in range(TILES):
            b = jnp.where(lane < LANES - q, rolled[t], rolled[t + 1])
            band[q, :, t * LANES : (t + 1) * LANES] = b
            tiles.append(jnp.where(lane + t * LANES < n, left * b, 0.0).astype(jnp.bfloat16))
        for e in range(-2, 3):
            for t, tile in enumerate(shift_tiles(tiles, -e, d1)):
                px[e + 2, q, :, t * LANES : (t + 1) * LANES] = tile

    def loop(start, count, body, init=None):
        if init is None:
            def step(s, _):
                for u in range(unroll):
                    body(start + s * unroll + u)
                return 0
            lax.fori_loop(0, count // unroll, step, 0)
            return None

        def step(s, carry):
            for u in range(unroll):
                carry = body(start + s * unroll + u, carry)
            return carry
        return lax.fori_loop(0, count // unroll, step, init)

    loop(0, 96, pair_row)

    lane512 = lax.broadcasted_iota(jnp.int32, (16, OFF), 1)

    def hidden_row(q, carry):
        g_acc, a_acc = carry
        stack = jnp.concatenate(
            [px[b - a + 2, q + a * d1] for a in TAPS for b in TAPS], axis=0
        )
        mask = lane512 < reach[q]
        first = jnp.where(mask, jnp.dot(w1[...], stack, preferred_element_type=jnp.float32), 0.0)
        cdf = 0.5 * (1.0 + lax.erf(first * INV_ROOT_TWO))
        slope = cdf + first * jnp.exp(-0.5 * first * first) * INV_ROOT_TWO_PI
        hidden = (first * cdf).astype(jnp.bfloat16)
        vstack = jnp.concatenate(
            [
                jnp.concatenate(
                    [vga[t, pl.ds(pl.multiple_of((q - a * d2) * 8, 8), 8), :] for a in TAPS], axis=0
                )
                for t in range(TILES)
            ],
            axis=1,
        ).astype(jnp.bfloat16)
        both = jnp.dot(vm[...], vstack, preferred_element_type=jnp.float32)
        grad_hidden = both[:16] + both[16:]
        gf = jnp.where(mask, slope * grad_hidden, 0.0).astype(jnp.bfloat16)
        tiles = [gf[:, t * LANES : (t + 1) * LANES] for t in range(TILES)]
        for e in range(-2, 3):
            for t, tile in enumerate(shift_tiles(tiles, e, d1)):
                gy[e + 2, q, :, t * LANES : (t + 1) * LANES] = tile
        hp = jnp.concatenate([hidden, px[2, q]], axis=0)
        zz = jnp.dot(zw[...], hp, preferred_element_type=jnp.float32)
        zz = zz[:16] + zz[16:]
        for t in range(TILES):
            z[t, pl.ds(pl.multiple_of(q * 16, 16), 16), :] = zz[:, t * LANES : (t + 1) * LANES]
        own = jnp.where((q >= 16) & (q < 80), 1.0, 0.0).astype(jnp.float32)
        last = (((1,), (1,)), ((), ()))
        g_acc = g_acc + own * lax.dot_general(gf, stack, last, preferred_element_type=jnp.float32)
        a_acc = a_acc + own * lax.dot_general(vstack, hp, last, preferred_element_type=jnp.float32)
        return g_acc, a_acc

    g_acc, a_acc = loop(
        8, 80, hidden_row, (jnp.zeros((16, 144), jnp.float32), jnp.zeros((24, 32), jnp.float32))
    )
    gconv[...] = jnp.zeros((16, 256), jnp.float32)
    gconv[:, :144] = g_acc
    acc[...] = jnp.zeros((24, LANES), jnp.float32)
    acc[:, :32] = a_acc

    lg[...] = jnp.zeros((16, LANES), jnp.float32)
    rg[...] = jnp.zeros((16, 5 * LANES), jnp.float32)

    def grad_row(q, carry):
        lg_acc, rg_acc = carry
        rr = q - 16
        stack = jnp.concatenate(
            [gy[b - a + 2, q - a * d1] for a in TAPS for b in TAPS], axis=0
        )
        grad_pair = jnp.dot(w1t[...], stack, preferred_element_type=jnp.float32)
        n = reach[q]
        left = pltpu.roll(lb[...], lax.rem(LANES - q, LANES), 1)[:, 0:1]
        prods = []
        spread = []
        for t in range(TILES):
            cols = slice(t * LANES, (t + 1) * LANES)
            g = vga[t, pl.ds(q * 8 + 2, 1), :]
            gp = jnp.where(lane + t * LANES < n, grad_pair[:, cols] + head[...] * g, 0.0)
            prods.append(gp * band[q, :, cols])
            spread.append(pltpu.roll(gp * left, rr, 1))
        total = (prods[0] + prods[1]) + (prods[2] + prods[3])
        lg_acc = jnp.where(lane == rr, jnp.sum(total, axis=1, keepdims=True), lg_acc)
        zero = jnp.zeros((16, LANES), jnp.float32)
        before = [zero] + spread
        after = spread + [zero]
        rg_acc = tuple(
            r + jnp.where(lane < rr, b, a) for r, b, a in zip(rg_acc, before, after)
        )
        return lg_acc, rg_acc

    zero = jnp.zeros((16, LANES), jnp.float32)
    lg_acc, rg_acc = loop(16, 64, grad_row, (zero, (zero,) * (TILES + 1)))
    lg[...] = lg_acc
    for t in range(TILES + 1):
        rg[:, t * LANES : (t + 1) * LANES] = rg_acc[t]

    def zrows(t, a, row):
        return z[t, pl.ds((16 + a * d2) * 16 + row, 64, stride=16), :]

    total = None
    for e in range(-2, 3):
        parts = [
            sum(zrows(t, a, (a + 1) * 3 + a + e + 1) for a in TAPS if -1 <= a + e <= 1)
            for t in range(TILES)
        ]
        parts = shift_tiles(parts, -e, d2)
        total = parts if total is None else [x + y for x, y in zip(total, parts)]
    lane64 = lane_ids(64)
    for t in range(TILES):
        contact[:, t * LANES : (t + 1) * LANES] = zrows(t, 0, 9) + jnp.where(
            lane64 + t * LANES < width[16:80], total[t], 0.0
        )


def weight_forms(first_w, second_w, head):
    w1 = first_w.reshape(16, 144)
    w1t = jnp.transpose(first_w, (3, 1, 2, 0)).reshape(16, 144)
    v = jnp.sum(second_w.astype(jnp.float32) * head[:, None, None, None], axis=0)
    def split(m):
        hi = m.astype(jnp.bfloat16)
        lo = (m - hi.astype(jnp.float32)).astype(jnp.bfloat16)
        return jnp.concatenate([hi, lo], axis=0)
    vt = jnp.transpose(v, (2, 0, 1))
    vm = jnp.concatenate(
        [jnp.pad(vt[:, a], ((0, 0), (2 - a, 3 + a))) for a in range(3)], axis=1
    )
    zw = jnp.concatenate(
        [
            jnp.pad(v.reshape(9, 16), ((0, 0), (0, 16))),
            jnp.pad(head[None], ((0, 0), (16, 0))),
            jnp.zeros((6, 32), jnp.float32),
        ],
        axis=0,
    )
    return w1, w1t, split(vm), split(zw)


def local_call(ends, dil, rb, lb, cot96, w1, w1t, vm, zw, head_col, unroll=2):
    v = pl.BlockSpec(memory_space=pltpu.VMEM)
    s = pl.BlockSpec(memory_space=pltpu.SMEM)
    f32 = jnp.float32
    return pl.pallas_call(
        functools.partial(local_kernel, unroll=unroll),
        out_shape=(
            jax.ShapeDtypeStruct((64, OFF), f32),
            jax.ShapeDtypeStruct((16, LANES), f32),
            jax.ShapeDtypeStruct((16, 5 * LANES), f32),
            jax.ShapeDtypeStruct((16, 256), f32),
            jax.ShapeDtypeStruct((24, LANES), f32),
        ),
        in_specs=[s, s] + [v] * 8,
        out_specs=[v] * 5,
        scratch_shapes=[
            pltpu.VMEM((5, 96, 16, OFF), jnp.bfloat16),
            pltpu.VMEM((5, 96, 16, OFF), jnp.bfloat16),
            pltpu.VMEM((96, 16, OFF), f32),
            pltpu.VMEM((TILES, 96 * 8, LANES), f32),
            pltpu.VMEM((TILES, 96 * 16, LANES), f32),
            pltpu.SMEM((96,), jnp.int32),
        ],
        compiler_params=pltpu.CompilerParams(vmem_limit_bytes=52 * 1024 * 1024),
    )(ends, dil, rb, lb, cot96, w1, w1t, vm, zw, head_col)


def peer(chrom, chan):
    return {"chrom": chrom, "chan": chan}


def hop(me, distance):
    count = lax.axis_size("chrom")
    return lax.rem(me + distance + count, count)


def gather_kernel(
    emb, wt, cot, full, rb, lb, cot96, wother, slots, send_sem, recv_sem,
):
    me = lax.axis_index("chrom")
    half = lax.axis_index("chan")
    other = 1 - half
    barrier = pltpu.get_barrier_semaphore()
    sources = [(hop(me, d), half) for d in range(1, BEHIND + 1)]
    sources += [(hop(me, -1), half), (me, other)]
    for chrom, chan in sources:
        pl.semaphore_signal(barrier, inc=1, device_id=peer(chrom, chan), device_id_type=MESH)
    pl.semaphore_wait(barrier, len(sources))

    def copy(index, src, dst, chrom, chan):
        c = pltpu.make_async_remote_copy(
            src_ref=src, dst_ref=dst, send_sem=send_sem.at[index], recv_sem=recv_sem.at[index],
            device_id=peer(chrom, chan), device_id_type=MESH,
        )
        c.start()
        return c

    mine = pl.ds(pl.multiple_of(half * 256, 256), 256)
    theirs = pl.ds(pl.multiple_of(other * 256, 256), 256)
    first = copy(0, emb, full.at[:, mine], me, other)
    rest = [
        copy(1, wt.at[:, theirs], wother, me, other),
        copy(2, cot.at[pl.ds(48, 16)], cot96.at[pl.ds(0, 16)], hop(me, 1), half),
        copy(3, cot.at[pl.ds(0, 16)], cot96.at[pl.ds(80, 16)], hop(me, -1), half),
    ]
    full[:, mine] = emb[...]
    cot96[16:80, :] = cot[...]
    first.wait_recv()
    twice = jnp.concatenate([full[...], full[...]], axis=0)
    last = (((1,), (1,)), ((), ()))
    left2 = lax.dot_general(wt[0:16, :], twice, last, preferred_element_type=jnp.float32)
    right2 = lax.dot_general(wt[16:32, :], twice, last, preferred_element_type=jnp.float32)
    lane = lane_ids(16)
    slots[1] = jnp.where(lane < ROWS, right2, left2)
    for d in range(1, BEHIND + 1):
        rest.append(copy(3 + d, slots.at[1], slots.at[1 + d], hop(me, -d), half))
    rest.append(copy(4 + BEHIND, slots.at[1], slots.at[0], hop(me, 1), half))
    first.wait_send()
    for c in rest:
        c.wait()
    for t in range(TILES + 1):
        low = pltpu.roll(slots[2 * t], 80, 1)
        mid = pltpu.roll(slots[2 * t + 1], 16, 1)
        high = pltpu.roll(slots[2 * t + 2], 80, 1)
        rb[:, t * LANES : (t + 1) * LANES] = jnp.where(
            lane < 16, low, jnp.where(lane < 80, mid, high)
        )
    lb[...] = jnp.where(
        lane < 16,
        pltpu.roll(slots[0], 16, 1),
        jnp.where(lane < 80, pltpu.roll(slots[1], 80, 1), pltpu.roll(slots[2], 16, 1)),
    )


def gather_call(emb, wt, cot):
    v = pl.BlockSpec(memory_space=pltpu.VMEM)
    f32, bf16 = jnp.float32, jnp.bfloat16
    copies = 5 + BEHIND
    return pl.pallas_call(
        gather_kernel,
        out_shape=(
            jax.ShapeDtypeStruct((ROWS, 512), bf16),
            jax.ShapeDtypeStruct((16, 5 * LANES), f32),
            jax.ShapeDtypeStruct((16, LANES), f32),
            jax.ShapeDtypeStruct((96, OFF), bf16),
            jax.ShapeDtypeStruct((32, 256), bf16),
        ),
        in_specs=[v] * 3,
        out_specs=[v] * 5,
        scratch_shapes=[
            pltpu.VMEM((BEHIND + 2, 16, LANES), f32),
            pltpu.SemaphoreType.DMA((copies,)),
            pltpu.SemaphoreType.DMA((copies,)),
        ],
        compiler_params=pltpu.CompilerParams(
            collective_id=0, has_side_effects=True, vmem_limit_bytes=16 * 1024 * 1024
        ),
    )(emb, wt, cot)


def reduce_kernel(
    scale, contact, rg, lg, gconv, acc, full, wt, wother,
    contacts, emb_grad, fin,
    csend, crecv, rsend, rrecv, lrsend, lrrecv, buf, arecv, brecv, send_sem, recv_sem,
):
    me = lax.axis_index("chrom")
    half = lax.axis_index("chan")
    other = 1 - half
    place = lax.rem(me, 16)
    plane = me // 16
    base = me - place
    group = [base + lax.rem(place + s, 16) for s in range(1, 16)]
    column = [lax.rem(plane + s, 8) for s in range(1, 8)]

    barrier = pltpu.get_barrier_semaphore()
    sources = [(hop(me, -d), half) for d in range(1, 9)] + [(me, other)]
    sources += [(g, half) for g in group] + [(p * 16 + place, half) for p in column]
    for chrom, chan in sources:
        pl.semaphore_signal(barrier, inc=1, device_id=peer(chrom, chan), device_id_type=MESH)

    csend[...] = contact[...].astype(jnp.bfloat16)
    for d in range(1, 9):
        piece = rg[:, (d // 2) * LANES : (d // 2 + 1) * LANES]
        rsend[d] = pltpu.roll(piece, 64, 1) if d % 2 else piece
    pl.semaphore_wait(barrier, len(sources))

    def copy(send, recv, src, dst, chrom, chan):
        c = pltpu.make_async_remote_copy(
            src_ref=src, dst_ref=dst, send_sem=send_sem.at[send], recv_sem=recv_sem.at[recv],
            device_id=peer(chrom, chan), device_id_type=MESH,
        )
        c.start()
        return c

    rights = [
        copy(d, d, rsend.at[d], rrecv.at[d], hop(me, d), half) for d in range(1, 9)
    ]
    swap = copy(0, 0, csend, crecv, me, other)
    lane = lane_ids(16)
    for c in rights:
        c.wait()
    right = rg[:, :LANES]
    for d in range(1, 9):
        right = right + rrecv[d]
    right = jnp.where(lane < ROWS, right, 0.0)
    lrsend[...] = jnp.concatenate([lg[...], right], axis=0).astype(jnp.bfloat16)
    trade = copy(9, 9, lrsend, lrrecv, me, other)

    wpart = jnp.dot(lrsend[:, :ROWS], full[...], preferred_element_type=jnp.float32)
    for j in range(16):
        i, t = j // 4, j % 4
        buf[j, 0:8, :] = wpart[8 * i : 8 * i + 8, t * LANES : (t + 1) * LANES]
        if j < 4:
            buf[j, 8:16, :] = gconv[8 * (j // 2) : 8 * (j // 2) + 8, (j % 2) * LANES : (j % 2 + 1) * LANES]
        elif j < 7:
            buf[j, 8:16, :] = acc[8 * (j - 4) : 8 * (j - 3), :]
        else:
            buf[j, 8:16, :] = jnp.zeros((8, LANES), jnp.float32)
    stage = []
    for s in range(1, 16):
        target = lax.rem(place + s, 16)
        stage.append(copy(9 + s, 9 + s, buf.at[target], arecv.at[s], base + target, half))

    swap.wait()
    contacts[...] = csend[...].astype(jnp.float32) + crecv[...].astype(jnp.float32)
    trade.wait()
    both = jnp.concatenate([lrsend[...], lrrecv[...]], axis=0)
    mine = pl.ds(pl.multiple_of(half * 256, 256), 256)
    weights = jnp.concatenate([wt[:, mine], wother[...]], axis=0)
    grads = lax.dot_general(
        both, weights, (((0,), (0,)), ((), ())), preferred_element_type=jnp.float32
    )
    emb_grad[...] = grads[:ROWS].astype(jnp.bfloat16)

    total = buf[place]
    for s, c in enumerate(stage):
        c.wait()
        total = total + arecv[s + 1]
    brecv[plane] = total
    stage = []
    for s in range(1, 8):
        target = lax.rem(plane + s, 8)
        stage.append((s, pltpu.make_async_remote_copy(
            src_ref=brecv.at[plane], dst_ref=brecv.at[plane],
            send_sem=send_sem.at[24 + s], recv_sem=recv_sem.at[25 + plane],
            device_id=peer(target * 16 + place, half), device_id_type=MESH,
        )))
        stage[-1][1].start()
    for s, c in stage:
        c.wait_send()
        source = lax.rem(plane + s, 8)
        pltpu.make_async_remote_copy(
            src_ref=brecv.at[source], dst_ref=brecv.at[source],
            send_sem=send_sem.at[24 + s], recv_sem=recv_sem.at[25 + source],
            device_id=peer(source * 16 + place, half), device_id_type=MESH,
        ).wait_recv()
    total = brecv[0]
    for p in range(1, 8):
        total = total + brecv[p]
    fin[place] = total * scale
    stage = []
    for s in range(1, 16):
        target = lax.rem(place + s, 16)
        stage.append((s, pltpu.make_async_remote_copy(
            src_ref=fin.at[place], dst_ref=fin.at[place],
            send_sem=send_sem.at[32 + s], recv_sem=recv_sem.at[33 + place],
            device_id=peer(base + target, half), device_id_type=MESH,
        )))
        stage[-1][1].start()
    for s, c in stage:
        c.wait_send()
        source = lax.rem(place + s, 16)
        pltpu.make_async_remote_copy(
            src_ref=fin.at[source], dst_ref=fin.at[source],
            send_sem=send_sem.at[32 + s], recv_sem=recv_sem.at[33 + source],
            device_id=peer(base + source, half), device_id_type=MESH,
        ).wait_recv()


def reduce_call(scale, contact, rg, lg, gconv, acc, full, wt, wother):
    v = pl.BlockSpec(memory_space=pltpu.VMEM)
    f32, bf16 = jnp.float32, jnp.bfloat16
    return pl.pallas_call(
        functools.partial(reduce_kernel, scale),
        out_shape=(
            jax.ShapeDtypeStruct((ROWS, OFF), f32),
            jax.ShapeDtypeStruct((ROWS, 256), bf16),
            jax.ShapeDtypeStruct((16, 16, LANES), f32),
        ),
        in_specs=[v] * 8,
        out_specs=[v] * 3,
        scratch_shapes=[
            pltpu.VMEM((ROWS, OFF), bf16),
            pltpu.VMEM((ROWS, OFF), bf16),
            pltpu.VMEM((9, 16, LANES), f32),
            pltpu.VMEM((9, 16, LANES), f32),
            pltpu.VMEM((32, LANES), bf16),
            pltpu.VMEM((32, LANES), bf16),
            pltpu.VMEM((16, 16, LANES), f32),
            pltpu.VMEM((16, 16, LANES), f32),
            pltpu.VMEM((8, 16, LANES), f32),
            pltpu.SemaphoreType.DMA((49,)),
            pltpu.SemaphoreType.DMA((49,)),
        ],
        compiler_params=pltpu.CompilerParams(
            collective_id=1, has_side_effects=True, vmem_limit_bytes=16 * 1024 * 1024
        ),
    )(contact, rg, lg, gconv, acc, full, wt, wother)


def on_device(
    embeddings,
    w_left,
    w_right,
    first_conv_weight,
    second_conv_weight,
    head_weight,
    cotangent,
    dilations,
    chrom_ends,
):
    bin_total = embeddings.shape[0] * lax.axis_size("chrom")
    scale = 1.0 / math.sqrt(bin_total * OFF)
    wt = jnp.concatenate([w_left.T, w_right.T], axis=0)
    full, rb, lb, cot96, wother = gather_call(embeddings, wt, cotangent)
    forms = weight_forms(first_conv_weight, second_conv_weight, head_weight)
    head_col = jnp.broadcast_to(head_weight[:, None], (16, LANES))
    contact, lg, rg, gconv, acc = local_call(
        chrom_ends, dilations, rb, lb, cot96, *forms, head_col
    )
    contacts, emb_grad, fin = reduce_call(
        scale, contact, rg, lg, gconv, acc, full, wt, wother
    )
    weights = jnp.transpose(fin[:, :8].reshape(4, 4, 8, LANES), (0, 2, 1, 3)).reshape(32, 512)
    first_grad = jnp.transpose(fin[:4, 8:].reshape(2, 2, 8, LANES), (0, 2, 1, 3)).reshape(16, 256)
    taps = fin[4:7, 8:]
    moved = jnp.stack([taps[0, 2:5, :16], taps[1, 1:4, :16], taps[2, 0:3, :16]])
    second_grad = head_weight[:, None, None, None] * moved[None]
    head_grad = taps[1, 2, 16:32] + jnp.sum(
        second_conv_weight.astype(jnp.float32) * moved[None], axis=(1, 2, 3)
    )
    return (
        contacts,
        emb_grad,
        weights[:16].T,
        weights[16:].T,
        first_grad[:, :144].reshape(16, 3, 3, 16),
        second_grad,
        head_grad,
    )


def solution(mesh):
    in_specs = (
        P("chrom", "chan"),
        P(None, "chan"),
        P(None, "chan"),
        P("chan", None, None, None),
        P("chan", None, None, None),
        P("chan"),
        P("chrom", None),
        P(),
        P(),
    )
    out_specs = (
        P("chrom", None),
        P("chrom", "chan"),
        P(None, "chan"),
        P(None, "chan"),
        P("chan", None, None, None),
        P("chan", None, None, None),
        P("chan"),
    )
    return jax.shard_map(
        on_device, mesh=mesh, in_specs=in_specs, out_specs=out_specs, check_vma=False
    )
```

```python
import functools
import math

import jax
import jax.numpy as jnp
from jax import lax
from jax.experimental import pallas as pl
from jax.experimental.pallas import tpu as pltpu
from jax.sharding import PartitionSpec as P

MESH = pl.DeviceIdType.MESH
ROWS = 64
BEHIND = 9

OFF = 512
LANES = 128
TILES = OFF // LANES
TAPS = (-1, 0, 1)
INV_ROOT_TWO = 0.7071067811865476
INV_ROOT_TWO_PI = 0.3989422804014327


def lane_ids(rows):
    return lax.broadcasted_iota(jnp.int32, (rows, LANES), 1)


def shift_tiles(tiles, count, dist):
    if count == 0:
        return tiles
    lane = lane_ids(tiles[0].shape[0])
    zero = jnp.zeros_like(tiles[0])
    if count > 0:
        amount = count * dist
        rolled = [pltpu.roll(t, amount, 1) for t in tiles]
        before = [zero] + rolled[:-1]
        return [jnp.where(lane < amount, b, r) for b, r in zip(before, rolled)]
    amount = LANES + count * dist
    rolled = [pltpu.roll(t, amount, 1) for t in tiles]
    after = rolled[1:] + [zero]
    return [jnp.where(lane < amount, r, a) for r, a in zip(rolled, after)]


def local_kernel(
    ends, dil, rb, lb, cot, w1, w1t, vm, zw, head,
    contact, lg, rg, gconv, taps,
    acc, px, gy, hid, band, vga, z, edge, lcol,
    *, unroll, unroll3, lag=1, lag2=2,
):
    row0 = lax.axis_index("chrom") * 64 - 16
    d1 = dil[0]
    d2 = dil[1]
    big = jnp.int32(1 << 30)

    ids = lax.broadcasted_iota(jnp.int32, (96, LANES), 0) + row0
    nxt = jnp.full((96, LANES), big)
    for j in range(8):
        nxt = jnp.minimum(nxt, jnp.where(ends[j] > ids, ends[j], big))
    width = jnp.where((ids >= 0) & (nxt < big), nxt - ids, 0)
    lane96 = lane_ids(96)
    vg = [
        jnp.where(
            lane96 + t * LANES < width, cot[:, t * LANES : (t + 1) * LANES].astype(jnp.float32), 0.0
        )
        for t in range(TILES)
    ]
    for e in range(-2, 3):
        for t, tile in enumerate(shift_tiles(vg, e, d2)):
            vga[t, pl.ds(e + 2, 96, stride=8), :] = tile
    for e in range(5, 8):
        for t in range(TILES):
            vga[t, pl.ds(e, 96, stride=8), :] = jnp.zeros((96, LANES), jnp.float32)

    lane = lane_ids(16)
    for t in range(TILES):
        edge[t] = jnp.minimum(width, OFF) - t * LANES
    for q in range(96):
        lcol[q] = jnp.broadcast_to(lb[:, q : q + 1], (16, LANES))

    def masks(q):
        return [lane < edge[t, pl.ds(q, 1), :] for t in range(TILES)]

    def band_row(p):
        back = lax.rem(LANES - p, LANES)
        rolled = [pltpu.roll(rb[:, t * LANES : (t + 1) * LANES], back, 1) for t in range(TILES + 1)]
        for t in range(TILES):
            band[p, :, t * LANES : (t + 1) * LANES] = jnp.where(
                lane < LANES - p, rolled[t], rolled[t + 1]
            )

    def pair_row(q):
        left = lcol[q]
        ends_at = [edge[t, pl.ds(q, 1), :] for t in range(TILES)]
        for e in range(-2, 3):
            move = e * d1
            for t in range(TILES):
                mask = lane < ends_at[t] - move
                if e < 0 and t == 0:
                    mask = mask & (lane >= -move)
                value = left * band[q + 16 + move, :, t * LANES : (t + 1) * LANES]
                px[e + 2, q, :, t * LANES : (t + 1) * LANES] = jnp.where(
                    mask, value, 0.0
                ).astype(jnp.bfloat16)

    def loop(start, count, unroll, body, init=None):
        if init is None:
            def step(s, _):
                for u in range(unroll):
                    body(start + s * unroll + u)
                return 0
            lax.fori_loop(0, count // unroll, step, 0)
            return None

        def step(s, carry):
            for u in range(unroll):
                carry = body(start + s * unroll + u, carry)
            return carry
        return lax.fori_loop(0, count // unroll, step, init)

    loop(0, 128, unroll, band_row)
    loop(0, 96, unroll, pair_row)

    def tap_rows(q):
        return jnp.concatenate(
            [
                jnp.concatenate(
                    [vga[t, pl.ds(pl.multiple_of((q - a * d2) * 8, 8), 8), :] for a in TAPS], axis=0
                )
                for t in range(TILES)
            ],
            axis=1,
        ).astype(jnp.bfloat16)

    def hidden_dots(q):
        stack = jnp.concatenate(
            [px[b - a + 2, q + a * d1] for a in TAPS for b in TAPS], axis=0
        )
        first = jnp.dot(w1[...], stack, preferred_element_type=jnp.float32)
        return first, jnp.dot(vm[...], tap_rows(q), preferred_element_type=jnp.float32)

    def hidden_values(q, first, grad_hidden):
        mask = jnp.concatenate(masks(q), axis=1)
        first = jnp.where(mask, first, 0.0)
        cdf = 0.5 * (1.0 + lax.erf(first * INV_ROOT_TWO))
        slope = cdf + first * jnp.exp(-0.5 * first * first) * INV_ROOT_TWO_PI
        hidden = (first * cdf).astype(jnp.bfloat16)
        gf = jnp.where(mask, slope * grad_hidden, 0.0).astype(jnp.bfloat16)
        tiles = [gf[:, t * LANES : (t + 1) * LANES] for t in range(TILES)]
        for e in range(-2, 3):
            for t, tile in enumerate(shift_tiles(tiles, e, d1)):
                gy[e + 2, q, :, t * LANES : (t + 1) * LANES] = tile
        hid[q] = hidden
        return hidden

    def head_dot(q, hidden):
        hp = jnp.concatenate([hidden, px[2, q]], axis=0)
        zz = jnp.dot(zw[...], hp, preferred_element_type=jnp.float32)
        for t in range(TILES):
            z[t, pl.ds(pl.multiple_of(q * 16, 16), 16), :] = zz[:, t * LANES : (t + 1) * LANES]

    def hidden_rows(s, _):
        rows = [8 + s * unroll + u for u in range(unroll)]
        dots, values = {}, {}
        for u in range(unroll + lag + lag2):
            if u < unroll:
                dots[u] = hidden_dots(rows[u])
            if 0 <= u - lag < unroll:
                values[u - lag] = hidden_values(rows[u - lag], *dots.pop(u - lag))
            if 0 <= u - lag - lag2:
                head_dot(rows[u - lag - lag2], values.pop(u - lag - lag2))
        return 0

    lax.fori_loop(0, 80 // unroll, hidden_rows, 0)

    def grad_row(q, carry):
        lg_acc, rg_acc, w_acc = carry
        rr = q - 16
        stack = jnp.concatenate(
            [gy[b - a + 2, q - a * d1] for a in TAPS for b in TAPS], axis=0
        )
        grad_pair = jnp.dot(w1t[...], stack, preferred_element_type=jnp.float32)
        left = lcol[q]
        prods = []
        spread = []
        for t, mask in enumerate(masks(q)):
            cols = slice(t * LANES, (t + 1) * LANES)
            g = vga[t, pl.ds(q * 8 + 2, 1), :]
            gp = jnp.where(mask, grad_pair[:, cols] + head[...] * g, 0.0)
            prods.append(gp * band[q + 16, :, cols])
            spread.append(pltpu.roll(gp * left, rr, 1))
        total = (prods[0] + prods[1]) + (prods[2] + prods[3])
        lg_acc = jnp.where(lane == rr, jnp.sum(total, axis=1, keepdims=True), lg_acc)
        zero = jnp.zeros((16, LANES), jnp.float32)
        before = [zero] + spread
        after = spread + [zero]
        rg_acc = tuple(
            r + jnp.where(lane < rr, b, a) for r, b, a in zip(rg_acc, before, after)
        )
        w_acc = w_acc + lax.dot_general(
            jnp.concatenate([stack, tap_rows(q)], axis=0),
            jnp.concatenate([px[2, q], hid[q]], axis=0),
            (((1,), (1,)), ((), ())),
            preferred_element_type=jnp.float32,
        )
        return lg_acc, rg_acc, w_acc

    zero = jnp.zeros((16, LANES), jnp.float32)
    lg_acc, rg_acc, w_acc = loop(
        16, 64, unroll3, grad_row, (zero, (zero,) * (TILES + 1), jnp.zeros((168, 32), jnp.float32))
    )
    lg[...] = lg_acc
    for t in range(TILES + 1):
        rg[:, t * LANES : (t + 1) * LANES] = rg_acc[t]
    acc[...] = jnp.zeros((256, LANES), jnp.float32)
    acc[:168, :32] = w_acc
    turned = acc[...].T
    gconv[...] = turned[:16]
    taps[...] = turned[16:32, LANES:]

    def zrows(t, a, row):
        return z[t, pl.ds((16 + a * d2) * 16 + row, 64, stride=16), :]

    total = None
    for e in range(-2, 3):
        parts = [
            sum(zrows(t, a, (a + 1) * 3 + a + e + 1) for a in TAPS if -1 <= a + e <= 1)
            for t in range(TILES)
        ]
        parts = shift_tiles(parts, -e, d2)
        total = parts if total is None else [x + y for x, y in zip(total, parts)]
    lane64 = lane_ids(64)
    for t in range(TILES):
        contact[:, t * LANES : (t + 1) * LANES] = zrows(t, 0, 9) + jnp.where(
            lane64 + t * LANES < width[16:80], total[t], 0.0
        )


def weight_forms(first_w, second_w, head):
    w1 = first_w.reshape(16, 144)
    w1t = jnp.transpose(first_w, (3, 1, 2, 0)).reshape(16, 144)
    v = jnp.sum(second_w.astype(jnp.float32) * head[:, None, None, None], axis=0)
    vt = jnp.transpose(v, (2, 0, 1))
    vm = jnp.concatenate(
        [jnp.pad(vt[:, a], ((0, 0), (2 - a, 3 + a))) for a in range(3)], axis=1
    )
    zw = jnp.concatenate(
        [
            jnp.pad(v.reshape(9, 16), ((0, 0), (0, 16))),
            jnp.pad(head[None], ((0, 0), (16, 0))),
            jnp.zeros((6, 32), jnp.float32),
        ],
        axis=0,
    )
    return w1, w1t, vm.astype(jnp.bfloat16), zw.astype(jnp.bfloat16)


def local_call(ends, dil, rb, lb, cot96, w1, w1t, vm, zw, head_col, unroll=8, unroll3=8, lag=3, lag2=2):
    v = pl.BlockSpec(memory_space=pltpu.VMEM)
    s = pl.BlockSpec(memory_space=pltpu.SMEM)
    f32 = jnp.float32
    return pl.pallas_call(
        functools.partial(local_kernel, unroll=unroll, unroll3=unroll3, lag=lag, lag2=lag2),
        out_shape=(
            jax.ShapeDtypeStruct((64, OFF), f32),
            jax.ShapeDtypeStruct((16, LANES), f32),
            jax.ShapeDtypeStruct((16, 5 * LANES), f32),
            jax.ShapeDtypeStruct((16, 256), f32),
            jax.ShapeDtypeStruct((16, LANES), f32),
        ),
        in_specs=[s, s] + [v] * 8,
        out_specs=[v] * 5,
        scratch_shapes=[
            pltpu.VMEM((256, LANES), f32),
            pltpu.VMEM((5, 96, 16, OFF), jnp.bfloat16),
            pltpu.VMEM((5, 96, 16, OFF), jnp.bfloat16),
            pltpu.VMEM((96, 16, OFF), jnp.bfloat16),
            pltpu.VMEM((128, 16, OFF), f32),
            pltpu.VMEM((TILES, 96 * 8, LANES), f32),
            pltpu.VMEM((TILES, 96 * 16, LANES), f32),
            pltpu.VMEM((TILES, 96, LANES), jnp.int32),
            pltpu.VMEM((96, 16, LANES), f32),
        ],
        compiler_params=pltpu.CompilerParams(vmem_limit_bytes=52 * 1024 * 1024),
    )(ends, dil, rb, lb, cot96, w1, w1t, vm, zw, head_col)


def peer(chrom, chan):
    return {"chrom": chrom, "chan": chan}


def hop(me, distance):
    count = lax.axis_size("chrom")
    return lax.rem(me + distance + count, count)


def gather_kernel(
    emb, wt, cot, full, rb, lb, cot96, wother, slots, send_sem, recv_sem,
):
    me = lax.axis_index("chrom")
    half = lax.axis_index("chan")
    other = 1 - half
    barrier = pltpu.get_barrier_semaphore()
    sources = [(hop(me, d), half) for d in range(1, BEHIND + 1)]
    sources += [(hop(me, -1), half), (me, other)]
    for chrom, chan in sources:
        pl.semaphore_signal(barrier, inc=1, device_id=peer(chrom, chan), device_id_type=MESH)
    pl.semaphore_wait(barrier, len(sources))

    def copy(index, src, dst, chrom, chan):
        c = pltpu.make_async_remote_copy(
            src_ref=src, dst_ref=dst, send_sem=send_sem.at[index], recv_sem=recv_sem.at[index],
            device_id=peer(chrom, chan), device_id_type=MESH,
        )
        c.start()
        return c

    mine = pl.ds(pl.multiple_of(half * 256, 256), 256)
    theirs = pl.ds(pl.multiple_of(other * 256, 256), 256)
    first = copy(0, emb, full.at[:, mine], me, other)
    rest = [
        copy(1, wt.at[:, theirs], wother, me, other),
        copy(2, cot.at[pl.ds(48, 16)], cot96.at[pl.ds(0, 16)], hop(me, 1), half),
        copy(3, cot.at[pl.ds(0, 16)], cot96.at[pl.ds(80, 16)], hop(me, -1), half),
    ]
    full[:, mine] = emb[...]
    cot96[16:80, :] = cot[...]
    first.wait_recv()
    twice = jnp.concatenate([full[...], full[...]], axis=0)
    last = (((1,), (1,)), ((), ()))
    left2 = lax.dot_general(wt[0:16, :], twice, last, preferred_element_type=jnp.float32)
    right2 = lax.dot_general(wt[16:32, :], twice, last, preferred_element_type=jnp.float32)
    lane = lane_ids(16)
    slots[1] = jnp.where(lane < ROWS, right2, left2)
    for d in range(1, BEHIND + 1):
        rest.append(copy(3 + d, slots.at[1], slots.at[1 + d], hop(me, -d), half))
    rest.append(copy(4 + BEHIND, slots.at[1], slots.at[0], hop(me, 1), half))
    first.wait_send()
    for c in rest:
        c.wait()
    for t in range(TILES + 1):
        low = pltpu.roll(slots[2 * t], 96, 1)
        mid = pltpu.roll(slots[2 * t + 1], 32, 1)
        high = pltpu.roll(slots[2 * t + 2], 96, 1)
        rb[:, t * LANES : (t + 1) * LANES] = jnp.where(
            lane < 32, low, jnp.where(lane < 96, mid, high)
        )
    lb[...] = jnp.where(
        lane < 16,
        pltpu.roll(slots[0], 16, 1),
        jnp.where(lane < 80, pltpu.roll(slots[1], 80, 1), pltpu.roll(slots[2], 16, 1)),
    )


def gather_call(emb, wt, cot):
    v = pl.BlockSpec(memory_space=pltpu.VMEM)
    f32, bf16 = jnp.float32, jnp.bfloat16
    copies = 5 + BEHIND
    return pl.pallas_call(
        gather_kernel,
        out_shape=(
            jax.ShapeDtypeStruct((ROWS, 512), bf16),
            jax.ShapeDtypeStruct((16, 5 * LANES), f32),
            jax.ShapeDtypeStruct((16, LANES), f32),
            jax.ShapeDtypeStruct((96, OFF), bf16),
            jax.ShapeDtypeStruct((32, 256), bf16),
        ),
        in_specs=[v] * 3,
        out_specs=[v] * 5,
        scratch_shapes=[
            pltpu.VMEM((BEHIND + 2, 16, LANES), f32),
            pltpu.SemaphoreType.DMA((copies,)),
            pltpu.SemaphoreType.DMA((copies,)),
        ],
        compiler_params=pltpu.CompilerParams(
            collective_id=0, has_side_effects=True, vmem_limit_bytes=16 * 1024 * 1024
        ),
    )(emb, wt, cot)


def reduce_kernel(
    scale, contact, rg, lg, gconv, taps, full, wt, wother,
    contacts, emb_grad, fin,
    csend, crecv, rsend, rrecv, lrsend, lrrecv, buf, arecv, brecv, send_sem, recv_sem,
):
    me = lax.axis_index("chrom")
    half = lax.axis_index("chan")
    other = 1 - half
    place = lax.rem(me, 16)
    plane = me // 16
    base = me - place
    group = [base + lax.rem(place + s, 16) for s in range(1, 16)]
    column = [lax.rem(plane + s, 8) for s in range(1, 8)]

    barrier = pltpu.get_barrier_semaphore()
    sources = [(hop(me, -d), half) for d in range(1, 9)] + [(me, other)]
    sources += [(g, half) for g in group] + [(p * 16 + place, half) for p in column]
    for chrom, chan in sources:
        pl.semaphore_signal(barrier, inc=1, device_id=peer(chrom, chan), device_id_type=MESH)

    csend[...] = contact[...].astype(jnp.bfloat16)
    for d in range(1, 9):
        piece = rg[:, (d // 2) * LANES : (d // 2 + 1) * LANES]
        rsend[d] = pltpu.roll(piece, 64, 1) if d % 2 else piece
    pl.semaphore_wait(barrier, len(sources))

    def copy(send, recv, src, dst, chrom, chan):
        c = pltpu.make_async_remote_copy(
            src_ref=src, dst_ref=dst, send_sem=send_sem.at[send], recv_sem=recv_sem.at[recv],
            device_id=peer(chrom, chan), device_id_type=MESH,
        )
        c.start()
        return c

    rights = [
        copy(d, d, rsend.at[d], rrecv.at[d], hop(me, d), half) for d in range(1, 9)
    ]
    swap = copy(0, 0, csend, crecv, me, other)
    lane = lane_ids(16)
    for c in rights:
        c.wait()
    right = rg[:, :LANES]
    for d in range(1, 9):
        right = right + rrecv[d]
    right = jnp.where(lane < ROWS, right, 0.0)
    lrsend[...] = jnp.concatenate([lg[...], right], axis=0).astype(jnp.bfloat16)
    trade = copy(9, 9, lrsend, lrrecv, me, other)

    wpart = jnp.dot(lrsend[:, :ROWS], full[...], preferred_element_type=jnp.float32)
    for j in range(16):
        i, t = j // 4, j % 4
        buf[j, 0:8, :] = wpart[8 * i : 8 * i + 8, t * LANES : (t + 1) * LANES]
        if j < 4:
            buf[j, 8:16, :] = gconv[8 * (j // 2) : 8 * (j // 2) + 8, (j % 2) * LANES : (j % 2 + 1) * LANES]
        elif j < 6:
            buf[j, 8:16, :] = taps[8 * (j - 4) : 8 * (j - 3), :]
        else:
            buf[j, 8:16, :] = jnp.zeros((8, LANES), jnp.float32)
    stage = []
    for s in range(1, 16):
        target = lax.rem(place + s, 16)
        stage.append(copy(9 + s, 9 + s, buf.at[target], arecv.at[s], base + target, half))

    swap.wait()
    contacts[...] = csend[...].astype(jnp.float32) + crecv[...].astype(jnp.float32)
    trade.wait()
    both = jnp.concatenate([lrsend[...], lrrecv[...]], axis=0)
    mine = pl.ds(pl.multiple_of(half * 256, 256), 256)
    weights = jnp.concatenate([wt[:, mine], wother[...]], axis=0)
    grads = lax.dot_general(
        both, weights, (((0,), (0,)), ((), ())), preferred_element_type=jnp.float32
    )
    emb_grad[...] = grads[:ROWS].astype(jnp.bfloat16)

    total = buf[place]
    for s, c in enumerate(stage):
        c.wait()
        total = total + arecv[s + 1]
    brecv[plane] = total
    stage = []
    for s in range(1, 8):
        target = lax.rem(plane + s, 8)
        stage.append((s, pltpu.make_async_remote_copy(
            src_ref=brecv.at[plane], dst_ref=brecv.at[plane],
            send_sem=send_sem.at[24 + s], recv_sem=recv_sem.at[25 + plane],
            device_id=peer(target * 16 + place, half), device_id_type=MESH,
        )))
        stage[-1][1].start()
    for s, c in stage:
        c.wait_send()
        source = lax.rem(plane + s, 8)
        pltpu.make_async_remote_copy(
            src_ref=brecv.at[source], dst_ref=brecv.at[source],
            send_sem=send_sem.at[24 + s], recv_sem=recv_sem.at[25 + source],
            device_id=peer(source * 16 + place, half), device_id_type=MESH,
        ).wait_recv()
    total = brecv[0]
    for p in range(1, 8):
        total = total + brecv[p]
    fin[place] = total * scale
    stage = []
    for s in range(1, 16):
        target = lax.rem(place + s, 16)
        stage.append((s, pltpu.make_async_remote_copy(
            src_ref=fin.at[place], dst_ref=fin.at[place],
            send_sem=send_sem.at[32 + s], recv_sem=recv_sem.at[33 + place],
            device_id=peer(base + target, half), device_id_type=MESH,
        )))
        stage[-1][1].start()
    for s, c in stage:
        c.wait_send()
        source = lax.rem(place + s, 16)
        pltpu.make_async_remote_copy(
            src_ref=fin.at[source], dst_ref=fin.at[source],
            send_sem=send_sem.at[32 + s], recv_sem=recv_sem.at[33 + source],
            device_id=peer(base + source, half), device_id_type=MESH,
        ).wait_recv()


def reduce_call(scale, contact, rg, lg, gconv, taps, full, wt, wother):
    v = pl.BlockSpec(memory_space=pltpu.VMEM)
    f32, bf16 = jnp.float32, jnp.bfloat16
    return pl.pallas_call(
        functools.partial(reduce_kernel, scale),
        out_shape=(
            jax.ShapeDtypeStruct((ROWS, OFF), f32),
            jax.ShapeDtypeStruct((ROWS, 256), bf16),
            jax.ShapeDtypeStruct((16, 16, LANES), f32),
        ),
        in_specs=[v] * 8,
        out_specs=[v] * 3,
        scratch_shapes=[
            pltpu.VMEM((ROWS, OFF), bf16),
            pltpu.VMEM((ROWS, OFF), bf16),
            pltpu.VMEM((9, 16, LANES), f32),
            pltpu.VMEM((9, 16, LANES), f32),
            pltpu.VMEM((32, LANES), bf16),
            pltpu.VMEM((32, LANES), bf16),
            pltpu.VMEM((16, 16, LANES), f32),
            pltpu.VMEM((16, 16, LANES), f32),
            pltpu.VMEM((8, 16, LANES), f32),
            pltpu.SemaphoreType.DMA((49,)),
            pltpu.SemaphoreType.DMA((49,)),
        ],
        compiler_params=pltpu.CompilerParams(
            collective_id=1, has_side_effects=True, vmem_limit_bytes=16 * 1024 * 1024
        ),
    )(contact, rg, lg, gconv, taps, full, wt, wother)


def on_device(
    embeddings,
    w_left,
    w_right,
    first_conv_weight,
    second_conv_weight,
    head_weight,
    cotangent,
    dilations,
    chrom_ends,
):
    bin_total = embeddings.shape[0] * lax.axis_size("chrom")
    scale = 1.0 / math.sqrt(bin_total * OFF)
    wt = jnp.concatenate([w_left.T, w_right.T], axis=0)
    full, rb, lb, cot96, wother = gather_call(embeddings, wt, cotangent)
    forms = weight_forms(first_conv_weight, second_conv_weight, head_weight)
    head_col = jnp.broadcast_to(head_weight[:, None], (16, LANES))
    contact, lg, rg, gconv, taps = local_call(
        chrom_ends, dilations, rb, lb, cot96, *forms, head_col
    )
    contacts, emb_grad, fin = reduce_call(
        scale, contact, rg, lg, gconv, taps, full, wt, wother
    )
    weights = jnp.transpose(fin[:, :8].reshape(4, 4, 8, LANES), (0, 2, 1, 3)).reshape(32, 512)
    sums = jnp.transpose(fin[:4, 8:].reshape(2, 2, 8, LANES), (0, 2, 1, 3)).reshape(16, 256)
    first_grad = jnp.transpose(sums[:, :144].reshape(16, 3, 3, 16), (3, 1, 2, 0))
    shifts = fin[4:6, 8:].reshape(16, LANES)[:, 16:40].reshape(16, 3, 8)
    moved = jnp.stack([shifts[:, 0, 2:5].T, shifts[:, 1, 1:4].T, shifts[:, 2, 0:3].T])
    second_grad = head_weight[:, None, None, None] * moved[None]
    head_grad = sums[:, 154] + jnp.sum(
        second_conv_weight.astype(jnp.float32) * moved[None], axis=(1, 2, 3)
    )
    return (
        contacts,
        emb_grad,
        weights[:16].T,
        weights[16:].T,
        first_grad,
        second_grad,
        head_grad,
    )


def solution(mesh):
    in_specs = (
        P("chrom", "chan"),
        P(None, "chan"),
        P(None, "chan"),
        P("chan", None, None, None),
        P("chan", None, None, None),
        P("chan"),
        P("chrom", None),
        P(),
        P(),
    )
    out_specs = (
        P("chrom", None),
        P("chrom", "chan"),
        P(None, "chan"),
        P(None, "chan"),
        P("chan", None, None, None),
        P("chan", None, None, None),
        P("chan"),
    )
    return jax.shard_map(
        on_device, mesh=mesh, in_specs=in_specs, out_specs=out_specs, check_vma=False
    )
```

```python
import functools
import math

import jax
import jax.numpy as jnp
from jax import lax
from jax.experimental import pallas as pl
from jax.experimental.pallas import tpu as pltpu
from jax.sharding import PartitionSpec as P

MESH = pl.DeviceIdType.MESH
F32 = jnp.float32
BF16 = jnp.bfloat16
OFF = 512
LANES = 128
TILES = OFF // LANES
ROWS = 64
RIM = 16
SLAB = ROWS + 2 * RIM
REACH = OFF // ROWS
BEHIND = REACH + 1
TAPS = (-1, 0, 1)
BATCH = 8
GROUP = 16
PLANES = 8
INV_ROOT_TWO = 0.7071067811865476
INV_ROOT_TWO_PI = 0.3989422804014327
LAST = (((1,), (1,)), ((), ()))
FIRST = (((0,), (0,)), ((), ()))


def ids(shape, dim):
    return lax.broadcasted_iota(jnp.int32, shape, dim)


def dot(a, b, dims=(((1,), (0,)), ((), ()))):
    return lax.dot_general(a, b, dims, preferred_element_type=F32)


def cols(t):
    return slice(t * LANES, (t + 1) * LANES)


def hop(me, distance):
    count = lax.axis_size("chrom")
    return lax.rem(me + distance + count, count)


def shift_tiles(tiles, count, dist):
    if count == 0:
        return tiles
    lane = ids((tiles[0].shape[0], LANES), 1)
    zero = jnp.zeros_like(tiles[0])
    if count > 0:
        amount = count * dist
        rolled = [pltpu.roll(t, amount, 1) for t in tiles]
        before = [zero] + rolled[:-1]
        return [jnp.where(lane < amount, b, r) for b, r in zip(before, rolled)]
    amount = LANES + count * dist
    rolled = [pltpu.roll(t, amount, 1) for t in tiles]
    after = rolled[1:] + [zero]
    return [jnp.where(lane < amount, r, a) for r, a in zip(rolled, after)]


def diagonal(column, lanes):
    shape = (16, lanes)
    return jnp.sum(jnp.where(ids(shape, 0) == ids(shape, 1), column, 0.0), axis=0, keepdims=True)


def head_column(head, lanes):
    sub = ids((16, lanes), 0)
    column = jnp.zeros((16, lanes), F32)
    for o in range(16):
        column = jnp.where(sub == o, head[o], column)
    return column


def band_kernel(
    scale,
    ends, dil, head, emb, w_left, w_right, first_w, second_w, cot,
    contacts, emb_grad, fin,
    wt, wother, w1, w1t, vm, zw,
    full, ahead, slots, cot96, rb, lb, lcol, edge, vga, band, px, gy, hid, z, zs, acc,
    csend, crecv, rsend, rrecv, lrsend, lrrecv, buf, arecv, brecv,
    send_sem, recv_sem, plane_send, plane_recv, last_send, last_recv,
):
    me = lax.axis_index("chrom")
    half = lax.axis_index("chan")
    other = 1 - half
    place = lax.rem(me, GROUP)
    plane = me // GROUP
    base = me - place
    mine = pl.ds(pl.multiple_of(half * 256, 256), 256)
    theirs = pl.ds(pl.multiple_of(other * 256, 256), 256)
    d1 = dil[0]
    d2 = dil[1]
    lane = ids((16, LANES), 1)

    barrier = pltpu.get_barrier_semaphore()
    sources = [(hop(me, d), half) for d in range(1, BEHIND + 1)]
    sources += [(hop(me, -d), half) for d in range(1, REACH + 1)]
    sources += [(base + lax.rem(place + s, GROUP), half) for s in range(1, GROUP)]
    sources += [(lax.rem(plane + s, PLANES) * GROUP + place, half) for s in range(1, PLANES)]
    sources += [(me, other)]
    for chrom, chan in sources:
        pl.semaphore_signal(
            barrier, inc=1, device_id={"chrom": chrom, "chan": chan}, device_id_type=MESH
        )

    def copy(index, src, dst, chrom, chan):
        c = pltpu.make_async_remote_copy(
            src_ref=src, dst_ref=dst, send_sem=send_sem.at[index], recv_sem=recv_sem.at[index],
            device_id={"chrom": chrom, "chan": chan}, device_id_type=MESH,
        )
        c.start()
        return c

    full[:, mine] = emb[...]
    wt[0:16, :] = w_left[...]
    wt[16:32, :] = w_right[...]
    cot96[RIM : RIM + ROWS, :] = cot[...]
    pl.semaphore_wait(barrier, len(sources))

    emb_copy = copy(0, emb, full.at[:, mine], me, other)
    rims = [
        copy(1, cot.at[pl.ds(ROWS - RIM, RIM)], cot96.at[pl.ds(0, RIM)], hop(me, 1), half),
        copy(2, cot.at[pl.ds(0, RIM)], cot96.at[pl.ds(RIM + ROWS, RIM)], hop(me, -1), half),
    ]
    w_copy = copy(3, wt.at[:, theirs], wother, me, other)

    head16 = head_column(head, 16)
    sub16 = ids((16, 16), 0)
    rows = jnp.zeros((16, 16), F32)
    form = jnp.zeros((16, 144), F32)
    form_t = jnp.zeros((16, 144), F32)
    for ab in range(9):
        at = (ids((16, 144), 1) == ids((16, 144), 0) + 16 * ab).astype(BF16)
        form = form + dot(first_w[ab], at)
        form_t = form_t + dot(first_w[ab], at, FIRST)
        row = jnp.sum(head16 * second_w[ab].astype(F32), axis=0, keepdims=True)
        rows = jnp.where(sub16 == ab, row, rows)
    w1[...] = form.astype(BF16)
    w1t[...] = form_t.astype(BF16)
    head_rows = jnp.where(sub16 == 9, diagonal(head16, 16), 0.0).astype(BF16)
    rows = rows.astype(BF16)
    low = (ids((16, 32), 1) == ids((16, 32), 0)).astype(BF16)
    high = (ids((16, 32), 1) == ids((16, 32), 0) + 16).astype(BF16)
    zw[...] = (dot(rows, low) + dot(head_rows, high)).astype(BF16)
    tap = ids((16, 24), 0)
    column = tap + 4 * ((tap >= 3).astype(jnp.int32) + (tap >= 6).astype(jnp.int32)) + 2
    spot = ((ids((16, 24), 1) == column) & (tap < 9)).astype(BF16)
    vm[...] = dot(rows, spot, FIRST).astype(BF16)

    emb_copy.wait_recv()
    twice = jnp.concatenate([full[...], full[...]], axis=0)
    slots[1] = jnp.where(lane < ROWS, dot(wt[16:32, :], twice, LAST), dot(wt[0:16, :], twice, LAST))
    tiles = [
        copy(3 + d, slots.at[1], slots.at[1 + d], hop(me, -d), half)
        for d in range(1, BEHIND + 1)
    ]
    tiles.append(copy(4 + BEHIND, slots.at[1], slots.at[0], hop(me, 1), half))
    ahead[0] = full[...]
    spread_copies = [
        copy(4 + BEHIND + d, full, ahead.at[d], hop(me, -d), half)
        for d in range(1, REACH + 1)
    ]

    for c in rims:
        c.wait()
    big = jnp.int32(1 << 30)
    bins = ids((SLAB, LANES), 0) + (me * ROWS - RIM)
    stop = jnp.full((SLAB, LANES), big)
    for j in range(8):
        stop = jnp.minimum(stop, jnp.where(ends[j] > bins, ends[j], big))
    width = jnp.where((bins >= 0) & (stop < big), jnp.minimum(stop - bins, OFF), 0)
    slab_lane = ids((SLAB, LANES), 1)
    masked = []
    for t in range(TILES):
        edge[t] = width - t * LANES
        masked.append(
            jnp.where(slab_lane < width - t * LANES, cot96[:, cols(t)].astype(F32), 0.0)
        )
    for e in range(-2, 3):
        for t, tile in enumerate(shift_tiles(masked, e, d2)):
            vga[:, t, e + 2, :] = tile
    for e in range(5, 8):
        for t in range(TILES):
            vga[:, t, e, :] = jnp.zeros((SLAB, LANES), F32)

    for c in tiles:
        c.wait()
    for t in range(TILES + 1):
        before = pltpu.roll(slots[2 * t], 96, 1)
        inside = pltpu.roll(slots[2 * t + 1], 32, 1)
        after = pltpu.roll(slots[2 * t + 2], 96, 1)
        rb[:, cols(t)] = jnp.where(lane < 32, before, jnp.where(lane < 96, inside, after))
    lb[...] = jnp.where(
        lane < RIM,
        pltpu.roll(slots[0], 16, 1),
        jnp.where(lane < RIM + ROWS, pltpu.roll(slots[1], 80, 1), pltpu.roll(slots[2], 16, 1)),
    )
    for q in range(SLAB):
        lcol[q] = jnp.broadcast_to(lb[:, q : q + 1], (16, LANES))

    def masks(q):
        return [lane < edge[t, pl.ds(q, 1), :] for t in range(TILES)]

    def band_rows(s, _):
        for u in range(BATCH):
            p = s * BATCH + u
            back = lax.rem(LANES - p, LANES)
            rolled = [pltpu.roll(rb[:, cols(t)], back, 1) for t in range(TILES + 1)]
            for t in range(TILES):
                band[p, :, cols(t)] = jnp.where(lane < LANES - p, rolled[t], rolled[t + 1])
        return 0

    lax.fori_loop(0, (SLAB + 2 * RIM) // BATCH, band_rows, 0)

    def pair_rows(s, _):
        for u in range(BATCH):
            q = s * BATCH + u
            left = lcol[q]
            limits = [edge[t, pl.ds(q, 1), :] for t in range(TILES)]
            for e in range(-2, 3):
                move = e * d1
                for t in range(TILES):
                    mask = lane < limits[t] - move
                    if e < 0 and t == 0:
                        mask = mask & (lane >= -move)
                    value = left * band[q + RIM + move, :, cols(t)]
                    px[e + 2, q, :, cols(t)] = jnp.where(mask, value, 0.0).astype(BF16)
        return 0

    lax.fori_loop(0, SLAB // BATCH, pair_rows, 0)

    def tap_rows(q):
        return jnp.concatenate(
            [
                jnp.concatenate([vga[q - a * d2, t] for a in TAPS], axis=0)
                for t in range(TILES)
            ],
            axis=1,
        ).astype(BF16)

    def hidden_dots(q):
        stack = jnp.concatenate([px[b - a + 2, q + a * d1] for a in TAPS for b in TAPS], axis=0)
        return dot(w1[...], stack), dot(vm[...], tap_rows(q))

    def hidden_values(q, first, grad_hidden):
        mask = jnp.concatenate(masks(q), axis=1)
        first = jnp.where(mask, first, 0.0)
        cdf = 0.5 * (1.0 + lax.erf(first * INV_ROOT_TWO))
        slope = cdf + first * jnp.exp(-0.5 * first * first) * INV_ROOT_TWO_PI
        hidden = (first * cdf).astype(BF16)
        grad_first = jnp.where(mask, slope * grad_hidden, 0.0).astype(BF16)
        parts = [grad_first[:, cols(t)] for t in range(TILES)]
        for e in range(-2, 3):
            for t, tile in enumerate(shift_tiles(parts, e, d1)):
                gy[e + 2, q, :, cols(t)] = tile
        hid[q] = hidden
        return hidden

    def head_dot(q, hidden):
        out = dot(zw[...], jnp.concatenate([hidden, px[2, q]], axis=0))
        for t in range(TILES):
            z[q, t] = out[:, cols(t)]

    def hidden_rows(s, _):
        lag, more = 3, 2
        dots, values = {}, {}
        for u in range(BATCH + lag + more):
            q = RIM // 2 + s * BATCH + u
            if u < BATCH:
                dots[u] = hidden_dots(q)
            if 0 <= u - lag < BATCH:
                values[u - lag] = hidden_values(q - lag, *dots.pop(u - lag))
            if u >= lag + more:
                head_dot(q - lag - more, values.pop(u - lag - more))
        return 0

    lax.fori_loop(0, (ROWS + RIM) // BATCH, hidden_rows, 0)

    def grad_rows(s, carry):
        for u in range(BATCH):
            carry = grad_row(s * BATCH + u, carry)
        return carry

    head_full = head_column(head, LANES)

    def grad_row(row, carry):
        left_acc, right_acc, weight_acc = carry
        q = row + RIM
        stack = jnp.concatenate([gy[b - a + 2, q - a * d1] for a in TAPS for b in TAPS], axis=0)
        grad_pair = dot(w1t[...], stack)
        left = lcol[q]
        prods, spread = [], []
        for t, mask in enumerate(masks(q)):
            g = vga[q, t, 2:3, :]
            part = jnp.where(mask, grad_pair[:, cols(t)] + head_full * g, 0.0)
            prods.append(part * band[q + RIM, :, cols(t)])
            spread.append(pltpu.roll(part * left, row, 1))
        total = (prods[0] + prods[1]) + (prods[2] + prods[3])
        left_acc = jnp.where(lane == row, jnp.sum(total, axis=1, keepdims=True), left_acc)
        zero = jnp.zeros((16, LANES), F32)
        right_acc = tuple(
            r + jnp.where(lane < row, b, a)
            for r, b, a in zip(right_acc, [zero] + spread, spread + [zero])
        )
        weight_acc = weight_acc + dot(
            jnp.concatenate([stack, tap_rows(q)], axis=0),
            jnp.concatenate([px[2, q], hid[q]], axis=0),
            LAST,
        )
        return left_acc, right_acc, weight_acc

    zero = jnp.zeros((16, LANES), F32)
    left_grad, right_terms, weight_acc = lax.fori_loop(
        0, ROWS // BATCH, grad_rows, (zero, (zero,) * (TILES + 1), jnp.zeros((168, 32), F32))
    )

    for d in range(1, REACH + 1):
        piece = right_terms[d // 2]
        rsend[d] = pltpu.roll(piece, ROWS, 1) if d % 2 else piece
    first_copy = 5 + BEHIND + REACH
    rights = [
        copy(first_copy + d, rsend.at[d], rrecv.at[d], hop(me, d), half)
        for d in range(1, REACH + 1)
    ]

    for c in spread_copies:
        c.wait()
    left_low = left_grad.astype(BF16)
    left_part = dot(left_low[:, :ROWS], ahead[0])
    right_part = jnp.zeros((16, OFF), F32)
    for t in range(TILES):
        pair_of = jnp.concatenate([ahead[2 * t], ahead[2 * t + 1]], axis=0)
        right_part = right_part + dot(right_terms[t].astype(BF16), pair_of)
    right_part = right_part + dot(right_terms[TILES][:, :ROWS].astype(BF16), ahead[REACH])
    acc[...] = jnp.zeros((256, LANES), F32)
    acc[:168, :32] = weight_acc
    turned = acc[...].T
    for j in range(GROUP):
        part = left_part if j < 8 else right_part
        r = 8 * ((j // 4) % 2)
        buf[j, 0:8, :] = part[r : r + 8, cols(j % 4)]
        if j < 4:
            r = 8 * (j // 2)
            buf[j, 8:16, :] = turned[r : r + 8, cols(j % 2)]
        elif j < 6:
            r = 8 * (j - 2)
            buf[j, 8:16, :] = turned[r : r + 8, cols(1)]
        else:
            buf[j, 8:16, :] = jnp.zeros((8, LANES), F32)
    group_copy = first_copy + REACH
    stage = []
    for s in range(1, GROUP):
        target = lax.rem(place + s, GROUP)
        stage.append(copy(group_copy + s, buf.at[target], arecv.at[s], base + target, half))

    def align_rows(s, _):
        for u in range(BATCH):
            row = s * BATCH + u
            for n, a in enumerate(TAPS):
                for t in range(TILES):
                    zs[n, t, pl.ds(pl.multiple_of(row * 16, 16), 16), :] = z[row + RIM + a * d2, t]
        return 0

    lax.fori_loop(0, ROWS // BATCH, align_rows, 0)

    def tap_sum(t, a, row):
        return zs[a + 1, t, pl.ds(row, ROWS, stride=16), :]

    total = None
    for e in range(-2, 3):
        parts = [
            sum(tap_sum(t, a, (a + 1) * 3 + a + e + 1) for a in TAPS if -1 <= a + e <= 1)
            for t in range(TILES)
        ]
        parts = shift_tiles(parts, -e, d2)
        total = parts if total is None else [x + y for x, y in zip(total, parts)]
    own_lane = ids((ROWS, LANES), 1)
    for t in range(TILES):
        second = jnp.where(own_lane < edge[t, RIM : RIM + ROWS, :], total[t], 0.0)
        csend[:, cols(t)] = (tap_sum(t, 0, 9) + second).astype(BF16)
    swap_copy = group_copy + GROUP
    swap = copy(swap_copy, csend, crecv, me, other)

    for c in rights:
        c.wait()
    right = right_terms[0]
    for d in range(1, REACH + 1):
        right = right + rrecv[d]
    right = jnp.where(lane < ROWS, right, 0.0)
    lrsend[...] = jnp.concatenate([left_low, right.astype(BF16)], axis=0)
    trade = copy(swap_copy + 1, lrsend, lrrecv, me, other)

    total = buf[place]
    for s, c in enumerate(stage):
        c.wait()
        total = total + arecv[s + 1]
    brecv[plane] = total

    def plane_copy(s, index, target):
        return pltpu.make_async_remote_copy(
            src_ref=brecv.at[index], dst_ref=brecv.at[index],
            send_sem=plane_send.at[s], recv_sem=plane_recv.at[index],
            device_id={"chrom": target * GROUP + place, "chan": half}, device_id_type=MESH,
        )

    planes = [(s, lax.rem(plane + s, PLANES)) for s in range(1, PLANES)]
    for s, p in planes:
        plane_copy(s, plane, p).start()

    emb_copy.wait_send()
    w_copy.wait()
    trade.wait()
    both = jnp.concatenate([lrsend[...], lrrecv[...]], axis=0)
    weights = jnp.concatenate([wt[:, mine], wother[...]], axis=0)
    emb_grad[...] = dot(both, weights, FIRST)[:ROWS].astype(BF16)
    swap.wait()
    contacts[...] = csend[...].astype(F32) + crecv[...].astype(F32)

    for s, p in planes:
        plane_copy(s, plane, p).wait_send()
        plane_copy(s, p, p).wait_recv()
    total = brecv[0]
    for p in range(1, PLANES):
        total = total + brecv[p]
    fin[place] = total * scale

    def last_copy(s, index, target):
        return pltpu.make_async_remote_copy(
            src_ref=fin.at[index], dst_ref=fin.at[index],
            send_sem=last_send.at[s], recv_sem=last_recv.at[index],
            device_id={"chrom": base + target, "chan": half}, device_id_type=MESH,
        )

    others = [(s, lax.rem(place + s, GROUP)) for s in range(1, GROUP)]
    for s, p in others:
        last_copy(s, place, p).start()
    for s, p in others:
        last_copy(s, place, p).wait_send()
        last_copy(s, p, p).wait_recv()


def band_call(scale, *operands):
    v = pl.BlockSpec(memory_space=pltpu.VMEM)
    m = pl.BlockSpec(memory_space=pltpu.SMEM)
    copies = 4 + BEHIND + REACH + 1 + REACH + GROUP + 4
    dma = pltpu.SemaphoreType.DMA
    return pl.pallas_call(
        functools.partial(band_kernel, scale),
        out_shape=(
            jax.ShapeDtypeStruct((ROWS, OFF), F32),
            jax.ShapeDtypeStruct((ROWS, 256), BF16),
            jax.ShapeDtypeStruct((GROUP, 16, LANES), F32),
        ),
        in_specs=[m] * 3 + [v] * 6,
        out_specs=[v] * 3,
        scratch_shapes=[
            pltpu.VMEM((32, 512), BF16),
            pltpu.VMEM((32, 256), BF16),
            pltpu.VMEM((16, 144), BF16),
            pltpu.VMEM((16, 144), BF16),
            pltpu.VMEM((16, 24), BF16),
            pltpu.VMEM((16, 32), BF16),
            pltpu.VMEM((ROWS, 512), BF16),
            pltpu.VMEM((REACH + 1, ROWS, 512), BF16),
            pltpu.VMEM((BEHIND + 2, 16, LANES), F32),
            pltpu.VMEM((SLAB, OFF), BF16),
            pltpu.VMEM((16, OFF + LANES), F32),
            pltpu.VMEM((16, LANES), F32),
            pltpu.VMEM((SLAB, 16, LANES), F32),
            pltpu.VMEM((TILES, SLAB, LANES), jnp.int32),
            pltpu.VMEM((SLAB, TILES, 8, LANES), F32),
            pltpu.VMEM((SLAB + 2 * RIM, 16, OFF), F32),
            pltpu.VMEM((5, SLAB, 16, OFF), BF16),
            pltpu.VMEM((5, SLAB, 16, OFF), BF16),
            pltpu.VMEM((SLAB, 16, OFF), BF16),
            pltpu.VMEM((SLAB, TILES, 16, LANES), F32),
            pltpu.VMEM((3, TILES, ROWS * 16, LANES), F32),
            pltpu.VMEM((256, LANES), F32),
            pltpu.VMEM((ROWS, OFF), BF16),
            pltpu.VMEM((ROWS, OFF), BF16),
            pltpu.VMEM((REACH + 1, 16, LANES), F32),
            pltpu.VMEM((REACH + 1, 16, LANES), F32),
            pltpu.VMEM((32, LANES), BF16),
            pltpu.VMEM((32, LANES), BF16),
            pltpu.VMEM((GROUP, 16, LANES), F32),
            pltpu.VMEM((GROUP, 16, LANES), F32),
            pltpu.VMEM((PLANES, 16, LANES), F32),
            dma((copies,)),
            dma((copies,)),
            dma((PLANES,)),
            dma((PLANES,)),
            dma((GROUP,)),
            dma((GROUP,)),
        ],
        compiler_params=pltpu.CompilerParams(
            collective_id=0, has_side_effects=True, vmem_limit_bytes=56 * 1024 * 1024
        ),
    )(*operands)


def output_kernel(
    head, fin, second_w, contacts_in, emb_grad_in,
    contacts, emb_grad, left_grad, right_grad, first_grad, second_grad, head_grad, wide,
):
    contacts[...] = contacts_in[...]
    emb_grad[...] = emb_grad_in[...]
    for j in range(GROUP):
        out = left_grad if j < 8 else right_grad
        r = 8 * ((j // 4) % 2)
        out[r : r + 8, cols(j % 4)] = fin[j, 0:8, :]
    wide[...] = jnp.zeros((LANES, 3 * LANES), F32)
    for j in range(4):
        r = 8 * (j // 2)
        wide[r : r + 8, cols(j % 2)] = fin[j, 8:16, :]
    wide[0:8, cols(2)] = fin[4, 8:16, :]
    wide[8:16, cols(2)] = fin[5, 8:16, :]
    turned = wide[...].T
    head_sum = wide[0:16, 154:155]
    head16 = head_column(head, 16)
    sums = jnp.zeros((16, 16), F32)
    for ab in range(9):
        a, b = ab // 3, ab % 3
        first_grad[ab] = turned[16 * ab : 16 * ab + 16, :16]
        row = 2 * LANES + 16 + 8 * a + (b - a + 2)
        moved = turned[row : row + 1, :16]
        second_grad[ab] = head16 * moved
        sums = sums + second_w[ab].astype(F32) * moved
    total = head_sum + jnp.sum(sums, axis=1, keepdims=True)
    head_grad[...] = diagonal(jnp.broadcast_to(total, (16, 16)), 16)


def output_call(head, fin, second_w, contacts, emb_grad):
    v = pl.BlockSpec(memory_space=pltpu.VMEM)
    m = pl.BlockSpec(memory_space=pltpu.SMEM)
    return pl.pallas_call(
        output_kernel,
        out_shape=(
            jax.ShapeDtypeStruct((ROWS, OFF), F32),
            jax.ShapeDtypeStruct((ROWS, 256), BF16),
            jax.ShapeDtypeStruct((16, 512), F32),
            jax.ShapeDtypeStruct((16, 512), F32),
            jax.ShapeDtypeStruct((9, 16, 16), F32),
            jax.ShapeDtypeStruct((9, 16, 16), F32),
            jax.ShapeDtypeStruct((1, 16), F32),
        ),
        in_specs=[m] + [v] * 4,
        out_specs=[v] * 7,
        scratch_shapes=[pltpu.VMEM((LANES, 3 * LANES), F32)],
    )(head, fin, second_w, contacts, emb_grad)


def on_device(
    embeddings,
    w_left,
    w_right,
    first_conv_weight,
    second_conv_weight,
    head_weight,
    cotangent,
    dilations,
    chrom_ends,
):
    bin_total = embeddings.shape[0] * lax.axis_size("chrom")
    scale = 1.0 / math.sqrt(bin_total * OFF)
    first_w = jnp.transpose(first_conv_weight, (1, 2, 0, 3)).reshape(9, 16, 16)
    second_w = jnp.transpose(second_conv_weight, (1, 2, 0, 3)).reshape(9, 16, 16)
    contacts, emb_grad, fin = band_call(
        scale, chrom_ends, dilations, head_weight, embeddings, w_left.T, w_right.T,
        first_w, second_w, cotangent,
    )
    contacts, emb_grad, left_grad, right_grad, first_grad, second_grad, head_grad = output_call(
        head_weight, fin, second_w, contacts, emb_grad
    )
    return (
        contacts,
        emb_grad,
        left_grad.T,
        right_grad.T,
        jnp.transpose(first_grad.reshape(3, 3, 16, 16), (2, 0, 1, 3)),
        jnp.transpose(second_grad.reshape(3, 3, 16, 16), (2, 0, 1, 3)),
        head_grad.reshape(16),
    )


def solution(mesh):
    in_specs = (
        P("chrom", "chan"),
        P(None, "chan"),
        P(None, "chan"),
        P("chan", None, None, None),
        P("chan", None, None, None),
        P("chan"),
        P("chrom", None),
        P(),
        P(),
    )
    out_specs = (
        P("chrom", None),
        P("chrom", "chan"),
        P(None, "chan"),
        P(None, "chan"),
        P("chan", None, None, None),
        P("chan", None, None, None),
        P("chan"),
    )
    return jax.shard_map(
        on_device, mesh=mesh, in_specs=in_specs, out_specs=out_specs, check_vma=False
    )
```

```python
import functools
import math

import jax
import jax.numpy as jnp
from jax import lax
from jax.experimental import pallas as pl
from jax.experimental.pallas import tpu as pltpu
from jax.sharding import PartitionSpec as P

MESH = pl.DeviceIdType.MESH
F32 = jnp.float32
BF16 = jnp.bfloat16
OFF = 512
LANES = 128
TILES = OFF // LANES
ROWS = 64
RIM = 16
SLAB = ROWS + 2 * RIM
REACH = OFF // ROWS
BEHIND = REACH + 1
TAPS = (-1, 0, 1)
BATCH = 8
GROUP = 16
PLANES = 8
INV_ROOT_TWO = 0.7071067811865476
INV_ROOT_TWO_PI = 0.3989422804014327
LAST = (((1,), (1,)), ((), ()))
FIRST = (((0,), (0,)), ((), ()))


def ids(shape, dim):
    return lax.broadcasted_iota(jnp.int32, shape, dim)


def dot(a, b, dims=(((1,), (0,)), ((), ()))):
    return lax.dot_general(a, b, dims, preferred_element_type=F32)


def cols(t):
    return slice(t * LANES, (t + 1) * LANES)


def hop(me, distance):
    count = lax.axis_size("chrom")
    return lax.rem(me + distance + count, count)


def shift_tiles(tiles, count, dist):
    if count == 0:
        return tiles
    lane = ids((tiles[0].shape[0], LANES), 1)
    zero = jnp.zeros_like(tiles[0])
    if count > 0:
        amount = count * dist
        rolled = [pltpu.roll(t, amount, 1) for t in tiles]
        before = [zero] + rolled[:-1]
        return [jnp.where(lane < amount, b, r) for b, r in zip(before, rolled)]
    amount = LANES + count * dist
    rolled = [pltpu.roll(t, amount, 1) for t in tiles]
    after = rolled[1:] + [zero]
    return [jnp.where(lane < amount, r, a) for r, a in zip(rolled, after)]


def diagonal(column, lanes):
    shape = (16, lanes)
    return jnp.sum(jnp.where(ids(shape, 0) == ids(shape, 1), column, 0.0), axis=0, keepdims=True)


def head_column(head, lanes):
    sub = ids((16, lanes), 0)
    column = jnp.zeros((16, lanes), F32)
    for o in range(16):
        column = jnp.where(sub == o, head[o], column)
    return column


def band_kernel(
    scale,
    ends, dil, head, emb, w_left, w_right, first_in, second_in, cot,
    contacts, emb_grad, fin,
    wt, wother, first_w, second_w, w1, w1t, vm, zw,
    full, ahead, slots, cot96, rb, lb, lcol, edge, vga, band, px, gy, hid, z, zs, acc,
    csend, crecv, rsend, rrecv, lrsend, lrrecv, buf, arecv, brecv,
    load_sem, send_sem, recv_sem, plane_send, plane_recv, last_send, last_recv,
):
    me = lax.axis_index("chrom")
    half = lax.axis_index("chan")
    other = 1 - half
    place = lax.rem(me, GROUP)
    plane = me // GROUP
    base = me - place
    mine = pl.ds(pl.multiple_of(half * 256, 256), 256)
    theirs = pl.ds(pl.multiple_of(other * 256, 256), 256)
    d1 = dil[0]
    d2 = dil[1]
    lane = ids((16, LANES), 1)

    barrier = pltpu.get_barrier_semaphore()
    sources = [(hop(me, d), half) for d in range(1, BEHIND + 1)]
    sources += [(hop(me, -d), half) for d in range(1, REACH + 1)]
    sources += [(base + lax.rem(place + s, GROUP), half) for s in range(1, GROUP)]
    sources += [(lax.rem(plane + s, PLANES) * GROUP + place, half) for s in range(1, PLANES)]
    sources += [(me, other)]
    for chrom, chan in sources:
        pl.semaphore_signal(
            barrier, inc=1, device_id={"chrom": chrom, "chan": chan}, device_id_type=MESH
        )

    def copy(index, src, dst, chrom, chan):
        c = pltpu.make_async_remote_copy(
            src_ref=src, dst_ref=dst, send_sem=send_sem.at[index], recv_sem=recv_sem.at[index],
            device_id={"chrom": chrom, "chan": chan}, device_id_type=MESH,
        )
        c.start()
        return c

    loads = [
        pltpu.make_async_copy(src, dst, load_sem.at[n])
        for n, (src, dst) in enumerate(
            [
                (emb, full.at[:, mine]),
                (w_left, wt.at[pl.ds(0, 16)]),
                (w_right, wt.at[pl.ds(16, 16)]),
                (first_in, first_w),
                (second_in, second_w),
                (cot, cot96.at[pl.ds(RIM, ROWS)]),
            ]
        )
    ]
    for load in loads:
        load.start()
    pl.semaphore_wait(barrier, len(sources))

    emb_copy = copy(0, emb, full.at[:, mine], me, other)
    rims = [
        copy(1, cot.at[pl.ds(ROWS - RIM, RIM)], cot96.at[pl.ds(0, RIM)], hop(me, 1), half),
        copy(2, cot.at[pl.ds(0, RIM)], cot96.at[pl.ds(RIM + ROWS, RIM)], hop(me, -1), half),
    ]
    for load in loads:
        load.wait()
    w_copy = copy(3, wt.at[:, theirs], wother, me, other)

    head16 = head_column(head, 16)
    sub16 = ids((16, 16), 0)
    rows = jnp.zeros((16, 16), F32)
    form = jnp.zeros((16, 144), F32)
    form_t = jnp.zeros((16, 144), F32)
    for ab in range(9):
        at = (ids((16, 144), 1) == ids((16, 144), 0) + 16 * ab).astype(BF16)
        form = form + dot(first_w[ab], at)
        form_t = form_t + dot(first_w[ab], at, FIRST)
        row = jnp.sum(head16 * second_w[ab].astype(F32), axis=0, keepdims=True)
        rows = jnp.where(sub16 == ab, row, rows)
    w1[...] = form.astype(BF16)
    w1t[...] = form_t.astype(BF16)
    head_rows = jnp.where(sub16 == 9, diagonal(head16, 16), 0.0).astype(BF16)
    rows = rows.astype(BF16)
    low = (ids((16, 32), 1) == ids((16, 32), 0)).astype(BF16)
    high = (ids((16, 32), 1) == ids((16, 32), 0) + 16).astype(BF16)
    zw[...] = (dot(rows, low) + dot(head_rows, high)).astype(BF16)
    tap = ids((16, 24), 0)
    column = tap + 4 * ((tap >= 3).astype(jnp.int32) + (tap >= 6).astype(jnp.int32)) + 2
    spot = ((ids((16, 24), 1) == column) & (tap < 9)).astype(BF16)
    vm[...] = dot(rows, spot, FIRST).astype(BF16)

    emb_copy.wait_recv()
    twice = jnp.concatenate([full[...], full[...]], axis=0)
    slots[1] = jnp.where(lane < ROWS, dot(wt[16:32, :], twice, LAST), dot(wt[0:16, :], twice, LAST))
    tiles = [
        copy(3 + d, slots.at[1], slots.at[1 + d], hop(me, -d), half)
        for d in range(1, BEHIND + 1)
    ]
    tiles.append(copy(4 + BEHIND, slots.at[1], slots.at[0], hop(me, 1), half))
    ahead[0] = full[...]
    far_copies = [
        copy(4 + BEHIND + d, full, ahead.at[d], hop(me, -d), half)
        for d in range(2, REACH + 1, 2)
    ]

    for c in rims:
        c.wait()
    big = jnp.int32(1 << 30)
    bins = ids((SLAB, LANES), 0) + (me * ROWS - RIM)
    stop = jnp.full((SLAB, LANES), big)
    for j in range(8):
        stop = jnp.minimum(stop, jnp.where(ends[j] > bins, ends[j], big))
    width = jnp.where((bins >= 0) & (stop < big), jnp.minimum(stop - bins, OFF), 0)
    slab_lane = ids((SLAB, LANES), 1)
    masked = []
    for t in range(TILES):
        edge[t] = width - t * LANES
        masked.append(
            jnp.where(slab_lane < width - t * LANES, cot96[:, cols(t)].astype(F32), 0.0)
        )
    for e in range(-2, 3):
        for t, tile in enumerate(shift_tiles(masked, e, d2)):
            vga[:, t, e + 2, :] = tile
    for e in range(5, 8):
        for t in range(TILES):
            vga[:, t, e, :] = jnp.zeros((SLAB, LANES), F32)

    for c in tiles:
        c.wait()
    for t in range(TILES + 1):
        before = pltpu.roll(slots[2 * t], 96, 1)
        inside = pltpu.roll(slots[2 * t + 1], 32, 1)
        after = pltpu.roll(slots[2 * t + 2], 96, 1)
        rb[:, cols(t)] = jnp.where(lane < 32, before, jnp.where(lane < 96, inside, after))
    lb[...] = jnp.where(
        lane < RIM,
        pltpu.roll(slots[0], 16, 1),
        jnp.where(lane < RIM + ROWS, pltpu.roll(slots[1], 80, 1), pltpu.roll(slots[2], 16, 1)),
    )
    for q in range(SLAB):
        lcol[q] = jnp.broadcast_to(lb[:, q : q + 1], (16, LANES))

    def masks(q):
        return [lane < edge[t, pl.ds(q, 1), :] for t in range(TILES)]

    def band_row(p):
        back = lax.rem(2 * LANES - p, LANES)
        rolled = [pltpu.roll(rb[:, cols(t)], back, 1) for t in range(TILES + 1)]
        for t in range(TILES):
            band[p, :, cols(t)] = jnp.where(lane < LANES - p, rolled[t], rolled[t + 1])

    def pair_row(q):
        left = lcol[q]
        limits = [edge[t, pl.ds(q, 1), :] for t in range(TILES)]
        for e in range(-2, 3):
            move = e * d1
            for t in range(TILES):
                mask = lane < limits[t] - move
                if e < 0 and t == 0:
                    mask = mask & (lane >= -move)
                value = left * band[q + RIM + move, :, cols(t)]
                px[e + 2, q, :, cols(t)] = jnp.where(mask, value, 0.0).astype(BF16)

    def first_band_rows(s, _):
        for u in range(BATCH):
            band_row(s * BATCH + u)
        return 0

    def pair_rows(s, _):
        for u in range(BATCH):
            pair_row(s * BATCH + u)
            band_row(2 * RIM + (s + 1) * BATCH + u)
        return 0

    lax.fori_loop(0, 2 * RIM // BATCH + 1, first_band_rows, 0)
    lax.fori_loop(0, SLAB // BATCH, pair_rows, 0)

    def tap_rows(q):
        return jnp.concatenate(
            [
                jnp.concatenate([vga[q - a * d2, t] for a in TAPS], axis=0)
                for t in range(TILES)
            ],
            axis=1,
        ).astype(BF16)

    def hidden_dots(q):
        stack = jnp.concatenate([px[b - a + 2, q + a * d1] for a in TAPS for b in TAPS], axis=0)
        return dot(w1[...], stack), dot(vm[...], tap_rows(q))

    def hidden_values(q, first, grad_hidden):
        mask = jnp.concatenate(masks(q), axis=1)
        first = jnp.where(mask, first, 0.0)
        cdf = 0.5 * (1.0 + lax.erf(first * INV_ROOT_TWO))
        slope = cdf + first * jnp.exp(-0.5 * first * first) * INV_ROOT_TWO_PI
        hidden = (first * cdf).astype(BF16)
        grad_first = jnp.where(mask, slope * grad_hidden, 0.0).astype(BF16)
        parts = [grad_first[:, cols(t)] for t in range(TILES)]
        for e in range(-2, 3):
            for t, tile in enumerate(shift_tiles(parts, e, d1)):
                gy[e + 2, q, :, cols(t)] = tile
        hid[q] = hidden
        return hidden

    def head_dot(q, hidden):
        out = dot(zw[...], jnp.concatenate([hidden, px[2, q]], axis=0))
        for t in range(TILES):
            z[q, t] = out[:, cols(t)]

    def hidden_rows(s, _):
        lag, more = 3, 2
        dots, values = {}, {}
        for u in range(BATCH + lag + more):
            q = RIM // 2 + s * BATCH + u
            if u < BATCH:
                dots[u] = hidden_dots(q)
            if 0 <= u - lag < BATCH:
                values[u - lag] = hidden_values(q - lag, *dots.pop(u - lag))
            if u >= lag + more:
                head_dot(q - lag - more, values.pop(u - lag - more))
        return 0

    lax.fori_loop(0, (ROWS + RIM) // BATCH, hidden_rows, 0)

    for c in far_copies:
        c.wait()
    core = lax.rem(me, 2)
    near_copies = [
        copy(5 + BEHIND + j, ahead.at[j + 2 - 2 * core], ahead.at[j + 1], me + 1 - 2 * core, half)
        for j in range(0, REACH, 2)
    ]

    def grad_rows(s, carry):
        for u in range(BATCH):
            carry = grad_row(s * BATCH + u, carry)
        return carry

    head_full = head_column(head, LANES)

    def grad_row(row, carry):
        left_acc, right_acc, weight_acc = carry
        q = row + RIM
        stack = jnp.concatenate([gy[b - a + 2, q - a * d1] for a in TAPS for b in TAPS], axis=0)
        grad_pair = dot(w1t[...], stack)
        left = lcol[q]
        prods, spread = [], []
        for t, mask in enumerate(masks(q)):
            g = vga[q, t, 2:3, :]
            part = jnp.where(mask, grad_pair[:, cols(t)] + head_full * g, 0.0)
            prods.append(part * band[q + RIM, :, cols(t)])
            spread.append(pltpu.roll(part * left, row, 1))
        total = (prods[0] + prods[1]) + (prods[2] + prods[3])
        left_acc = jnp.where(lane == row, jnp.sum(total, axis=1, keepdims=True), left_acc)
        zero = jnp.zeros((16, LANES), F32)
        right_acc = tuple(
            r + jnp.where(lane < row, b, a)
            for r, b, a in zip(right_acc, [zero] + spread, spread + [zero])
        )
        weight_acc = weight_acc + dot(
            jnp.concatenate([stack, tap_rows(q)], axis=0),
            jnp.concatenate([px[2, q], hid[q]], axis=0),
            LAST,
        )
        return left_acc, right_acc, weight_acc

    zero = jnp.zeros((16, LANES), F32)
    left_grad, right_terms, weight_acc = lax.fori_loop(
        0, ROWS // BATCH, grad_rows, (zero, (zero,) * (TILES + 1), jnp.zeros((168, 32), F32))
    )

    for c in near_copies:
        c.wait()
    left_low = left_grad.astype(BF16)
    left_part = dot(left_low[:, :ROWS], ahead[0])
    right_part = jnp.zeros((16, OFF), F32)
    for t in range(TILES):
        pair_of = jnp.concatenate([ahead[2 * t], ahead[2 * t + 1]], axis=0)
        right_part = right_part + dot(right_terms[t].astype(BF16), pair_of)
    right_part = right_part + dot(right_terms[TILES][:, :ROWS].astype(BF16), ahead[REACH])
    acc[...] = jnp.zeros((256, LANES), F32)
    acc[:168, :32] = weight_acc
    turned = acc[...].T
    for j in range(GROUP):
        part = left_part if j < 8 else right_part
        r = 8 * ((j // 4) % 2)
        buf[j, 0:8, :] = part[r : r + 8, cols(j % 4)]
        if j < 4:
            r = 8 * (j // 2)
            buf[j, 8:16, :] = turned[r : r + 8, cols(j % 2)]
        elif j < 6:
            r = 8 * (j - 2)
            buf[j, 8:16, :] = turned[r : r + 8, cols(1)]
        else:
            buf[j, 8:16, :] = jnp.zeros((8, LANES), F32)
    first_copy = 5 + BEHIND + REACH
    group_copy = first_copy + REACH
    stage = []
    for s in range(1, GROUP):
        target = lax.rem(place + s, GROUP)
        stage.append(copy(group_copy + s, buf.at[target], arecv.at[s], base + target, half))

    for d in range(1, REACH + 1):
        piece = right_terms[d // 2]
        rsend[d] = pltpu.roll(piece, ROWS, 1) if d % 2 else piece
    rights = [
        copy(first_copy + d, rsend.at[d], rrecv.at[d], hop(me, d), half)
        for d in range(1, REACH + 1)
    ]

    def align_rows(s, _):
        for u in range(BATCH):
            row = s * BATCH + u
            for n, a in enumerate(TAPS):
                for t in range(TILES):
                    zs[n, t, pl.ds(pl.multiple_of(row * 16, 16), 16), :] = z[row + RIM + a * d2, t]
        return 0

    lax.fori_loop(0, ROWS // BATCH, align_rows, 0)

    def tap_sum(t, a, row):
        return zs[a + 1, t, pl.ds(row, ROWS, stride=16), :]

    total = None
    for e in range(-2, 3):
        parts = [
            sum(tap_sum(t, a, (a + 1) * 3 + a + e + 1) for a in TAPS if -1 <= a + e <= 1)
            for t in range(TILES)
        ]
        parts = shift_tiles(parts, -e, d2)
        total = parts if total is None else [x + y for x, y in zip(total, parts)]
    own_lane = ids((ROWS, LANES), 1)
    for t in range(TILES):
        second = jnp.where(own_lane < edge[t, RIM : RIM + ROWS, :], total[t], 0.0)
        csend[:, cols(t)] = (tap_sum(t, 0, 9) + second).astype(BF16)
    swap_copy = group_copy + GROUP
    swap = copy(swap_copy, csend, crecv, me, other)

    total = buf[place]
    for s, c in enumerate(stage):
        c.wait()
        total = total + arecv[s + 1]
    brecv[plane] = total

    def plane_copy(s, index, target):
        return pltpu.make_async_remote_copy(
            src_ref=brecv.at[index], dst_ref=brecv.at[index],
            send_sem=plane_send.at[s], recv_sem=plane_recv.at[index],
            device_id={"chrom": target * GROUP + place, "chan": half}, device_id_type=MESH,
        )

    planes = [(s, lax.rem(plane + s, PLANES)) for s in range(1, PLANES)]
    for s, p in planes:
        plane_copy(s, plane, p).start()

    for c in rights:
        c.wait()
    right = right_terms[0]
    for d in range(1, REACH + 1):
        right = right + rrecv[d]
    right = jnp.where(lane < ROWS, right, 0.0)
    lrsend[...] = jnp.concatenate([left_low, right.astype(BF16)], axis=0)
    trade = copy(swap_copy + 1, lrsend, lrrecv, me, other)

    for s, p in planes:
        plane_copy(s, plane, p).wait_send()
        plane_copy(s, p, p).wait_recv()
    total = brecv[0]
    for p in range(1, PLANES):
        total = total + brecv[p]
    fin[place] = total * scale

    def last_copy(s, index, target):
        return pltpu.make_async_remote_copy(
            src_ref=fin.at[index], dst_ref=fin.at[index],
            send_sem=last_send.at[s], recv_sem=last_recv.at[index],
            device_id={"chrom": base + target, "chan": half}, device_id_type=MESH,
        )

    others = [(s, lax.rem(place + s, GROUP)) for s in range(1, GROUP)]
    for s, p in others:
        last_copy(s, place, p).start()
    emb_copy.wait_send()
    w_copy.wait()
    trade.wait()
    both = jnp.concatenate([lrsend[...], lrrecv[...]], axis=0)
    weights = jnp.concatenate([wt[:, mine], wother[...]], axis=0)
    emb_grad[...] = dot(both, weights, FIRST)[:ROWS].astype(BF16)
    swap.wait()
    contacts[...] = csend[...].astype(F32) + crecv[...].astype(F32)

    for s, p in others:
        last_copy(s, place, p).wait_send()
        last_copy(s, p, p).wait_recv()


def band_call(scale, *operands):
    v = pl.BlockSpec(memory_space=pltpu.VMEM)
    m = pl.BlockSpec(memory_space=pltpu.SMEM)
    copies = 4 + BEHIND + REACH + 1 + REACH + GROUP + 4
    dma = pltpu.SemaphoreType.DMA
    return pl.pallas_call(
        functools.partial(band_kernel, scale),
        out_shape=(
            jax.ShapeDtypeStruct((ROWS, OFF), F32),
            jax.ShapeDtypeStruct((ROWS, 256), BF16),
            jax.ShapeDtypeStruct((GROUP, 16, LANES), F32),
        ),
        in_specs=[m] * 3 + [pl.BlockSpec(memory_space=pl.ANY)] * 6,
        out_specs=[v] * 3,
        scratch_shapes=[
            pltpu.VMEM((32, 512), BF16),
            pltpu.VMEM((32, 256), BF16),
            pltpu.VMEM((9, 16, 16), BF16),
            pltpu.VMEM((9, 16, 16), BF16),
            pltpu.VMEM((16, 144), BF16),
            pltpu.VMEM((16, 144), BF16),
            pltpu.VMEM((16, 24), BF16),
            pltpu.VMEM((16, 32), BF16),
            pltpu.VMEM((ROWS, 512), BF16),
            pltpu.VMEM((REACH + 1, ROWS, 512), BF16),
            pltpu.VMEM((BEHIND + 2, 16, LANES), F32),
            pltpu.VMEM((SLAB, OFF), BF16),
            pltpu.VMEM((16, OFF + LANES), F32),
            pltpu.VMEM((16, LANES), F32),
            pltpu.VMEM((SLAB, 16, LANES), F32),
            pltpu.VMEM((TILES, SLAB, LANES), jnp.int32),
            pltpu.VMEM((SLAB, TILES, 8, LANES), F32),
            pltpu.VMEM((SLAB + 2 * RIM + BATCH, 16, OFF), F32),
            pltpu.VMEM((5, SLAB, 16, OFF), BF16),
            pltpu.VMEM((5, SLAB, 16, OFF), BF16),
            pltpu.VMEM((SLAB, 16, OFF), BF16),
            pltpu.VMEM((SLAB, TILES, 16, LANES), F32),
            pltpu.VMEM((3, TILES, ROWS * 16, LANES), F32),
            pltpu.VMEM((256, LANES), F32),
            pltpu.VMEM((ROWS, OFF), BF16),
            pltpu.VMEM((ROWS, OFF), BF16),
            pltpu.VMEM((REACH + 1, 16, LANES), F32),
            pltpu.VMEM((REACH + 1, 16, LANES), F32),
            pltpu.VMEM((32, LANES), BF16),
            pltpu.VMEM((32, LANES), BF16),
            pltpu.VMEM((GROUP, 16, LANES), F32),
            pltpu.VMEM((GROUP, 16, LANES), F32),
            pltpu.VMEM((PLANES, 16, LANES), F32),
            dma((6,)),
            dma((copies,)),
            dma((copies,)),
            dma((PLANES,)),
            dma((PLANES,)),
            dma((GROUP,)),
            dma((GROUP,)),
        ],
        compiler_params=pltpu.CompilerParams(
            collective_id=0, has_side_effects=True, vmem_limit_bytes=56 * 1024 * 1024
        ),
    )(*operands)


def output_kernel(
    head, fin, second_w, contacts_in, emb_grad_in,
    contacts, emb_grad, left_grad, right_grad, first_grad, second_grad, head_grad, wide,
):
    contacts[...] = contacts_in[...]
    emb_grad[...] = emb_grad_in[...]
    for j in range(GROUP):
        out = left_grad if j < 8 else right_grad
        r = 8 * ((j // 4) % 2)
        out[r : r + 8, cols(j % 4)] = fin[j, 0:8, :]
    wide[...] = jnp.zeros((LANES, 3 * LANES), F32)
    for j in range(4):
        r = 8 * (j // 2)
        wide[r : r + 8, cols(j % 2)] = fin[j, 8:16, :]
    wide[0:8, cols(2)] = fin[4, 8:16, :]
    wide[8:16, cols(2)] = fin[5, 8:16, :]
    turned = wide[...].T
    head_sum = wide[0:16, 154:155]
    head16 = head_column(head, 16)
    sums = jnp.zeros((16, 16), F32)
    for ab in range(9):
        a, b = ab // 3, ab % 3
        first_grad[ab] = turned[16 * ab : 16 * ab + 16, :16]
        row = 2 * LANES + 16 + 8 * a + (b - a + 2)
        moved = turned[row : row + 1, :16]
        second_grad[ab] = head16 * moved
        sums = sums + second_w[ab].astype(F32) * moved
    total = head_sum + jnp.sum(sums, axis=1, keepdims=True)
    head_grad[...] = diagonal(jnp.broadcast_to(total, (16, 16)), 16)


def output_call(head, fin, second_w, contacts, emb_grad):
    v = pl.BlockSpec(memory_space=pltpu.VMEM)
    m = pl.BlockSpec(memory_space=pltpu.SMEM)
    return pl.pallas_call(
        output_kernel,
        out_shape=(
            jax.ShapeDtypeStruct((ROWS, OFF), F32),
            jax.ShapeDtypeStruct((ROWS, 256), BF16),
            jax.ShapeDtypeStruct((16, 512), F32),
            jax.ShapeDtypeStruct((16, 512), F32),
            jax.ShapeDtypeStruct((9, 16, 16), F32),
            jax.ShapeDtypeStruct((9, 16, 16), F32),
            jax.ShapeDtypeStruct((1, 16), F32),
        ),
        in_specs=[m] + [v] * 4,
        out_specs=[v] * 7,
        scratch_shapes=[pltpu.VMEM((LANES, 3 * LANES), F32)],
    )(head, fin, second_w, contacts, emb_grad)


def on_device(
    embeddings,
    w_left,
    w_right,
    first_conv_weight,
    second_conv_weight,
    head_weight,
    cotangent,
    dilations,
    chrom_ends,
):
    bin_total = embeddings.shape[0] * lax.axis_size("chrom")
    scale = 1.0 / math.sqrt(bin_total * OFF)
    first_w = jnp.transpose(first_conv_weight, (1, 2, 0, 3)).reshape(9, 16, 16)
    second_w = jnp.transpose(second_conv_weight, (1, 2, 0, 3)).reshape(9, 16, 16)
    contacts, emb_grad, fin = band_call(
        scale, chrom_ends, dilations, head_weight, embeddings, w_left.T, w_right.T,
        first_w, second_w, cotangent,
    )
    contacts, emb_grad, left_grad, right_grad, first_grad, second_grad, head_grad = output_call(
        head_weight, fin, second_w, contacts, emb_grad
    )
    return (
        contacts,
        emb_grad,
        left_grad.T,
        right_grad.T,
        jnp.transpose(first_grad.reshape(3, 3, 16, 16), (2, 0, 1, 3)),
        jnp.transpose(second_grad.reshape(3, 3, 16, 16), (2, 0, 1, 3)),
        head_grad.reshape(16),
    )


def solution(mesh):
    in_specs = (
        P("chrom", "chan"),
        P(None, "chan"),
        P(None, "chan"),
        P("chan", None, None, None),
        P("chan", None, None, None),
        P("chan"),
        P("chrom", None),
        P(),
        P(),
    )
    out_specs = (
        P("chrom", None),
        P("chrom", "chan"),
        P(None, "chan"),
        P(None, "chan"),
        P("chan", None, None, None),
        P("chan", None, None, None),
        P("chan"),
    )
    return jax.shard_map(
        on_device, mesh=mesh, in_specs=in_specs, out_specs=out_specs, check_vma=False
    )
```

```python
import functools
import math

import jax
import jax.numpy as jnp
from jax import lax
from jax.experimental import pallas as pl
from jax.experimental.pallas import tpu as pltpu
from jax.sharding import PartitionSpec as P

MESH = pl.DeviceIdType.MESH
F32 = jnp.float32
BF16 = jnp.bfloat16
OFF = 512
LANES = 128
TILES = OFF // LANES
ROWS = 64
RIM = 16
SLAB = ROWS + 2 * RIM
REACH = OFF // ROWS
BEHIND = REACH + 1
TAPS = (-1, 0, 1)
BATCH = 8
WIDE = 1
GROUP = 16
PLANES = 8
INV_ROOT_TWO = 0.7071067811865476
INV_ROOT_TWO_PI = 0.3989422804014327
LAST = (((1,), (1,)), ((), ()))
FIRST = (((0,), (0,)), ((), ()))


def ids(shape, dim):
    return lax.broadcasted_iota(jnp.int32, shape, dim)


def dot(a, b, dims=(((1,), (0,)), ((), ()))):
    return lax.dot_general(a, b, dims, preferred_element_type=F32)


def cols(t):
    return slice(t * LANES, (t + 1) * LANES)


def hop(me, distance):
    count = lax.axis_size("chrom")
    return lax.rem(me + distance + count, count)


def shift_tiles(tiles, count, dist):
    if count == 0:
        return tiles
    lane = ids((tiles[0].shape[0], LANES), 1)
    zero = jnp.zeros_like(tiles[0])
    if count > 0:
        amount = count * dist
        rolled = [pltpu.roll(t, amount, 1) for t in tiles]
        before = [zero] + rolled[:-1]
        return [jnp.where(lane < amount, b, r) for b, r in zip(before, rolled)]
    amount = LANES + count * dist
    rolled = [pltpu.roll(t, amount, 1) for t in tiles]
    after = rolled[1:] + [zero]
    return [jnp.where(lane < amount, r, a) for r, a in zip(rolled, after)]


def diagonal(column, lanes):
    shape = (16, lanes)
    return jnp.sum(jnp.where(ids(shape, 0) == ids(shape, 1), column, 0.0), axis=0, keepdims=True)


def head_column(head, lanes):
    sub = ids((16, lanes), 0)
    column = jnp.zeros((16, lanes), F32)
    for o in range(16):
        column = jnp.where(sub == o, head[o], column)
    return column


def band_kernel(
    scale,
    ends, dil, head, emb, w_left, w_right, first_in, second_in, cot,
    contacts, emb_grad, fin,
    wt, wother, first_w, second_w, w1, w1t, vm, zw,
    full, slots, cot96, rb, lb, lcol, edge, vga, band, px, gy, hid, z, zs, acc,
    csend, crecv, rsend, rrecv, lrsend, lrrecv, buf, arecv, brecv,
    load_sem, send_sem, recv_sem, plane_send, plane_recv, last_send, last_recv,
):
    me = lax.axis_index("chrom")
    half = lax.axis_index("chan")
    other = 1 - half
    place = lax.rem(me, GROUP)
    plane = me // GROUP
    base = me - place
    mine = pl.ds(pl.multiple_of(half * 256, 256), 256)
    theirs = pl.ds(pl.multiple_of(other * 256, 256), 256)
    d1 = dil[0]
    d2 = dil[1]
    lane = ids((16, LANES), 1)

    barrier = pltpu.get_barrier_semaphore()
    sources = [(hop(me, d), half) for d in range(1, BEHIND + 1)]
    sources += [(hop(me, -d), half) for d in range(1, REACH + 1)]
    sources += [(base + lax.rem(place + s, GROUP), half) for s in range(1, GROUP)]
    sources += [(lax.rem(plane + s, PLANES) * GROUP + place, half) for s in range(1, PLANES)]
    sources += [(me, other)]
    for chrom, chan in sources:
        pl.semaphore_signal(
            barrier, inc=1, device_id={"chrom": chrom, "chan": chan}, device_id_type=MESH
        )

    def copy(index, src, dst, chrom, chan):
        c = pltpu.make_async_remote_copy(
            src_ref=src, dst_ref=dst, send_sem=send_sem.at[index], recv_sem=recv_sem.at[index],
            device_id={"chrom": chrom, "chan": chan}, device_id_type=MESH,
        )
        c.start()
        return c

    loads = [
        pltpu.make_async_copy(src, dst, load_sem.at[n])
        for n, (src, dst) in enumerate(
            [
                (emb, full.at[:, mine]),
                (w_left, wt.at[pl.ds(0, 16)]),
                (w_right, wt.at[pl.ds(16, 16)]),
                (first_in, first_w),
                (second_in, second_w),
                (cot, cot96.at[pl.ds(RIM, ROWS)]),
            ]
        )
    ]
    for load in loads:
        load.start()
    pl.semaphore_wait(barrier, len(sources))

    emb_copy = copy(0, emb, full.at[:, mine], me, other)
    rims = [
        copy(1, cot.at[pl.ds(ROWS - RIM, RIM)], cot96.at[pl.ds(0, RIM)], hop(me, 1), half),
        copy(2, cot.at[pl.ds(0, RIM)], cot96.at[pl.ds(RIM + ROWS, RIM)], hop(me, -1), half),
    ]
    for load in loads:
        load.wait()
    w_copy = copy(3, wt.at[:, theirs], wother, me, other)

    head16 = head_column(head, 16)
    sub16 = ids((16, 16), 0)
    rows = jnp.zeros((16, 16), F32)
    form = jnp.zeros((16, 144), F32)
    form_t = jnp.zeros((16, 144), F32)
    for ab in range(9):
        at = (ids((16, 144), 1) == ids((16, 144), 0) + 16 * ab).astype(BF16)
        form = form + dot(first_w[ab], at)
        form_t = form_t + dot(first_w[ab], at, FIRST)
        row = jnp.sum(head16 * second_w[ab].astype(F32), axis=0, keepdims=True)
        rows = jnp.where(sub16 == ab, row, rows)
    w1[...] = form.astype(BF16)
    w1t[...] = form_t.astype(BF16)
    head_rows = jnp.where(sub16 == 9, diagonal(head16, 16), 0.0).astype(BF16)
    rows = rows.astype(BF16)
    low = (ids((16, 32), 1) == ids((16, 32), 0)).astype(BF16)
    high = (ids((16, 32), 1) == ids((16, 32), 0) + 16).astype(BF16)
    zw[...] = (dot(rows, low) + dot(head_rows, high)).astype(BF16)
    tap = ids((16, 24), 0)
    column = tap + 4 * ((tap >= 3).astype(jnp.int32) + (tap >= 6).astype(jnp.int32)) + 2
    spot = ((ids((16, 24), 1) == column) & (tap < 9)).astype(BF16)
    vm[...] = dot(rows, spot, FIRST).astype(BF16)

    emb_copy.wait_recv()
    twice = jnp.concatenate([full[...], full[...]], axis=0)
    slots[1] = jnp.where(lane < ROWS, dot(wt[16:32, :], twice, LAST), dot(wt[0:16, :], twice, LAST))
    tiles = [
        copy(3 + d, slots.at[1], slots.at[1 + d], hop(me, -d), half)
        for d in range(1, BEHIND + 1)
    ]
    tiles.append(copy(4 + BEHIND, slots.at[1], slots.at[0], hop(me, 1), half))
    for c in rims:
        c.wait()
    big = jnp.int32(1 << 30)
    bins = ids((SLAB, LANES), 0) + (me * ROWS - RIM)
    stop = jnp.full((SLAB, LANES), big)
    for j in range(8):
        stop = jnp.minimum(stop, jnp.where(ends[j] > bins, ends[j], big))
    width = jnp.where((bins >= 0) & (stop < big), jnp.minimum(stop - bins, OFF), 0)
    slab_lane = ids((SLAB, LANES), 1)
    masked = []
    for t in range(TILES):
        edge[t] = width - t * LANES
        masked.append(
            jnp.where(slab_lane < width - t * LANES, cot96[:, cols(t)].astype(F32), 0.0)
        )
    for e in range(-2, 3):
        for t, tile in enumerate(shift_tiles(masked, e, d2)):
            vga[:, t, e + 2, :] = tile
    for e in range(5, 8):
        for t in range(TILES):
            vga[:, t, e, :] = jnp.zeros((SLAB, LANES), F32)

    for c in tiles:
        c.wait()
    for t in range(TILES + 1):
        before = pltpu.roll(slots[2 * t], 96, 1)
        inside = pltpu.roll(slots[2 * t + 1], 32, 1)
        after = pltpu.roll(slots[2 * t + 2], 96, 1)
        rb[:, cols(t)] = jnp.where(lane < 32, before, jnp.where(lane < 96, inside, after))
    lb[...] = jnp.where(
        lane < RIM,
        pltpu.roll(slots[0], 16, 1),
        jnp.where(lane < RIM + ROWS, pltpu.roll(slots[1], 80, 1), pltpu.roll(slots[2], 16, 1)),
    )
    for q in range(SLAB):
        lcol[q] = jnp.broadcast_to(lb[:, q : q + 1], (16, LANES))

    def masks(q):
        return [lane < edge[t, pl.ds(q, 1), :] for t in range(TILES)]

    def band_row(p):
        back = lax.rem(2 * LANES - p, LANES)
        rolled = [pltpu.roll(rb[:, cols(t)], back, 1) for t in range(TILES + 1)]
        for t in range(TILES):
            band[p, :, cols(t)] = jnp.where(lane < LANES - p, rolled[t], rolled[t + 1])

    def pair_row(q):
        left = lcol[q]
        limits = [edge[t, pl.ds(q, 1), :] for t in range(TILES)]
        for e in range(-2, 3):
            move = e * d1
            for t in range(TILES):
                mask = lane < limits[t] - move
                if e < 0 and t == 0:
                    mask = mask & (lane >= -move)
                value = left * band[q + RIM + move, :, cols(t)]
                px[e + 2, q, :, cols(t)] = jnp.where(mask, value, 0.0).astype(BF16)

    def first_band_rows(s, _):
        for u in range(BATCH):
            band_row(s * BATCH + u)
        return 0

    def pair_rows(s, _):
        for u in range(BATCH):
            pair_row(s * BATCH + u)
            band_row(2 * RIM + (s + 1) * BATCH + u)
        return 0

    lax.fori_loop(0, 2 * RIM // BATCH + 1, first_band_rows, 0)
    lax.fori_loop(0, SLAB // BATCH, pair_rows, 0)

    def tap_rows(q):
        return jnp.concatenate(
            [
                jnp.concatenate([vga[q - a * d2, t] for a in TAPS], axis=0)
                for t in range(TILES)
            ],
            axis=1,
        ).astype(BF16)

    def hidden_dots(q):
        stack = jnp.concatenate([px[b - a + 2, q + a * d1] for a in TAPS for b in TAPS], axis=0)
        return dot(w1[...], stack), dot(vm[...], tap_rows(q))

    def hidden_values(q, first, grad_hidden):
        mask = jnp.concatenate(masks(q), axis=1)
        first = jnp.where(mask, first, 0.0)
        cdf = 0.5 * (1.0 + lax.erf(first * INV_ROOT_TWO))
        slope = cdf + first * jnp.exp(-0.5 * first * first) * INV_ROOT_TWO_PI
        hidden = (first * cdf).astype(BF16)
        grad_first = jnp.where(mask, slope * grad_hidden, 0.0).astype(BF16)
        parts = [grad_first[:, cols(t)] for t in range(TILES)]
        for e in range(-2, 3):
            for t, tile in enumerate(shift_tiles(parts, e, d1)):
                gy[e + 2, q, :, cols(t)] = tile
        hid[q] = hidden
        return hidden

    def head_dot(q, hidden):
        out = dot(zw[...], jnp.concatenate([hidden, px[2, q]], axis=0))
        for t in range(TILES):
            z[q, t] = out[:, cols(t)]

    def hidden_rows(s, _):
        lag, more = 3, 2
        dots, values = {}, {}
        for u in range(BATCH + lag + more):
            q = RIM // 2 + s * BATCH + u
            if u < BATCH:
                dots[u] = hidden_dots(q)
            if 0 <= u - lag < BATCH:
                values[u - lag] = hidden_values(q - lag, *dots.pop(u - lag))
            if u >= lag + more:
                head_dot(q - lag - more, values.pop(u - lag - more))
        return 0

    lax.fori_loop(0, (ROWS + RIM) // BATCH, hidden_rows, 0)

    def grad_rows(s, carry):
        for u in range(BATCH):
            carry = grad_row(s * BATCH + u, carry)
        return carry

    head_full = head_column(head, LANES)

    def grad_row(row, carry):
        left_acc, right_acc = carry
        q = row + RIM
        stack = jnp.concatenate([gy[b - a + 2, q - a * d1] for a in TAPS for b in TAPS], axis=0)
        grad_pair = dot(w1t[...], stack)
        left = lcol[q]
        prods, spread = [], []
        for t, mask in enumerate(masks(q)):
            g = vga[q, t, 2:3, :]
            part = jnp.where(mask, grad_pair[:, cols(t)] + head_full * g, 0.0)
            prods.append(part * band[q + RIM, :, cols(t)])
            spread.append(pltpu.roll(part * left, row, 1))
        total = (prods[0] + prods[1]) + (prods[2] + prods[3])
        left_acc = jnp.where(lane == row, jnp.sum(total, axis=1, keepdims=True), left_acc)
        zero = jnp.zeros((16, LANES), F32)
        right_acc = tuple(
            r + jnp.where(lane < row, b, a)
            for r, b, a in zip(right_acc, [zero] + spread, spread + [zero])
        )
        return left_acc, right_acc

    zero = jnp.zeros((16, LANES), F32)
    left_grad, right_terms = lax.fori_loop(
        0, ROWS // BATCH, grad_rows, (zero, (zero,) * (TILES + 1))
    )

    for d in range(1, REACH + 1):
        piece = right_terms[d // 2]
        rsend[d] = pltpu.roll(piece, ROWS, 1) if d % 2 else piece
    first_copy = 5 + BEHIND
    rights = [
        copy(first_copy + d, rsend.at[d], rrecv.at[d], hop(me, d), half)
        for d in range(1, REACH + 1)
    ]

    def weight_rows(s, weight_acc):
        for u in range(0, BATCH, WIDE):
            left_side, right_side = [], []
            for n in range(WIDE):
                q = RIM + s * BATCH + u + n
                taken = [gy[b - a + 2, q - a * d1] for a in TAPS for b in TAPS]
                left_side.append(jnp.concatenate(taken + [tap_rows(q)], axis=0))
                right_side.append(jnp.concatenate([px[2, q], hid[q]], axis=0))
            weight_acc = weight_acc + dot(
                jnp.concatenate(left_side, axis=1), jnp.concatenate(right_side, axis=1), LAST
            )
        return weight_acc

    acc[...] = jnp.zeros((256, LANES), F32)
    acc[:168, :32] = lax.fori_loop(
        0, ROWS // BATCH, weight_rows, jnp.zeros((168, 32), F32)
    )
    turned = acc[...].T

    def align_rows(s, _):
        for u in range(BATCH):
            row = s * BATCH + u
            for n, a in enumerate(TAPS):
                for t in range(TILES):
                    zs[n, t, pl.ds(pl.multiple_of(row * 16, 16), 16), :] = z[row + RIM + a * d2, t]
        return 0

    lax.fori_loop(0, ROWS // BATCH, align_rows, 0)

    def tap_sum(t, a, row):
        return zs[a + 1, t, pl.ds(row, ROWS, stride=16), :]

    total = None
    for e in range(-2, 3):
        parts = [
            sum(tap_sum(t, a, (a + 1) * 3 + a + e + 1) for a in TAPS if -1 <= a + e <= 1)
            for t in range(TILES)
        ]
        parts = shift_tiles(parts, -e, d2)
        total = parts if total is None else [x + y for x, y in zip(total, parts)]
    own_lane = ids((ROWS, LANES), 1)
    for t in range(TILES):
        second = jnp.where(own_lane < edge[t, RIM : RIM + ROWS, :], total[t], 0.0)
        csend[:, cols(t)] = (tap_sum(t, 0, 9) + second).astype(BF16)
    swap_copy = first_copy + REACH + 1
    swap = copy(swap_copy, csend, crecv, me, other)

    for c in rights:
        c.wait()
    right = right_terms[0]
    for d in range(1, REACH + 1):
        right = right + rrecv[d]
    right = jnp.where(lane < ROWS, right, 0.0)
    lrsend[...] = jnp.concatenate([left_grad, right], axis=0).astype(BF16)
    trade = copy(swap_copy + 1, lrsend, lrrecv, me, other)

    part = dot(lrsend[:, :ROWS], full[...])
    for j in range(GROUP):
        r = 8 * (j // 4)
        buf[j, 0:8, :] = part[r : r + 8, cols(j % 4)]
        if j < 4:
            r = 8 * (j // 2)
            buf[j, 8:16, :] = turned[r : r + 8, cols(j % 2)]
        elif j < 6:
            r = 8 * (j - 2)
            buf[j, 8:16, :] = turned[r : r + 8, cols(1)]
        else:
            buf[j, 8:16, :] = jnp.zeros((8, LANES), F32)
    group_copy = swap_copy + 1
    stage = []
    for s in range(1, GROUP):
        target = lax.rem(place + s, GROUP)
        stage.append(copy(group_copy + s, buf.at[target], arecv.at[s], base + target, half))

    total = buf[place]
    for s, c in enumerate(stage):
        c.wait()
        total = total + arecv[s + 1]
    brecv[plane] = total

    def plane_copy(s, index, target):
        return pltpu.make_async_remote_copy(
            src_ref=brecv.at[index], dst_ref=brecv.at[index],
            send_sem=plane_send.at[s], recv_sem=plane_recv.at[index],
            device_id={"chrom": target * GROUP + place, "chan": half}, device_id_type=MESH,
        )

    planes = [(s, lax.rem(plane + s, PLANES)) for s in range(1, PLANES)]
    for s, p in planes:
        plane_copy(s, plane, p).start()

    for s, p in planes:
        plane_copy(s, plane, p).wait_send()
        plane_copy(s, p, p).wait_recv()
    total = brecv[0]
    for p in range(1, PLANES):
        total = total + brecv[p]
    fin[place] = total * scale

    def last_copy(s, index, target):
        return pltpu.make_async_remote_copy(
            src_ref=fin.at[index], dst_ref=fin.at[index],
            send_sem=last_send.at[s], recv_sem=last_recv.at[index],
            device_id={"chrom": base + target, "chan": half}, device_id_type=MESH,
        )

    others = [(s, lax.rem(place + s, GROUP)) for s in range(1, GROUP)]
    for s, p in others:
        last_copy(s, place, p).start()
    emb_copy.wait_send()
    w_copy.wait()
    trade.wait()
    both = jnp.concatenate([lrsend[...], lrrecv[...]], axis=0)
    weights = jnp.concatenate([wt[:, mine], wother[...]], axis=0)
    emb_grad[...] = dot(both, weights, FIRST)[:ROWS].astype(BF16)
    swap.wait()
    contacts[...] = csend[...].astype(F32) + crecv[...].astype(F32)

    for s, p in others:
        last_copy(s, place, p).wait_send()
        last_copy(s, p, p).wait_recv()


def band_call(scale, *operands):
    v = pl.BlockSpec(memory_space=pltpu.VMEM)
    m = pl.BlockSpec(memory_space=pltpu.SMEM)
    copies = 5 + BEHIND + REACH + 3 + GROUP
    dma = pltpu.SemaphoreType.DMA
    return pl.pallas_call(
        functools.partial(band_kernel, scale),
        out_shape=(
            jax.ShapeDtypeStruct((ROWS, OFF), F32),
            jax.ShapeDtypeStruct((ROWS, 256), BF16),
            jax.ShapeDtypeStruct((GROUP, 16, LANES), F32),
        ),
        in_specs=[m] * 3 + [pl.BlockSpec(memory_space=pl.ANY)] * 6,
        out_specs=[v] * 3,
        scratch_shapes=[
            pltpu.VMEM((32, 512), BF16),
            pltpu.VMEM((32, 256), BF16),
            pltpu.VMEM((9, 16, 16), BF16),
            pltpu.VMEM((9, 16, 16), BF16),
            pltpu.VMEM((16, 144), BF16),
            pltpu.VMEM((16, 144), BF16),
            pltpu.VMEM((16, 24), BF16),
            pltpu.VMEM((16, 32), BF16),
            pltpu.VMEM((ROWS, 512), BF16),
            pltpu.VMEM((BEHIND + 2, 16, LANES), F32),
            pltpu.VMEM((SLAB, OFF), BF16),
            pltpu.VMEM((16, OFF + LANES), F32),
            pltpu.VMEM((16, LANES), F32),
            pltpu.VMEM((SLAB, 16, LANES), F32),
            pltpu.VMEM((TILES, SLAB, LANES), jnp.int32),
            pltpu.VMEM((SLAB, TILES, 8, LANES), F32),
            pltpu.VMEM((SLAB + 2 * RIM + BATCH, 16, OFF), F32),
            pltpu.VMEM((5, SLAB, 16, OFF), BF16),
            pltpu.VMEM((5, SLAB, 16, OFF), BF16),
            pltpu.VMEM((SLAB, 16, OFF), BF16),
            pltpu.VMEM((SLAB, TILES, 16, LANES), F32),
            pltpu.VMEM((3, TILES, ROWS * 16, LANES), F32),
            pltpu.VMEM((256, LANES), F32),
            pltpu.VMEM((ROWS, OFF), BF16),
            pltpu.VMEM((ROWS, OFF), BF16),
            pltpu.VMEM((REACH + 1, 16, LANES), F32),
            pltpu.VMEM((REACH + 1, 16, LANES), F32),
            pltpu.VMEM((32, LANES), BF16),
            pltpu.VMEM((32, LANES), BF16),
            pltpu.VMEM((GROUP, 16, LANES), F32),
            pltpu.VMEM((GROUP, 16, LANES), F32),
            pltpu.VMEM((PLANES, 16, LANES), F32),
            dma((6,)),
            dma((copies,)),
            dma((copies,)),
            dma((PLANES,)),
            dma((PLANES,)),
            dma((GROUP,)),
            dma((GROUP,)),
        ],
        compiler_params=pltpu.CompilerParams(
            collective_id=0, has_side_effects=True, vmem_limit_bytes=56 * 1024 * 1024
        ),
    )(*operands)


def output_kernel(
    head, fin, second_w, contacts_in, emb_grad_in,
    contacts, emb_grad, left_grad, right_grad, first_grad, second_grad, head_grad, wide,
):
    contacts[...] = contacts_in[...]
    emb_grad[...] = emb_grad_in[...]
    for j in range(GROUP):
        out = left_grad if j < 8 else right_grad
        r = 8 * ((j // 4) % 2)
        out[r : r + 8, cols(j % 4)] = fin[j, 0:8, :]
    wide[...] = jnp.zeros((LANES, 3 * LANES), F32)
    for j in range(4):
        r = 8 * (j // 2)
        wide[r : r + 8, cols(j % 2)] = fin[j, 8:16, :]
    wide[0:8, cols(2)] = fin[4, 8:16, :]
    wide[8:16, cols(2)] = fin[5, 8:16, :]
    turned = wide[...].T
    head_sum = wide[0:16, 154:155]
    head16 = head_column(head, 16)
    sums = jnp.zeros((16, 16), F32)
    for ab in range(9):
        a, b = ab // 3, ab % 3
        first_grad[ab] = turned[16 * ab : 16 * ab + 16, :16]
        row = 2 * LANES + 16 + 8 * a + (b - a + 2)
        moved = turned[row : row + 1, :16]
        second_grad[ab] = head16 * moved
        sums = sums + second_w[ab].astype(F32) * moved
    total = head_sum + jnp.sum(sums, axis=1, keepdims=True)
    head_grad[...] = diagonal(jnp.broadcast_to(total, (16, 16)), 16)


def output_call(head, fin, second_w, contacts, emb_grad):
    v = pl.BlockSpec(memory_space=pltpu.VMEM)
    m = pl.BlockSpec(memory_space=pltpu.SMEM)
    return pl.pallas_call(
        output_kernel,
        out_shape=(
            jax.ShapeDtypeStruct((ROWS, OFF), F32),
            jax.ShapeDtypeStruct((ROWS, 256), BF16),
            jax.ShapeDtypeStruct((16, 512), F32),
            jax.ShapeDtypeStruct((16, 512), F32),
            jax.ShapeDtypeStruct((9, 16, 16), F32),
            jax.ShapeDtypeStruct((9, 16, 16), F32),
            jax.ShapeDtypeStruct((1, 16), F32),
        ),
        in_specs=[m] + [v] * 4,
        out_specs=[v] * 7,
        scratch_shapes=[pltpu.VMEM((LANES, 3 * LANES), F32)],
    )(head, fin, second_w, contacts, emb_grad)


def on_device(
    embeddings,
    w_left,
    w_right,
    first_conv_weight,
    second_conv_weight,
    head_weight,
    cotangent,
    dilations,
    chrom_ends,
):
    bin_total = embeddings.shape[0] * lax.axis_size("chrom")
    scale = 1.0 / math.sqrt(bin_total * OFF)
    first_w = jnp.transpose(first_conv_weight, (1, 2, 0, 3)).reshape(9, 16, 16)
    second_w = jnp.transpose(second_conv_weight, (1, 2, 0, 3)).reshape(9, 16, 16)
    contacts, emb_grad, fin = band_call(
        scale, chrom_ends, dilations, head_weight, embeddings, w_left.T, w_right.T,
        first_w, second_w, cotangent,
    )
    contacts, emb_grad, left_grad, right_grad, first_grad, second_grad, head_grad = output_call(
        head_weight, fin, second_w, contacts, emb_grad
    )
    return (
        contacts,
        emb_grad,
        left_grad.T,
        right_grad.T,
        jnp.transpose(first_grad.reshape(3, 3, 16, 16), (2, 0, 1, 3)),
        jnp.transpose(second_grad.reshape(3, 3, 16, 16), (2, 0, 1, 3)),
        head_grad.reshape(16),
    )


def solution(mesh):
    in_specs = (
        P("chrom", "chan"),
        P(None, "chan"),
        P(None, "chan"),
        P("chan", None, None, None),
        P("chan", None, None, None),
        P("chan"),
        P("chrom", None),
        P(),
        P(),
    )
    out_specs = (
        P("chrom", None),
        P("chrom", "chan"),
        P(None, "chan"),
        P(None, "chan"),
        P("chan", None, None, None),
        P("chan", None, None, None),
        P("chan"),
    )
    return jax.shard_map(
        on_device, mesh=mesh, in_specs=in_specs, out_specs=out_specs, check_vma=False
    )
```

```python
import functools
import math

import jax
import jax.numpy as jnp
from jax import lax
from jax.experimental import pallas as pl
from jax.experimental.pallas import tpu as pltpu
from jax.sharding import PartitionSpec as P

MESH = pl.DeviceIdType.MESH
F32 = jnp.float32
BF16 = jnp.bfloat16
OFF = 512
LANES = 128
TILES = OFF // LANES
ROWS = 64
RIM = 16
SLAB = ROWS + 2 * RIM
REACH = OFF // ROWS
BEHIND = REACH + 1
TAPS = (-1, 0, 1)
BATCH = 8
WIDE = 16
GROUP = 16
PLANES = 8
INV_ROOT_TWO = 0.7071067811865476
TWO_OVER_ROOT_PI = 1.1283791670955126
LOG2_E = 1.4426950408889634
LAST = (((1,), (1,)), ((), ()))
FIRST = (((0,), (0,)), ((), ()))


def ids(shape, dim):
    return lax.broadcasted_iota(jnp.int32, shape, dim)


def dot(a, b, dims=(((1,), (0,)), ((), ()))):
    return lax.dot_general(a, b, dims, preferred_element_type=F32)


def cols(t):
    return slice(t * LANES, (t + 1) * LANES)


def hop(me, distance):
    count = lax.axis_size("chrom")
    return lax.rem(me + distance + count, count)


def shift_tiles(tiles, count, dist):
    if count == 0:
        return tiles
    lane = ids((tiles[0].shape[0], LANES), 1)
    zero = jnp.zeros_like(tiles[0])
    if count > 0:
        amount = count * dist
        rolled = [pltpu.roll(t, amount, 1) for t in tiles]
        before = [zero] + rolled[:-1]
        return [jnp.where(lane < amount, b, r) for b, r in zip(before, rolled)]
    amount = LANES + count * dist
    rolled = [pltpu.roll(t, amount, 1) for t in tiles]
    after = rolled[1:] + [zero]
    return [jnp.where(lane < amount, r, a) for r, a in zip(rolled, after)]


def diagonal(column, lanes):
    shape = (16, lanes)
    return jnp.sum(jnp.where(ids(shape, 0) == ids(shape, 1), column, 0.0), axis=0, keepdims=True)


def head_column(head, lanes):
    sub = ids((16, lanes), 0)
    column = jnp.zeros((16, lanes), F32)
    for o in range(WIDE):
        column = jnp.where(sub == o, head[o], column)
    return column


def band_kernel(
    scale,
    ends_in, dil_in, head_in, emb, w_left, w_right, first_in, second_in, cot,
    contacts, emb_grad, fin,
    ends, dil, head,
    wt, wother, first_w, second_w, w1, w1t, vm, zw,
    full, slots, cot96, rb, lb, lcol, edge, vga, band, px, gy, hid, z, zs, acc,
    csend, crecv, rsend, rrecv, lrsend, lrrecv, buf, arecv, brecv,
    load_sem, send_sem, recv_sem, plane_send, plane_recv, last_send, last_recv,
):
    me = lax.axis_index("chrom")
    half = lax.axis_index("chan")
    other = 1 - half
    place = lax.rem(me, GROUP)
    plane = me // GROUP
    base = me - place
    mine = pl.ds(pl.multiple_of(half * 256, 256), 256)
    theirs = pl.ds(pl.multiple_of(other * 256, 256), 256)
    lane = ids((16, LANES), 1)

    barrier = pltpu.get_barrier_semaphore()
    sources = [(hop(me, d), half) for d in range(1, BEHIND + 1)]
    sources += [(hop(me, -d), half) for d in range(1, REACH + 1)]
    sources += [(base + lax.rem(place + s, GROUP), half) for s in range(1, GROUP)]
    sources += [(lax.rem(plane + s, PLANES) * GROUP + place, half) for s in range(1, PLANES)]
    sources += [(me, other)]
    for chrom, chan in sources:
        pl.semaphore_signal(
            barrier, inc=1, device_id={"chrom": chrom, "chan": chan}, device_id_type=MESH
        )

    def copy(index, src, dst, chrom, chan):
        c = pltpu.make_async_remote_copy(
            src_ref=src, dst_ref=dst, send_sem=send_sem.at[index], recv_sem=recv_sem.at[index],
            device_id={"chrom": chrom, "chan": chan}, device_id_type=MESH,
        )
        c.start()
        return c

    loads = [
        pltpu.make_async_copy(src, dst, load_sem.at[n])
        for n, (src, dst) in enumerate(
            [
                (emb, full.at[:, mine]),
                (w_left, wt.at[pl.ds(0, 16)]),
                (w_right, wt.at[pl.ds(16, 16)]),
                (first_in, first_w),
                (second_in, second_w),
                (cot, cot96.at[pl.ds(RIM, ROWS)]),
                (ends_in, ends),
                (dil_in, dil),
                (head_in, head),
            ]
        )
    ]
    for load in loads:
        load.start()
    pl.semaphore_wait(barrier, len(sources))

    emb_copy = copy(0, emb, full.at[:, mine], me, other)
    rims = [
        copy(1, cot.at[pl.ds(ROWS - RIM, RIM)], cot96.at[pl.ds(0, RIM)], hop(me, 1), half),
        copy(2, cot.at[pl.ds(0, RIM)], cot96.at[pl.ds(RIM + ROWS, RIM)], hop(me, -1), half),
    ]
    for load in loads:
        load.wait()
    d1 = dil[0]
    d2 = dil[1]
    w_copy = copy(3, wt.at[:, theirs], wother, me, other)

    head16 = head_column(head, 16)
    sub16 = ids((16, 16), 0)
    rows = jnp.zeros((16, 16), F32)
    form = jnp.zeros((16, 144), F32)
    form_t = jnp.zeros((16, 144), F32)
    for ab in range(9):
        at = (ids((16, 144), 1) == ids((16, 144), 0) + 16 * ab).astype(BF16)
        form = form + dot(first_w[ab], at)
        form_t = form_t + dot(first_w[ab], at, FIRST)
        row = jnp.sum(head16 * second_w[ab].astype(F32), axis=0, keepdims=True)
        rows = jnp.where(sub16 == ab, row, rows)
    w1[...] = form.astype(BF16)
    w1t[...] = form_t.astype(BF16)
    head_rows = jnp.where(sub16 == 9, diagonal(head16, 16), 0.0).astype(BF16)
    rows = rows.astype(BF16)
    low = (ids((16, 32), 1) == ids((16, 32), 0)).astype(BF16)
    high = (ids((16, 32), 1) == ids((16, 32), 0) + 16).astype(BF16)
    half_rows = rows * jnp.bfloat16(0.5)
    zw[...] = (dot(half_rows, low) + dot(head_rows, high)).astype(BF16)
    tap = ids((16, 24), 0)
    column = tap + 4 * ((tap >= 3).astype(jnp.int32) + (tap >= 6).astype(jnp.int32)) + 2
    spot = ((ids((16, 24), 1) == column) & (tap < 9)).astype(BF16)
    vm[...] = dot(half_rows, spot, FIRST).astype(BF16)

    emb_copy.wait_recv()
    twice = jnp.concatenate([full[...], full[...]], axis=0)
    slots[1] = jnp.where(lane < ROWS, dot(wt[16:32, :], twice, LAST), dot(wt[0:16, :], twice, LAST))
    tiles = [
        copy(3 + d, slots.at[1], slots.at[1 + d], hop(me, -d), half)
        for d in range(1, BEHIND + 1)
    ]
    tiles.append(copy(4 + BEHIND, slots.at[1], slots.at[0], hop(me, 1), half))
    for c in rims:
        c.wait()
    big = jnp.int32(1 << 30)
    bins = ids((SLAB, LANES), 0) + (me * ROWS - RIM)
    stop = jnp.full((SLAB, LANES), big)
    for j in range(8):
        stop = jnp.minimum(stop, jnp.where(ends[j] > bins, ends[j], big))
    width = jnp.where((bins >= 0) & (stop < big), jnp.minimum(stop - bins, OFF), 0)
    slab_lane = ids((SLAB, LANES), 1)
    masked = []
    for t in range(TILES):
        edge[t] = width - t * LANES
        masked.append(
            jnp.where(slab_lane < width - t * LANES, cot96[:, cols(t)].astype(F32), 0.0)
        )
    for e in range(-2, 3):
        for t, tile in enumerate(shift_tiles(masked, e, d2)):
            vga[:, t, e + 2, :] = tile
    for e in range(5, 8):
        for t in range(TILES):
            vga[:, t, e, :] = jnp.zeros((SLAB, LANES), F32)

    for c in tiles:
        c.wait()
    for t in range(TILES + 1):
        before = pltpu.roll(slots[2 * t], 96, 1)
        inside = pltpu.roll(slots[2 * t + 1], 32, 1)
        after = pltpu.roll(slots[2 * t + 2], 96, 1)
        rb[:, cols(t)] = jnp.where(lane < 32, before, jnp.where(lane < 96, inside, after))
    lb[...] = jnp.where(
        lane < RIM,
        pltpu.roll(slots[0], 16, 1),
        jnp.where(lane < RIM + ROWS, pltpu.roll(slots[1], 80, 1), pltpu.roll(slots[2], 16, 1)),
    )
    for q in range(SLAB):
        lcol[q] = jnp.broadcast_to(lb[:, q : q + 1], (16, LANES))

    def masks(q):
        return [lane < edge[t, pl.ds(q, 1), :] for t in range(TILES)]

    def band_row(p):
        back = lax.rem(2 * LANES - p, LANES)
        rolled = [pltpu.roll(rb[:, cols(t)], back, 1) for t in range(TILES + 1)]
        for t in range(TILES):
            band[p, :, cols(t)] = jnp.where(lane < LANES - p, rolled[t], rolled[t + 1])

    def pair_row(q):
        left = lcol[q]
        limits = [edge[t, pl.ds(q, 1), :] for t in range(TILES)]
        for e in range(-2, 3):
            move = e * d1
            for t in range(TILES):
                mask = lane < limits[t] - move
                if e < 0 and t == 0:
                    mask = mask & (lane >= -move)
                value = left * band[q + RIM + move, :, cols(t)]
                px[e + 2, q, :, cols(t)] = jnp.where(mask, value, 0.0).astype(BF16)

    def first_band_rows(s, _):
        for u in range(BATCH):
            band_row(s * BATCH + u)
        return 0

    def pair_rows(s, _):
        for u in range(BATCH):
            pair_row(s * BATCH + u)
            band_row(2 * RIM + (s + 1) * BATCH + u)
        return 0

    lax.fori_loop(0, 2 * RIM // BATCH + 1, first_band_rows, 0)
    lax.fori_loop(0, SLAB // BATCH, pair_rows, 0)

    def tap_rows(q):
        return jnp.concatenate(
            [
                jnp.concatenate([vga[q - a * d2, t] for a in TAPS], axis=0)
                for t in range(TILES)
            ],
            axis=1,
        ).astype(BF16)

    def hidden_dots(q):
        stack = jnp.concatenate([px[b - a + 2, q + a * d1] for a in TAPS for b in TAPS], axis=0)
        return dot(w1[...], stack), dot(vm[...], tap_rows(q))

    def hidden_values(q, first, grad_hidden):
        mask = jnp.concatenate(masks(q), axis=1)
        first = jnp.where(mask, first, 0.0)
        scaled = first * INV_ROOT_TWO
        cdf = 1.0 + lax.erf(scaled)
        slope = cdf + scaled * jnp.exp2(scaled * scaled * -LOG2_E) * TWO_OVER_ROOT_PI
        hidden = (first * cdf).astype(BF16)
        grad_first = jnp.where(mask, slope * grad_hidden, 0.0).astype(BF16)
        parts = [grad_first[:, cols(t)] for t in range(TILES)]
        for e in range(-2, 3):
            for t, tile in enumerate(shift_tiles(parts, e, d1)):
                gy[e + 2, q, :, cols(t)] = tile
        hid[q] = hidden

    def hidden_rows(s, _):
        lag = 3
        dots = {}
        for u in range(WIDE + lag):
            q = RIM // 2 + s * WIDE + u
            if u < WIDE:
                dots[u] = hidden_dots(q)
            if u >= lag:
                hidden_values(q - lag, *dots.pop(u - lag))
        return 0

    lax.fori_loop(0, (ROWS + RIM) // WIDE, hidden_rows, 0)

    def grad_rows(s, carry):
        for u in range(WIDE):
            carry = grad_row(s * WIDE + u, carry)
        return carry

    head_full = head_column(head, LANES)

    def grad_row(row, carry):
        left_acc, right_acc = carry
        q = row + RIM
        stack = jnp.concatenate([gy[b - a + 2, q - a * d1] for a in TAPS for b in TAPS], axis=0)
        grad_pair = dot(w1t[...], stack)
        left = lcol[q]
        prods, spread = [], []
        for t, mask in enumerate(masks(q)):
            g = vga[q, t, 2:3, :]
            part = jnp.where(mask, grad_pair[:, cols(t)] + head_full * g, 0.0)
            prods.append(part * band[q + RIM, :, cols(t)])
            spread.append(pltpu.roll(part * left, row, 1))
        total = (prods[0] + prods[1]) + (prods[2] + prods[3])
        left_acc = jnp.where(lane == row, jnp.sum(total, axis=1, keepdims=True), left_acc)
        zero = jnp.zeros((16, LANES), F32)
        right_acc = tuple(
            r + jnp.where(lane < row, b, a)
            for r, b, a in zip(right_acc, [zero] + spread, spread + [zero])
        )
        return left_acc, right_acc

    zero = jnp.zeros((16, LANES), F32)
    left_grad, right_terms = lax.fori_loop(
        0, ROWS // WIDE, grad_rows, (zero, (zero,) * (TILES + 1))
    )

    for d in range(1, REACH + 1):
        piece = right_terms[d // 2]
        rsend[d] = pltpu.roll(piece, ROWS, 1) if d % 2 else piece
    first_copy = 5 + BEHIND
    rights = [
        copy(first_copy + d, rsend.at[d], rrecv.at[d], hop(me, d), half)
        for d in range(1, REACH + 1)
    ]

    def weight_rows(s, weight_acc):
        for u in range(WIDE):
            q = RIM + s * WIDE + u
            taken = [gy[b - a + 2, q - a * d1] for a in TAPS for b in TAPS]
            weight_acc = weight_acc + dot(
                jnp.concatenate(taken + [tap_rows(q)], axis=0),
                jnp.concatenate([px[2, q], hid[q]], axis=0),
                LAST,
            )
        return weight_acc

    acc[...] = jnp.zeros((256, LANES), F32)
    acc[:168, :32] = lax.fori_loop(
        0, ROWS // WIDE, weight_rows, jnp.zeros((168, 32), F32)
    )
    turned = acc[...].T

    swap_copy = first_copy + REACH + 1
    for c in rights:
        c.wait()
    right = right_terms[0]
    for d in range(1, REACH + 1):
        right = right + rrecv[d]
    right = jnp.where(lane < ROWS, right, 0.0)
    lrsend[...] = jnp.concatenate([left_grad, right], axis=0).astype(BF16)
    trade = copy(swap_copy + 1, lrsend, lrrecv, me, other)

    part = dot(lrsend[:, :ROWS], full[...])
    for j in range(GROUP):
        r = 8 * (j // 4)
        buf[j, 0:8, :] = part[r : r + 8, cols(j % 4)]
        if j < 4:
            r = 8 * (j // 2)
            buf[j, 8:16, :] = turned[r : r + 8, cols(j % 2)]
        elif j < 6:
            r = 8 * (j - 2)
            buf[j, 8:16, :] = turned[r : r + 8, cols(1)]
        else:
            buf[j, 8:16, :] = jnp.zeros((8, LANES), F32)
    group_copy = swap_copy + 1
    stage = []
    for s in range(1, GROUP):
        target = lax.rem(place + s, GROUP)
        stage.append(copy(group_copy + s, buf.at[target], arecv.at[s], base + target, half))

    def head_rows_of(s, _):
        for u in range(BATCH):
            q = RIM // 2 + s * BATCH + u
            out = dot(zw[...], jnp.concatenate([hid[q], px[2, q]], axis=0))
            for t in range(TILES):
                z[q, t] = out[:, cols(t)]
        return 0

    lax.fori_loop(0, (ROWS + RIM) // BATCH, head_rows_of, 0)

    def align_rows(s, _):
        for u in range(BATCH):
            row = s * BATCH + u
            for n, a in enumerate(TAPS):
                for t in range(TILES):
                    zs[n, t, pl.ds(pl.multiple_of(row * 16, 16), 16), :] = z[row + RIM + a * d2, t]
        return 0

    lax.fori_loop(0, ROWS // BATCH, align_rows, 0)

    def tap_sum(t, a, row):
        return zs[a + 1, t, pl.ds(row, ROWS, stride=16), :]

    total = None
    for e in range(-2, 3):
        parts = [
            sum(tap_sum(t, a, (a + 1) * 3 + a + e + 1) for a in TAPS if -1 <= a + e <= 1)
            for t in range(TILES)
        ]
        parts = shift_tiles(parts, -e, d2)
        total = parts if total is None else [x + y for x, y in zip(total, parts)]
    own_lane = ids((ROWS, LANES), 1)
    for t in range(TILES):
        second = jnp.where(own_lane < edge[t, RIM : RIM + ROWS, :], total[t], 0.0)
        csend[:, cols(t)] = (tap_sum(t, 0, 9) + second).astype(BF16)
    swap = copy(swap_copy, csend, crecv, me, other)

    total = buf[place]
    for s, c in enumerate(stage):
        c.wait()
        total = total + arecv[s + 1]
    brecv[plane] = total

    def plane_copy(s, index, target):
        return pltpu.make_async_remote_copy(
            src_ref=brecv.at[index], dst_ref=brecv.at[index],
            send_sem=plane_send.at[s], recv_sem=plane_recv.at[index],
            device_id={"chrom": target * GROUP + place, "chan": half}, device_id_type=MESH,
        )

    planes = [(s, lax.rem(plane + s, PLANES)) for s in range(1, PLANES)]
    for s, p in planes:
        plane_copy(s, plane, p).start()

    for s, p in planes:
        plane_copy(s, plane, p).wait_send()
        plane_copy(s, p, p).wait_recv()
    total = brecv[0]
    for p in range(1, PLANES):
        total = total + brecv[p]
    fin[place] = total * scale

    def last_copy(s, index, target):
        return pltpu.make_async_remote_copy(
            src_ref=fin.at[index], dst_ref=fin.at[index],
            send_sem=last_send.at[s], recv_sem=last_recv.at[index],
            device_id={"chrom": base + target, "chan": half}, device_id_type=MESH,
        )

    others = [(s, lax.rem(place + s, GROUP)) for s in range(1, GROUP)]
    for s, p in others:
        last_copy(s, place, p).start()
    emb_copy.wait_send()
    w_copy.wait()
    trade.wait()
    both = jnp.concatenate([lrsend[...], lrrecv[...]], axis=0)
    weights = jnp.concatenate([wt[:, mine], wother[...]], axis=0)
    emb_grad[...] = dot(both, weights, FIRST)[:ROWS].astype(BF16)
    swap.wait()
    contacts[...] = csend[...].astype(F32) + crecv[...].astype(F32)

    for s, p in others:
        last_copy(s, place, p).wait_send()
        last_copy(s, p, p).wait_recv()


def band_call(scale, *operands):
    v = pl.BlockSpec(memory_space=pltpu.VMEM)
    copies = 5 + BEHIND + REACH + 3 + GROUP
    dma = pltpu.SemaphoreType.DMA
    return pl.pallas_call(
        functools.partial(band_kernel, scale),
        out_shape=(
            jax.ShapeDtypeStruct((ROWS, OFF), F32),
            jax.ShapeDtypeStruct((ROWS, 256), BF16),
            jax.ShapeDtypeStruct((GROUP, 16, LANES), F32),
        ),
        in_specs=[pl.BlockSpec(memory_space=pltpu.HBM)] * 9,
        out_specs=[v] * 3,
        scratch_shapes=[
            pltpu.SMEM((8,), jnp.int32),
            pltpu.SMEM((2,), jnp.int32),
            pltpu.SMEM((16,), F32),
            pltpu.VMEM((32, 512), BF16),
            pltpu.VMEM((32, 256), BF16),
            pltpu.VMEM((9, 16, 16), BF16),
            pltpu.VMEM((9, 16, 16), BF16),
            pltpu.VMEM((16, 144), BF16),
            pltpu.VMEM((16, 144), BF16),
            pltpu.VMEM((16, 24), BF16),
            pltpu.VMEM((16, 32), BF16),
            pltpu.VMEM((ROWS, 512), BF16),
            pltpu.VMEM((BEHIND + 2, 16, LANES), F32),
            pltpu.VMEM((SLAB, OFF), BF16),
            pltpu.VMEM((16, OFF + LANES), F32),
            pltpu.VMEM((16, LANES), F32),
            pltpu.VMEM((SLAB, 16, LANES), F32),
            pltpu.VMEM((TILES, SLAB, LANES), jnp.int32),
            pltpu.VMEM((SLAB, TILES, 8, LANES), F32),
            pltpu.VMEM((SLAB + 2 * RIM + BATCH, 16, OFF), F32),
            pltpu.VMEM((5, SLAB, 16, OFF), BF16),
            pltpu.VMEM((5, SLAB, 16, OFF), BF16),
            pltpu.VMEM((SLAB, 16, OFF), BF16),
            pltpu.VMEM((SLAB, TILES, 16, LANES), F32),
            pltpu.VMEM((3, TILES, ROWS * 16, LANES), F32),
            pltpu.VMEM((256, LANES), F32),
            pltpu.VMEM((ROWS, OFF), BF16),
            pltpu.VMEM((ROWS, OFF), BF16),
            pltpu.VMEM((REACH + 1, 16, LANES), F32),
            pltpu.VMEM((REACH + 1, 16, LANES), F32),
            pltpu.VMEM((32, LANES), BF16),
            pltpu.VMEM((32, LANES), BF16),
            pltpu.VMEM((GROUP, 16, LANES), F32),
            pltpu.VMEM((GROUP, 16, LANES), F32),
            pltpu.VMEM((PLANES, 16, LANES), F32),
            dma((9,)),
            dma((copies,)),
            dma((copies,)),
            dma((PLANES,)),
            dma((PLANES,)),
            dma((GROUP,)),
            dma((GROUP,)),
        ],
        compiler_params=pltpu.CompilerParams(
            collective_id=0, has_side_effects=True, vmem_limit_bytes=56 * 1024 * 1024
        ),
    )(*operands)


def output_kernel(
    head, fin, second_w, contacts_in, emb_grad_in,
    contacts, emb_grad, left_grad, right_grad, first_grad, second_grad, head_grad, wide,
):
    contacts[...] = contacts_in[...]
    emb_grad[...] = emb_grad_in[...]
    for j in range(GROUP):
        out = left_grad if j < 8 else right_grad
        r = 8 * ((j // 4) % 2)
        out[r : r + 8, cols(j % 4)] = fin[j, 0:8, :]
    wide[...] = jnp.zeros((LANES, 3 * LANES), F32)
    for j in range(4):
        r = 8 * (j // 2)
        wide[r : r + 8, cols(j % 2)] = fin[j, 8:16, :]
    wide[0:8, cols(2)] = fin[4, 8:16, :]
    wide[8:16, cols(2)] = fin[5, 8:16, :]
    turned = wide[...].T
    head_sum = wide[0:16, 154:155]
    head16 = head_column(head, 16)
    sums = jnp.zeros((16, 16), F32)
    for ab in range(9):
        a, b = ab // 3, ab % 3
        first_grad[ab] = turned[16 * ab : 16 * ab + 16, :16]
        row = 2 * LANES + 16 + 8 * a + (b - a + 2)
        moved = 0.5 * turned[row : row + 1, :16]
        second_grad[ab] = head16 * moved
        sums = sums + second_w[ab].astype(F32) * moved
    total = head_sum + jnp.sum(sums, axis=1, keepdims=True)
    head_grad[...] = diagonal(jnp.broadcast_to(total, (16, 16)), 16)


def output_call(head, fin, second_w, contacts, emb_grad):
    v = pl.BlockSpec(memory_space=pltpu.VMEM)
    m = pl.BlockSpec(memory_space=pltpu.SMEM)
    return pl.pallas_call(
        output_kernel,
        out_shape=(
            jax.ShapeDtypeStruct((ROWS, OFF), F32),
            jax.ShapeDtypeStruct((ROWS, 256), BF16),
            jax.ShapeDtypeStruct((16, 512), F32),
            jax.ShapeDtypeStruct((16, 512), F32),
            jax.ShapeDtypeStruct((9, 16, 16), F32),
            jax.ShapeDtypeStruct((9, 16, 16), F32),
            jax.ShapeDtypeStruct((1, 16), F32),
        ),
        in_specs=[m] + [v] * 4,
        out_specs=[v] * 7,
        scratch_shapes=[pltpu.VMEM((LANES, 3 * LANES), F32)],
    )(head, fin, second_w, contacts, emb_grad)


def on_device(
    embeddings,
    w_left,
    w_right,
    first_conv_weight,
    second_conv_weight,
    head_weight,
    cotangent,
    dilations,
    chrom_ends,
):
    bin_total = embeddings.shape[0] * lax.axis_size("chrom")
    scale = 1.0 / math.sqrt(bin_total * OFF)
    first_w = jnp.transpose(first_conv_weight, (1, 2, 0, 3)).reshape(9, 16, 16)
    second_w = jnp.transpose(second_conv_weight, (1, 2, 0, 3)).reshape(9, 16, 16)
    contacts, emb_grad, fin = band_call(
        scale, chrom_ends, dilations, head_weight, embeddings, w_left.T, w_right.T,
        first_w, second_w, cotangent,
    )
    contacts, emb_grad, left_grad, right_grad, first_grad, second_grad, head_grad = output_call(
        head_weight, fin, second_w, contacts, emb_grad
    )
    return (
        contacts,
        emb_grad,
        left_grad.T,
        right_grad.T,
        jnp.transpose(first_grad.reshape(3, 3, 16, 16), (2, 0, 1, 3)),
        jnp.transpose(second_grad.reshape(3, 3, 16, 16), (2, 0, 1, 3)),
        head_grad.reshape(16),
    )


def solution(mesh):
    in_specs = (
        P("chrom", "chan"),
        P(None, "chan"),
        P(None, "chan"),
        P("chan", None, None, None),
        P("chan", None, None, None),
        P("chan"),
        P("chrom", None),
        P(),
        P(),
    )
    out_specs = (
        P("chrom", None),
        P("chrom", "chan"),
        P(None, "chan"),
        P(None, "chan"),
        P("chan", None, None, None),
        P("chan", None, None, None),
        P("chan"),
    )
    return jax.shard_map(
        on_device, mesh=mesh, in_specs=in_specs, out_specs=out_specs, check_vma=False
    )
```

```python
import functools
import math

import jax
import jax.numpy as jnp
from jax import lax
from jax.experimental import pallas as pl
from jax.experimental.pallas import tpu as pltpu
from jax.sharding import PartitionSpec as P

MESH = pl.DeviceIdType.MESH
F32 = jnp.float32
BF16 = jnp.bfloat16
OFF = 512
LANES = 128
TILES = OFF // LANES
ROWS = 64
RIM = 16
SLAB = ROWS + 2 * RIM
REACH = OFF // ROWS
BEHIND = REACH + 1
TAPS = (-1, 0, 1)
BATCH = 8
WIDE = 16
LONG = 40
GROUP = 16
PLANES = 8
INV_ROOT_TWO = 0.7071067811865476
TWO_OVER_ROOT_PI = 1.1283791670955126
LOG2_E = 1.4426950408889634
LAST = (((1,), (1,)), ((), ()))
FIRST = (((0,), (0,)), ((), ()))


def ids(shape, dim):
    return lax.broadcasted_iota(jnp.int32, shape, dim)


def dot(a, b, dims=(((1,), (0,)), ((), ()))):
    return lax.dot_general(a, b, dims, preferred_element_type=F32)


def cols(t):
    return slice(t * LANES, (t + 1) * LANES)


def hop(me, distance):
    count = lax.axis_size("chrom")
    return lax.rem(me + distance + count, count)


def shift_tiles(tiles, count, dist):
    if count == 0:
        return tiles
    lane = ids((tiles[0].shape[0], LANES), 1)
    zero = jnp.zeros_like(tiles[0])
    if count > 0:
        amount = count * dist
        rolled = [pltpu.roll(t, amount, 1) for t in tiles]
        before = [zero] + rolled[:-1]
        return [jnp.where(lane < amount, b, r) for b, r in zip(before, rolled)]
    amount = LANES + count * dist
    rolled = [pltpu.roll(t, amount, 1) for t in tiles]
    after = rolled[1:] + [zero]
    return [jnp.where(lane < amount, r, a) for r, a in zip(rolled, after)]


def diagonal(column, lanes):
    shape = (16, lanes)
    return jnp.sum(jnp.where(ids(shape, 0) == ids(shape, 1), column, 0.0), axis=0, keepdims=True)


def head_column(head, lanes):
    sub = ids((16, lanes), 0)
    column = jnp.zeros((16, lanes), F32)
    for o in range(WIDE):
        column = jnp.where(sub == o, head[o], column)
    return column


def band_kernel(
    scale,
    ends_in, dil_in, head_in, emb, w_left, w_right, first_in, second_in, cot,
    contacts, emb_grad, fin,
    ends, dil, head,
    wt, wother, first_w, second_w, w1, w1t, vm, zw,
    full, slots, cot96, rb, lb, lcol, edge, vga, band, px, gy, hid, parts_of, z, zs, acc,
    csend, crecv, rsend, rrecv, lrsend, lrrecv, buf, arecv, brecv,
    load_sem, send_sem, recv_sem, plane_send, plane_recv, last_send, last_recv,
):
    me = lax.axis_index("chrom")
    half = lax.axis_index("chan")
    other = 1 - half
    place = lax.rem(me, GROUP)
    plane = me // GROUP
    base = me - place
    mine = pl.ds(pl.multiple_of(half * 256, 256), 256)
    theirs = pl.ds(pl.multiple_of(other * 256, 256), 256)
    lane = ids((16, LANES), 1)

    barrier = pltpu.get_barrier_semaphore()
    sources = [(hop(me, d), half) for d in range(1, BEHIND + 1)]
    sources += [(hop(me, -d), half) for d in range(1, REACH + 1)]
    sources += [(base + lax.rem(place + s, GROUP), half) for s in range(1, GROUP)]
    sources += [(lax.rem(plane + s, PLANES) * GROUP + place, half) for s in range(1, PLANES)]
    sources += [(me, other)]
    for chrom, chan in sources:
        pl.semaphore_signal(
            barrier, inc=1, device_id={"chrom": chrom, "chan": chan}, device_id_type=MESH
        )

    def copy(index, src, dst, chrom, chan):
        c = pltpu.make_async_remote_copy(
            src_ref=src, dst_ref=dst, send_sem=send_sem.at[index], recv_sem=recv_sem.at[index],
            device_id={"chrom": chrom, "chan": chan}, device_id_type=MESH,
        )
        c.start()
        return c

    loads = [
        pltpu.make_async_copy(src, dst, load_sem.at[n])
        for n, (src, dst) in enumerate(
            [
                (emb, full.at[:, mine]),
                (w_left, wt.at[pl.ds(0, 16)]),
                (w_right, wt.at[pl.ds(16, 16)]),
                (first_in, first_w),
                (second_in, second_w),
                (cot, cot96.at[pl.ds(RIM, ROWS)]),
                (ends_in, ends),
                (dil_in, dil),
                (head_in, head),
            ]
        )
    ]
    for load in loads:
        load.start()
    pl.semaphore_wait(barrier, len(sources))

    emb_copy = copy(0, emb, full.at[:, mine], me, other)
    rims = [
        copy(1, cot.at[pl.ds(ROWS - RIM, RIM)], cot96.at[pl.ds(0, RIM)], hop(me, 1), half),
        copy(2, cot.at[pl.ds(0, RIM)], cot96.at[pl.ds(RIM + ROWS, RIM)], hop(me, -1), half),
    ]
    for load in loads:
        load.wait()
    d1 = dil[0]
    d2 = dil[1]
    w_copy = copy(3, wt.at[:, theirs], wother, me, other)

    head16 = head_column(head, 16)
    sub16 = ids((16, 16), 0)
    rows = jnp.zeros((16, 16), F32)
    form = jnp.zeros((16, 144), F32)
    form_t = jnp.zeros((16, 144), F32)
    for ab in range(9):
        at = (ids((16, 144), 1) == ids((16, 144), 0) + 16 * ab).astype(BF16)
        form = form + dot(first_w[ab], at)
        form_t = form_t + dot(first_w[ab], at, FIRST)
        row = jnp.sum(head16 * second_w[ab].astype(F32), axis=0, keepdims=True)
        rows = jnp.where(sub16 == ab, row, rows)
    w1[...] = form.astype(BF16)
    w1t[...] = form_t.astype(BF16)
    head_rows = jnp.where(sub16 == 9, diagonal(head16, 16), 0.0).astype(BF16)
    rows = rows.astype(BF16)
    low = (ids((16, 32), 1) == ids((16, 32), 0)).astype(BF16)
    high = (ids((16, 32), 1) == ids((16, 32), 0) + 16).astype(BF16)
    half_rows = rows * jnp.bfloat16(0.5)
    zw[...] = (dot(half_rows, low) + dot(head_rows, high)).astype(BF16)
    tap = ids((16, 24), 0)
    column = tap + 4 * ((tap >= 3).astype(jnp.int32) + (tap >= 6).astype(jnp.int32)) + 2
    spot = ((ids((16, 24), 1) == column) & (tap < 9)).astype(BF16)
    vm[...] = dot(half_rows, spot, FIRST).astype(BF16)

    emb_copy.wait_recv()
    twice = jnp.concatenate([full[...], full[...]], axis=0)
    slots[1] = jnp.where(lane < ROWS, dot(wt[16:32, :], twice, LAST), dot(wt[0:16, :], twice, LAST))
    tiles = [
        copy(3 + d, slots.at[1], slots.at[1 + d], hop(me, -d), half)
        for d in range(1, BEHIND + 1)
    ]
    tiles.append(copy(4 + BEHIND, slots.at[1], slots.at[0], hop(me, 1), half))
    for c in rims:
        c.wait()
    big = jnp.int32(1 << 30)
    bins = ids((SLAB, LANES), 0) + (me * ROWS - RIM)
    stop = jnp.full((SLAB, LANES), big)
    for j in range(8):
        stop = jnp.minimum(stop, jnp.where(ends[j] > bins, ends[j], big))
    width = jnp.where((bins >= 0) & (stop < big), jnp.minimum(stop - bins, OFF), 0)
    slab_lane = ids((SLAB, LANES), 1)
    masked = []
    for t in range(TILES):
        edge[t] = width - t * LANES
        masked.append(
            jnp.where(slab_lane < width - t * LANES, cot96[:, cols(t)].astype(F32), 0.0)
        )
    for e in range(-2, 3):
        for t, tile in enumerate(shift_tiles(masked, e, d2)):
            vga[:, t, e + 2, :] = tile
    for e in range(5, 8):
        for t in range(TILES):
            vga[:, t, e, :] = jnp.zeros((SLAB, LANES), F32)

    for c in (tiles[-1], tiles[0]):
        c.wait()
    lb[...] = jnp.where(
        lane < RIM,
        pltpu.roll(slots[0], 16, 1),
        jnp.where(lane < RIM + ROWS, pltpu.roll(slots[1], 80, 1), pltpu.roll(slots[2], 16, 1)),
    )
    for q in range(SLAB):
        lcol[q] = jnp.broadcast_to(lb[:, q : q + 1], (16, LANES))
    for t in range(TILES + 1):
        for c in tiles[max(2 * t - 1, 1) : min(2 * t + 1, BEHIND)]:
            c.wait()
        before = pltpu.roll(slots[2 * t], 96, 1)
        inside = pltpu.roll(slots[2 * t + 1], 32, 1)
        after = pltpu.roll(slots[2 * t + 2], 96, 1)
        rb[:, cols(t)] = jnp.where(lane < 32, before, jnp.where(lane < 96, inside, after))

    def masks(q):
        return [lane < edge[t, pl.ds(q, 1), :] for t in range(TILES)]

    def band_row(p):
        back = lax.rem(2 * LANES - p, LANES)
        rolled = [pltpu.roll(rb[:, cols(t)], back, 1) for t in range(TILES + 1)]
        for t in range(TILES):
            band[p, :, cols(t)] = jnp.where(lane < LANES - p, rolled[t], rolled[t + 1])

    def pair_row(q):
        left = lcol[q]
        limits = [edge[t, pl.ds(q, 1), :] for t in range(TILES)]
        for e in range(-2, 3):
            move = e * d1
            for t in range(TILES):
                mask = lane < limits[t] - move
                if e < 0 and t == 0:
                    mask = mask & (lane >= -move)
                value = left * band[q + RIM + move, :, cols(t)]
                px[e + 2, q, :, cols(t)] = jnp.where(mask, value, 0.0).astype(BF16)

    def first_band_rows(s, _):
        for u in range(BATCH):
            band_row(s * BATCH + u)
        return 0

    def pair_rows(s, _):
        for u in range(BATCH):
            pair_row(s * BATCH + u)
            band_row(2 * RIM + (s + 1) * BATCH + u)
        return 0

    lax.fori_loop(0, 2 * RIM // BATCH + 1, first_band_rows, 0)
    lax.fori_loop(0, SLAB // BATCH, pair_rows, 0)

    def tap_rows(q):
        return jnp.concatenate(
            [
                jnp.concatenate([vga[q - a * d2, t] for a in TAPS], axis=0)
                for t in range(TILES)
            ],
            axis=1,
        ).astype(BF16)

    def hidden_dots(q):
        stack = jnp.concatenate([px[b - a + 2, q + a * d1] for a in TAPS for b in TAPS], axis=0)
        return dot(w1[...], stack), dot(vm[...], tap_rows(q))

    def hidden_values(q, first, grad_hidden):
        mask = jnp.concatenate(masks(q), axis=1)
        first = jnp.where(mask, first, 0.0)
        scaled = first * INV_ROOT_TWO
        cdf = 1.0 + lax.erf(scaled)
        slope = cdf + scaled * jnp.exp2(scaled * scaled * -LOG2_E) * TWO_OVER_ROOT_PI
        hidden = (first * cdf).astype(BF16)
        grad_first = jnp.where(mask, slope * grad_hidden, 0.0).astype(BF16)
        parts = [grad_first[:, cols(t)] for t in range(TILES)]
        for e in range(-2, 3):
            for t, tile in enumerate(shift_tiles(parts, e, d1)):
                gy[e + 2, q, :, cols(t)] = tile
        hid[q] = hidden

    def hidden_rows(s, _):
        lag = 3
        dots = {}
        for u in range(LONG + lag):
            q = RIM // 2 + s * LONG + u
            if u < LONG:
                dots[u] = hidden_dots(q)
            if u >= lag:
                hidden_values(q - lag, *dots.pop(u - lag))
        return 0

    lax.fori_loop(0, (ROWS + RIM) // LONG, hidden_rows, 0)

    def grad_rows(s, carry):
        for u in range(WIDE):
            carry = grad_row(s * WIDE + u, carry)
        return carry

    head_full = head_column(head, LANES)

    def grad_row(row, right_acc):
        q = row + RIM
        stack = jnp.concatenate([gy[b - a + 2, q - a * d1] for a in TAPS for b in TAPS], axis=0)
        grad_pair = dot(w1t[...], stack)
        left = lcol[q]
        spread = []
        for t, mask in enumerate(masks(q)):
            g = vga[q, t, 2:3, :]
            part = jnp.where(mask, grad_pair[:, cols(t)] + head_full * g, 0.0)
            parts_of[row, :, cols(t)] = part
            spread.append(pltpu.roll(part * left, row, 1))
        zero = jnp.zeros((16, LANES), F32)
        return tuple(
            r + jnp.where(lane < row, b, a)
            for r, b, a in zip(right_acc, [zero] + spread, spread + [zero])
        )

    right_terms = lax.fori_loop(
        0, ROWS // WIDE, grad_rows, (jnp.zeros((16, LANES), F32),) * (TILES + 1)
    )

    for d in range(1, REACH + 1):
        piece = right_terms[d // 2]
        rsend[d] = pltpu.roll(piece, ROWS, 1) if d % 2 else piece
    first_copy = 5 + BEHIND
    rights = [
        copy(first_copy + d, rsend.at[d], rrecv.at[d], hop(me, d), half)
        for d in range(1, REACH + 1)
    ]

    def left_rows(s, left_acc):
        for u in range(WIDE):
            row = s * WIDE + u
            prods = [
                parts_of[row, :, cols(t)] * band[row + 2 * RIM, :, cols(t)] for t in range(TILES)
            ]
            total = (prods[0] + prods[1]) + (prods[2] + prods[3])
            left_acc = jnp.where(lane == row, jnp.sum(total, axis=1, keepdims=True), left_acc)
        return left_acc

    left_grad = lax.fori_loop(0, ROWS // WIDE, left_rows, jnp.zeros((16, LANES), F32))

    def weight_rows(s, weight_acc):
        for u in range(WIDE):
            q = RIM + s * WIDE + u
            taken = [gy[b - a + 2, q - a * d1] for a in TAPS for b in TAPS]
            weight_acc = weight_acc + dot(
                jnp.concatenate(taken + [tap_rows(q)], axis=0),
                jnp.concatenate([px[2, q], hid[q]], axis=0),
                LAST,
            )
        return weight_acc

    acc[...] = jnp.zeros((256, LANES), F32)
    acc[:168, :32] = lax.fori_loop(
        0, ROWS // WIDE, weight_rows, jnp.zeros((168, 32), F32)
    )
    turned = acc[...].T

    swap_copy = first_copy + REACH + 1
    for c in rights:
        c.wait()
    right = right_terms[0]
    for d in range(1, REACH + 1):
        right = right + rrecv[d]
    right = jnp.where(lane < ROWS, right, 0.0)
    lrsend[...] = jnp.concatenate([left_grad, right], axis=0).astype(BF16)
    trade = copy(swap_copy + 1, lrsend, lrrecv, me, other)

    part = dot(lrsend[:, :ROWS], full[...])
    for j in range(GROUP):
        r = 8 * (j // 4)
        buf[j, 0:8, :] = part[r : r + 8, cols(j % 4)]
        if j < 4:
            r = 8 * (j // 2)
            buf[j, 8:16, :] = turned[r : r + 8, cols(j % 2)]
        elif j < 6:
            r = 8 * (j - 2)
            buf[j, 8:16, :] = turned[r : r + 8, cols(1)]
        else:
            buf[j, 8:16, :] = jnp.zeros((8, LANES), F32)
    group_copy = swap_copy + 1
    stage = []
    for s in range(1, GROUP):
        target = lax.rem(place + s, GROUP)
        stage.append(copy(group_copy + s, buf.at[target], arecv.at[s], base + target, half))

    def head_rows_of(s, _):
        for u in range(BATCH):
            q = RIM // 2 + s * BATCH + u
            out = dot(zw[...], jnp.concatenate([hid[q], px[2, q]], axis=0))
            for t in range(TILES):
                z[q, t] = out[:, cols(t)]
        return 0

    lax.fori_loop(0, (ROWS + RIM) // BATCH, head_rows_of, 0)

    def align_rows(s, _):
        for u in range(BATCH):
            row = s * BATCH + u
            for n, a in enumerate(TAPS):
                for t in range(TILES):
                    zs[n, t, pl.ds(pl.multiple_of(row * 16, 16), 16), :] = z[row + RIM + a * d2, t]
        return 0

    lax.fori_loop(0, ROWS // BATCH, align_rows, 0)

    def tap_sum(t, a, row):
        return zs[a + 1, t, pl.ds(row, ROWS, stride=16), :]

    total = None
    for e in range(-2, 3):
        parts = [
            sum(tap_sum(t, a, (a + 1) * 3 + a + e + 1) for a in TAPS if -1 <= a + e <= 1)
            for t in range(TILES)
        ]
        parts = shift_tiles(parts, -e, d2)
        total = parts if total is None else [x + y for x, y in zip(total, parts)]
    own_lane = ids((ROWS, LANES), 1)
    for t in range(TILES):
        second = jnp.where(own_lane < edge[t, RIM : RIM + ROWS, :], total[t], 0.0)
        csend[:, cols(t)] = (tap_sum(t, 0, 9) + second).astype(BF16)
    swap = copy(swap_copy, csend, crecv, me, other)

    total = buf[place]
    for s, c in enumerate(stage):
        c.wait()
        total = total + arecv[s + 1]
    brecv[plane] = total

    def plane_copy(s, index, target):
        return pltpu.make_async_remote_copy(
            src_ref=brecv.at[index], dst_ref=brecv.at[index],
            send_sem=plane_send.at[s], recv_sem=plane_recv.at[index],
            device_id={"chrom": target * GROUP + place, "chan": half}, device_id_type=MESH,
        )

    planes = [(s, lax.rem(plane + s, PLANES)) for s in range(1, PLANES)]
    for s, p in planes:
        plane_copy(s, plane, p).start()

    for s, p in planes:
        plane_copy(s, plane, p).wait_send()
        plane_copy(s, p, p).wait_recv()
    total = brecv[0]
    for p in range(1, PLANES):
        total = total + brecv[p]
    fin[place] = total * scale

    def last_copy(s, index, target):
        return pltpu.make_async_remote_copy(
            src_ref=fin.at[index], dst_ref=fin.at[index],
            send_sem=last_send.at[s], recv_sem=last_recv.at[index],
            device_id={"chrom": base + target, "chan": half}, device_id_type=MESH,
        )

    others = [(s, lax.rem(place + s, GROUP)) for s in range(1, GROUP)]
    for s, p in others:
        last_copy(s, place, p).start()
    emb_copy.wait_send()
    w_copy.wait()
    trade.wait()
    both = jnp.concatenate([lrsend[...], lrrecv[...]], axis=0)
    weights = jnp.concatenate([wt[:, mine], wother[...]], axis=0)
    emb_grad[...] = dot(both, weights, FIRST)[:ROWS].astype(BF16)
    swap.wait()
    contacts[...] = csend[...].astype(F32) + crecv[...].astype(F32)

    for s, p in others:
        last_copy(s, place, p).wait_send()
        last_copy(s, p, p).wait_recv()


def band_call(scale, *operands):
    v = pl.BlockSpec(memory_space=pltpu.VMEM)
    copies = 5 + BEHIND + REACH + 3 + GROUP
    dma = pltpu.SemaphoreType.DMA
    return pl.pallas_call(
        functools.partial(band_kernel, scale),
        out_shape=(
            jax.ShapeDtypeStruct((ROWS, OFF), F32),
            jax.ShapeDtypeStruct((ROWS, 256), BF16),
            jax.ShapeDtypeStruct((GROUP, 16, LANES), F32),
        ),
        in_specs=[pl.BlockSpec(memory_space=pltpu.HBM)] * 9,
        out_specs=[v] * 3,
        scratch_shapes=[
            pltpu.SMEM((8,), jnp.int32),
            pltpu.SMEM((2,), jnp.int32),
            pltpu.SMEM((16,), F32),
            pltpu.VMEM((32, 512), BF16),
            pltpu.VMEM((32, 256), BF16),
            pltpu.VMEM((9, 16, 16), BF16),
            pltpu.VMEM((9, 16, 16), BF16),
            pltpu.VMEM((16, 144), BF16),
            pltpu.VMEM((16, 144), BF16),
            pltpu.VMEM((16, 24), BF16),
            pltpu.VMEM((16, 32), BF16),
            pltpu.VMEM((ROWS, 512), BF16),
            pltpu.VMEM((BEHIND + 2, 16, LANES), F32),
            pltpu.VMEM((SLAB, OFF), BF16),
            pltpu.VMEM((16, OFF + LANES), F32),
            pltpu.VMEM((16, LANES), F32),
            pltpu.VMEM((SLAB, 16, LANES), F32),
            pltpu.VMEM((TILES, SLAB, LANES), jnp.int32),
            pltpu.VMEM((SLAB, TILES, 8, LANES), F32),
            pltpu.VMEM((SLAB + 2 * RIM + BATCH, 16, OFF), F32),
            pltpu.VMEM((5, SLAB, 16, OFF), BF16),
            pltpu.VMEM((5, SLAB, 16, OFF), BF16),
            pltpu.VMEM((SLAB, 16, OFF), BF16),
            pltpu.VMEM((ROWS, 16, OFF), F32),
            pltpu.VMEM((SLAB, TILES, 16, LANES), F32),
            pltpu.VMEM((3, TILES, ROWS * 16, LANES), F32),
            pltpu.VMEM((256, LANES), F32),
            pltpu.VMEM((ROWS, OFF), BF16),
            pltpu.VMEM((ROWS, OFF), BF16),
            pltpu.VMEM((REACH + 1, 16, LANES), F32),
            pltpu.VMEM((REACH + 1, 16, LANES), F32),
            pltpu.VMEM((32, LANES), BF16),
            pltpu.VMEM((32, LANES), BF16),
            pltpu.VMEM((GROUP, 16, LANES), F32),
            pltpu.VMEM((GROUP, 16, LANES), F32),
            pltpu.VMEM((PLANES, 16, LANES), F32),
            dma((9,)),
            dma((copies,)),
            dma((copies,)),
            dma((PLANES,)),
            dma((PLANES,)),
            dma((GROUP,)),
            dma((GROUP,)),
        ],
        compiler_params=pltpu.CompilerParams(
            collective_id=0, has_side_effects=True, vmem_limit_bytes=56 * 1024 * 1024
        ),
    )(*operands)


def output_kernel(
    head, fin, second_w, contacts_in, emb_grad_in,
    contacts, emb_grad, left_grad, right_grad, first_grad, second_grad, head_grad, wide,
):
    contacts[...] = contacts_in[...]
    emb_grad[...] = emb_grad_in[...]
    for j in range(GROUP):
        out = left_grad if j < 8 else right_grad
        r = 8 * ((j // 4) % 2)
        out[r : r + 8, cols(j % 4)] = fin[j, 0:8, :]
    wide[...] = jnp.zeros((LANES, 3 * LANES), F32)
    for j in range(4):
        r = 8 * (j // 2)
        wide[r : r + 8, cols(j % 2)] = fin[j, 8:16, :]
    wide[0:8, cols(2)] = fin[4, 8:16, :]
    wide[8:16, cols(2)] = fin[5, 8:16, :]
    turned = wide[...].T
    head_sum = wide[0:16, 154:155]
    head16 = head_column(head, 16)
    sums = jnp.zeros((16, 16), F32)
    for ab in range(9):
        a, b = ab // 3, ab % 3
        first_grad[ab] = turned[16 * ab : 16 * ab + 16, :16]
        row = 2 * LANES + 16 + 8 * a + (b - a + 2)
        moved = 0.5 * turned[row : row + 1, :16]
        second_grad[ab] = head16 * moved
        sums = sums + second_w[ab].astype(F32) * moved
    total = head_sum + jnp.sum(sums, axis=1, keepdims=True)
    head_grad[...] = diagonal(jnp.broadcast_to(total, (16, 16)), 16)


def output_call(head, fin, second_w, contacts, emb_grad):
    v = pl.BlockSpec(memory_space=pltpu.VMEM)
    m = pl.BlockSpec(memory_space=pltpu.SMEM)
    return pl.pallas_call(
        output_kernel,
        out_shape=(
            jax.ShapeDtypeStruct((ROWS, OFF), F32),
            jax.ShapeDtypeStruct((ROWS, 256), BF16),
            jax.ShapeDtypeStruct((16, 512), F32),
            jax.ShapeDtypeStruct((16, 512), F32),
            jax.ShapeDtypeStruct((9, 16, 16), F32),
            jax.ShapeDtypeStruct((9, 16, 16), F32),
            jax.ShapeDtypeStruct((1, 16), F32),
        ),
        in_specs=[m] + [v] * 4,
        out_specs=[v] * 7,
        scratch_shapes=[pltpu.VMEM((LANES, 3 * LANES), F32)],
    )(head, fin, second_w, contacts, emb_grad)


def on_device(
    embeddings,
    w_left,
    w_right,
    first_conv_weight,
    second_conv_weight,
    head_weight,
    cotangent,
    dilations,
    chrom_ends,
):
    bin_total = embeddings.shape[0] * lax.axis_size("chrom")
    scale = 1.0 / math.sqrt(bin_total * OFF)
    first_w = jnp.transpose(first_conv_weight, (1, 2, 0, 3)).reshape(9, 16, 16)
    second_w = jnp.transpose(second_conv_weight, (1, 2, 0, 3)).reshape(9, 16, 16)
    contacts, emb_grad, fin = band_call(
        scale, chrom_ends, dilations, head_weight, embeddings, w_left.T, w_right.T,
        first_w, second_w, cotangent,
    )
    contacts, emb_grad, left_grad, right_grad, first_grad, second_grad, head_grad = output_call(
        head_weight, fin, second_w, contacts, emb_grad
    )
    return (
        contacts,
        emb_grad,
        left_grad.T,
        right_grad.T,
        jnp.transpose(first_grad.reshape(3, 3, 16, 16), (2, 0, 1, 3)),
        jnp.transpose(second_grad.reshape(3, 3, 16, 16), (2, 0, 1, 3)),
        head_grad.reshape(16),
    )


def solution(mesh):
    in_specs = (
        P("chrom", "chan"),
        P(None, "chan"),
        P(None, "chan"),
        P("chan", None, None, None),
        P("chan", None, None, None),
        P("chan"),
        P("chrom", None),
        P(),
        P(),
    )
    out_specs = (
        P("chrom", None),
        P("chrom", "chan"),
        P(None, "chan"),
        P(None, "chan"),
        P("chan", None, None, None),
        P("chan", None, None, None),
        P("chan"),
    )
    return jax.shard_map(
        on_device, mesh=mesh, in_specs=in_specs, out_specs=out_specs, check_vma=False
    )
```

```python
import functools
import math

import jax
import jax.numpy as jnp
from jax import lax
from jax.experimental import pallas as pl
from jax.experimental.pallas import tpu as pltpu
from jax.sharding import PartitionSpec as P

MESH = pl.DeviceIdType.MESH
F32 = jnp.float32
BF16 = jnp.bfloat16
OFF = 512
LANES = 128
TILES = OFF // LANES
ROWS = 64
RIM = 16
SLAB = ROWS + 2 * RIM
REACH = OFF // ROWS
BEHIND = REACH + 1
TAPS = (-1, 0, 1)
BATCH = 8
WIDE = 16
LONG = 40
GROUP = 16
PLANES = 8
INV_ROOT_TWO = 0.7071067811865476
TWO_OVER_ROOT_PI = 1.1283791670955126
LOG2_E = 1.4426950408889634
LAST = (((1,), (1,)), ((), ()))
FIRST = (((0,), (0,)), ((), ()))


def ids(shape, dim):
    return lax.broadcasted_iota(jnp.int32, shape, dim)


def dot(a, b, dims=(((1,), (0,)), ((), ()))):
    return lax.dot_general(a, b, dims, preferred_element_type=F32)


def cols(t):
    return slice(t * LANES, (t + 1) * LANES)


def hop(me, distance):
    count = lax.axis_size("chrom")
    return lax.rem(me + distance + count, count)


def shift_tiles(tiles, count, dist):
    if count == 0:
        return tiles
    lane = ids((tiles[0].shape[0], LANES), 1)
    zero = jnp.zeros_like(tiles[0])
    if count > 0:
        amount = count * dist
        rolled = [pltpu.roll(t, amount, 1) for t in tiles]
        before = [zero] + rolled[:-1]
        return [jnp.where(lane < amount, b, r) for b, r in zip(before, rolled)]
    amount = LANES + count * dist
    rolled = [pltpu.roll(t, amount, 1) for t in tiles]
    after = rolled[1:] + [zero]
    return [jnp.where(lane < amount, r, a) for r, a in zip(rolled, after)]


def diagonal(column, lanes):
    shape = (16, lanes)
    return jnp.sum(jnp.where(ids(shape, 0) == ids(shape, 1), column, 0.0), axis=0, keepdims=True)


def head_column(head, lanes):
    sub = ids((16, lanes), 0)
    column = jnp.zeros((16, lanes), F32)
    for o in range(WIDE):
        column = jnp.where(sub == o, head[o], column)
    return column


def band_kernel(
    scale,
    ends_in, dil_in, head_in, emb, w_left, w_right, first_in, second_in, cot,
    contacts, emb_grad, fin,
    ends, dil, head,
    wt, wother, first_w, second_w, w1, w1t, vm, zw,
    full, slots, cot96, rb, lb, lcol, edge, vga, band, px, gy, hid, parts_of, z, zs, acc,
    csend, crecv, rsend, rrecv, lrsend, lrrecv, buf, arecv, brecv,
    load_sem, send_sem, recv_sem, plane_send, plane_recv, last_send, last_recv,
):
    me = lax.axis_index("chrom")
    half = lax.axis_index("chan")
    other = 1 - half
    place = lax.rem(me, GROUP)
    plane = me // GROUP
    base = me - place
    mine = pl.ds(pl.multiple_of(half * 256, 256), 256)
    theirs = pl.ds(pl.multiple_of(other * 256, 256), 256)
    lane = ids((16, LANES), 1)

    barrier = pltpu.get_barrier_semaphore()
    far_first = sorted(range(1, PLANES), key=lambda s: -min(s, PLANES - s))
    sources = [(lax.rem(plane + s, PLANES) * GROUP + place, half) for s in far_first]
    sources += [(hop(me, d), half) for d in range(BEHIND, 0, -1)]
    sources += [(hop(me, -d), half) for d in range(REACH, 0, -1)]
    sources += [(me, other)]
    sources += [(base + lax.rem(place + s, GROUP), half) for s in range(1, GROUP)]
    for chrom, chan in sources:
        pl.semaphore_signal(
            barrier, inc=1, device_id={"chrom": chrom, "chan": chan}, device_id_type=MESH
        )

    def copy(index, src, dst, chrom, chan):
        c = pltpu.make_async_remote_copy(
            src_ref=src, dst_ref=dst, send_sem=send_sem.at[index], recv_sem=recv_sem.at[index],
            device_id={"chrom": chrom, "chan": chan}, device_id_type=MESH,
        )
        c.start()
        return c

    loads = [
        pltpu.make_async_copy(src, dst, load_sem.at[n])
        for n, (src, dst) in enumerate(
            [
                (emb, full.at[:, mine]),
                (w_left, wt.at[pl.ds(0, 16)]),
                (w_right, wt.at[pl.ds(16, 16)]),
                (first_in, first_w),
                (second_in, second_w),
                (cot, cot96.at[pl.ds(RIM, ROWS)]),
                (ends_in, ends),
                (dil_in, dil),
                (head_in, head),
            ]
        )
    ]
    for load in loads:
        load.start()
    pl.semaphore_wait(barrier, len(sources))

    emb_copy = copy(0, emb, full.at[:, mine], me, other)
    rims = [
        copy(1, cot.at[pl.ds(ROWS - RIM, RIM)], cot96.at[pl.ds(0, RIM)], hop(me, 1), half),
        copy(2, cot.at[pl.ds(0, RIM)], cot96.at[pl.ds(RIM + ROWS, RIM)], hop(me, -1), half),
    ]
    for load in loads:
        load.wait()
    d1 = dil[0]
    d2 = dil[1]
    w_copy = copy(3, wt.at[:, theirs], wother, me, other)

    head16 = head_column(head, 16)
    sub16 = ids((16, 16), 0)
    rows = jnp.zeros((16, 16), F32)
    form = jnp.zeros((16, 144), F32)
    form_t = jnp.zeros((16, 144), F32)
    for ab in range(9):
        at = (ids((16, 144), 1) == ids((16, 144), 0) + 16 * ab).astype(BF16)
        form = form + dot(first_w[ab], at)
        form_t = form_t + dot(first_w[ab], at, FIRST)
        row = jnp.sum(head16 * second_w[ab].astype(F32), axis=0, keepdims=True)
        rows = jnp.where(sub16 == ab, row, rows)
    w1[...] = form.astype(BF16)
    w1t[...] = form_t.astype(BF16)
    head_rows = jnp.where(sub16 == 9, diagonal(head16, 16), 0.0).astype(BF16)
    rows = rows.astype(BF16)
    low = (ids((16, 32), 1) == ids((16, 32), 0)).astype(BF16)
    high = (ids((16, 32), 1) == ids((16, 32), 0) + 16).astype(BF16)
    half_rows = rows * jnp.bfloat16(0.5)
    zw[...] = (dot(half_rows, low) + dot(head_rows, high)).astype(BF16)
    tap = ids((16, 24), 0)
    column = tap + 4 * ((tap >= 3).astype(jnp.int32) + (tap >= 6).astype(jnp.int32)) + 2
    spot = ((ids((16, 24), 1) == column) & (tap < 9)).astype(BF16)
    vm[...] = dot(half_rows, spot, FIRST).astype(BF16)

    emb_copy.wait_recv()
    twice = jnp.concatenate([full[...], full[...]], axis=0)
    slots[1] = jnp.where(lane < ROWS, dot(wt[16:32, :], twice, LAST), dot(wt[0:16, :], twice, LAST))
    tiles = [
        copy(3 + d, slots.at[1], slots.at[1 + d], hop(me, -d), half)
        for d in range(1, BEHIND + 1)
    ]
    tiles.append(copy(4 + BEHIND, slots.at[1], slots.at[0], hop(me, 1), half))
    for c in rims:
        c.wait()
    big = jnp.int32(1 << 30)
    bins = ids((SLAB, LANES), 0) + (me * ROWS - RIM)
    stop = jnp.full((SLAB, LANES), big)
    for j in range(8):
        stop = jnp.minimum(stop, jnp.where(ends[j] > bins, ends[j], big))
    width = jnp.where((bins >= 0) & (stop < big), jnp.minimum(stop - bins, OFF), 0)
    slab_lane = ids((SLAB, LANES), 1)
    masked = []
    for t in range(TILES):
        edge[t] = width - t * LANES
        masked.append(
            jnp.where(slab_lane < width - t * LANES, cot96[:, cols(t)].astype(F32), 0.0)
        )
    for e in range(-2, 3):
        for t, tile in enumerate(shift_tiles(masked, e, d2)):
            vga[:, t, e + 2, :] = tile
    for e in range(5, 8):
        for t in range(TILES):
            vga[:, t, e, :] = jnp.zeros((SLAB, LANES), F32)

    for c in (tiles[-1], tiles[0]):
        c.wait()
    lb[...] = jnp.where(
        lane < RIM,
        pltpu.roll(slots[0], 16, 1),
        jnp.where(lane < RIM + ROWS, pltpu.roll(slots[1], 80, 1), pltpu.roll(slots[2], 16, 1)),
    )
    for q in range(SLAB):
        lcol[q] = jnp.broadcast_to(lb[:, q : q + 1], (16, LANES))
    for t in range(TILES + 1):
        for c in tiles[max(2 * t - 1, 1) : min(2 * t + 1, BEHIND)]:
            c.wait()
        before = pltpu.roll(slots[2 * t], 96, 1)
        inside = pltpu.roll(slots[2 * t + 1], 32, 1)
        after = pltpu.roll(slots[2 * t + 2], 96, 1)
        rb[:, cols(t)] = jnp.where(lane < 32, before, jnp.where(lane < 96, inside, after))

    def masks(q):
        return [lane < edge[t, pl.ds(q, 1), :] for t in range(TILES)]

    def band_row(p):
        back = lax.rem(2 * LANES - p, LANES)
        rolled = [pltpu.roll(rb[:, cols(t)], back, 1) for t in range(TILES + 1)]
        for t in range(TILES):
            band[p, :, cols(t)] = jnp.where(lane < LANES - p, rolled[t], rolled[t + 1])

    def pair_row(q):
        left = lcol[q]
        limits = [edge[t, pl.ds(q, 1), :] for t in range(TILES)]
        for e in range(-2, 2):
            move = e * d1
            tiles = []
            for t in range(TILES):
                mask = lane < limits[t] - move
                if e < 0 and t == 0:
                    mask = mask & (lane >= -move)
                value = left * band[q + RIM + move, :, cols(t)]
                tiles.append(jnp.where(mask, value, 0.0).astype(BF16))
                px[e + 2, q, :, cols(t)] = tiles[t]
            if e == 0:
                centre = tiles
        for t, tile in enumerate(shift_tiles(centre, -2, d1)):
            px[4, q, :, cols(t)] = tile

    def first_band_rows(s, _):
        for u in range(20):
            band_row(s * 20 + u)
        return 0

    def pair_rows(s, _):
        for u in range(BATCH):
            pair_row(s * BATCH + u)
            band_row(2 * RIM + (s + 1) * BATCH + u)
        return 0

    lax.fori_loop(0, (2 * RIM + BATCH) // 20, first_band_rows, 0)
    lax.fori_loop(0, SLAB // BATCH, pair_rows, 0)

    def tap_rows(q):
        return jnp.concatenate(
            [
                jnp.concatenate([vga[q - a * d2, t] for a in TAPS], axis=0)
                for t in range(TILES)
            ],
            axis=1,
        ).astype(BF16)

    def hidden_dots(q):
        stack = jnp.concatenate([px[b - a + 2, q + a * d1] for a in TAPS for b in TAPS], axis=0)
        return dot(w1[...], stack), dot(vm[...], tap_rows(q))

    def hidden_values(q, first, grad_hidden):
        mask = jnp.concatenate(masks(q), axis=1)
        first = jnp.where(mask, first, 0.0)
        scaled = first * INV_ROOT_TWO
        cdf = 1.0 + lax.erf(scaled)
        slope = cdf + scaled * jnp.exp2(scaled * scaled * -LOG2_E) * TWO_OVER_ROOT_PI
        hidden = (first * cdf).astype(BF16)
        grad_first = jnp.where(mask, slope * grad_hidden, 0.0).astype(BF16)
        parts = [grad_first[:, cols(t)] for t in range(TILES)]
        for e in range(-2, 3):
            for t, tile in enumerate(shift_tiles(parts, e, d1)):
                gy[e + 2, q, :, cols(t)] = tile
        hid[q] = hidden

    def hidden_rows(s, _):
        lag = 3
        dots = {}
        for u in range(LONG + lag):
            q = RIM // 2 + s * LONG + u
            if u < LONG:
                dots[u] = hidden_dots(q)
            if u >= lag:
                hidden_values(q - lag, *dots.pop(u - lag))
        return 0

    lax.fori_loop(0, (ROWS + RIM) // LONG, hidden_rows, 0)

    def grad_rows(s, carry):
        for u in range(WIDE):
            carry = grad_row(s * WIDE + u, carry)
        return carry

    head_full = head_column(head, LANES)

    def grad_row(row, right_acc):
        q = row + RIM
        stack = jnp.concatenate([gy[b - a + 2, q - a * d1] for a in TAPS for b in TAPS], axis=0)
        grad_pair = dot(w1t[...], stack)
        left = lcol[q]
        spread = []
        for t, mask in enumerate(masks(q)):
            g = vga[q, t, 2:3, :]
            part = jnp.where(mask, grad_pair[:, cols(t)] + head_full * g, 0.0)
            parts_of[row, :, cols(t)] = part
            spread.append(pltpu.roll(part * left, row, 1))
        zero = jnp.zeros((16, LANES), F32)
        return tuple(
            r + jnp.where(lane < row, b, a)
            for r, b, a in zip(right_acc, [zero] + spread, spread + [zero])
        )

    right_terms = lax.fori_loop(
        0, ROWS // WIDE, grad_rows, (jnp.zeros((16, LANES), F32),) * (TILES + 1)
    )

    for d in range(1, REACH + 1):
        piece = right_terms[d // 2]
        rsend[d] = pltpu.roll(piece, ROWS, 1) if d % 2 else piece
    first_copy = 5 + BEHIND
    rights = [
        copy(first_copy + d, rsend.at[d], rrecv.at[d], hop(me, d), half)
        for d in range(1, REACH + 1)
    ]

    def left_rows(s, left_acc):
        for u in range(WIDE):
            row = s * WIDE + u
            prods = [
                parts_of[row, :, cols(t)] * band[row + 2 * RIM, :, cols(t)] for t in range(TILES)
            ]
            total = (prods[0] + prods[1]) + (prods[2] + prods[3])
            left_acc = jnp.where(lane == row, jnp.sum(total, axis=1, keepdims=True), left_acc)
        return left_acc

    left_grad = lax.fori_loop(0, ROWS // WIDE, left_rows, jnp.zeros((16, LANES), F32))

    def weight_rows(s, weight_acc):
        for u in range(WIDE):
            q = RIM + s * WIDE + u
            taken = [gy[b - a + 2, q - a * d1] for a in TAPS for b in TAPS]
            weight_acc = weight_acc + dot(
                jnp.concatenate(taken + [tap_rows(q)], axis=0),
                jnp.concatenate([px[2, q], hid[q]], axis=0),
                LAST,
            )
        return weight_acc

    acc[...] = jnp.zeros((256, LANES), F32)
    acc[:168, :32] = lax.fori_loop(
        0, ROWS // WIDE, weight_rows, jnp.zeros((168, 32), F32)
    )
    turned = acc[...].T

    swap_copy = first_copy + REACH + 1
    for c in rights:
        c.wait()
    right = right_terms[0]
    for d in range(1, REACH + 1):
        right = right + rrecv[d]
    right = jnp.where(lane < ROWS, right, 0.0)
    lrsend[...] = jnp.concatenate([left_grad, right], axis=0).astype(BF16)
    trade = copy(swap_copy + 1, lrsend, lrrecv, me, other)

    part = dot(lrsend[:, :ROWS], full[...])
    for j in range(GROUP):
        r = 8 * (j // 4)
        buf[j, 0:8, :] = part[r : r + 8, cols(j % 4)]
        if j < 4:
            r = 8 * (j // 2)
            buf[j, 8:16, :] = turned[r : r + 8, cols(j % 2)]
        elif j < 6:
            r = 8 * (j - 2)
            buf[j, 8:16, :] = turned[r : r + 8, cols(1)]
        else:
            buf[j, 8:16, :] = jnp.zeros((8, LANES), F32)
    group_copy = swap_copy + 1
    stage = []
    for s in range(1, GROUP):
        target = lax.rem(place + s, GROUP)
        stage.append(copy(group_copy + s, buf.at[target], arecv.at[s], base + target, half))

    def head_rows_of(s, _):
        for u in range(BATCH):
            q = RIM // 2 + s * BATCH + u
            out = dot(zw[...], jnp.concatenate([hid[q], px[2, q]], axis=0))
            for t in range(TILES):
                z[q, t] = out[:, cols(t)]
        return 0

    lax.fori_loop(0, (ROWS + RIM) // BATCH, head_rows_of, 0)

    def align_rows(s, _):
        for u in range(BATCH):
            row = s * BATCH + u
            for n, a in enumerate(TAPS):
                for t in range(TILES):
                    zs[n, t, pl.ds(pl.multiple_of(row * 16, 16), 16), :] = z[row + RIM + a * d2, t]
        return 0

    lax.fori_loop(0, ROWS // BATCH, align_rows, 0)

    def tap_sum(t, a, row):
        return zs[a + 1, t, pl.ds(row, ROWS, stride=16), :]

    total = None
    for e in range(-2, 3):
        parts = [
            sum(tap_sum(t, a, (a + 1) * 3 + a + e + 1) for a in TAPS if -1 <= a + e <= 1)
            for t in range(TILES)
        ]
        parts = shift_tiles(parts, -e, d2)
        total = parts if total is None else [x + y for x, y in zip(total, parts)]
    own_lane = ids((ROWS, LANES), 1)
    for t in range(TILES):
        second = jnp.where(own_lane < edge[t, RIM : RIM + ROWS, :], total[t], 0.0)
        csend[:, cols(t)] = (tap_sum(t, 0, 9) + second).astype(BF16)
    swap = copy(swap_copy, csend, crecv, me, other)

    total = buf[place]
    for s, c in enumerate(stage):
        c.wait()
        total = total + arecv[s + 1]
    brecv[plane] = total

    def plane_copy(s, index, target):
        return pltpu.make_async_remote_copy(
            src_ref=brecv.at[index], dst_ref=brecv.at[index],
            send_sem=plane_send.at[s], recv_sem=plane_recv.at[index],
            device_id={"chrom": target * GROUP + place, "chan": half}, device_id_type=MESH,
        )

    planes = [(s, lax.rem(plane + s, PLANES)) for s in far_first]
    for s, p in planes:
        plane_copy(s, plane, p).start()

    for s, p in planes:
        plane_copy(s, plane, p).wait_send()
        plane_copy(s, p, p).wait_recv()
    total = brecv[0]
    for p in range(1, PLANES):
        total = total + brecv[p]
    fin[place] = total * scale

    def last_copy(s, index, target):
        return pltpu.make_async_remote_copy(
            src_ref=fin.at[index], dst_ref=fin.at[index],
            send_sem=last_send.at[s], recv_sem=last_recv.at[index],
            device_id={"chrom": base + target, "chan": half}, device_id_type=MESH,
        )

    others = [(s, lax.rem(place + s, GROUP)) for s in range(1, GROUP)]
    for s, p in others:
        last_copy(s, place, p).start()
    emb_copy.wait_send()
    w_copy.wait()
    trade.wait()
    both = jnp.concatenate([lrsend[...], lrrecv[...]], axis=0)
    weights = jnp.concatenate([wt[:, mine], wother[...]], axis=0)
    emb_grad[...] = dot(both, weights, FIRST)[:ROWS].astype(BF16)
    swap.wait()
    contacts[...] = csend[...].astype(F32) + crecv[...].astype(F32)

    for s, p in others:
        last_copy(s, place, p).wait_send()
        last_copy(s, p, p).wait_recv()


def band_call(scale, *operands):
    v = pl.BlockSpec(memory_space=pltpu.VMEM)
    copies = 5 + BEHIND + REACH + 3 + GROUP
    dma = pltpu.SemaphoreType.DMA
    return pl.pallas_call(
        functools.partial(band_kernel, scale),
        out_shape=(
            jax.ShapeDtypeStruct((ROWS, OFF), F32),
            jax.ShapeDtypeStruct((ROWS, 256), BF16),
            jax.ShapeDtypeStruct((GROUP, 16, LANES), F32),
        ),
        in_specs=[pl.BlockSpec(memory_space=pltpu.HBM)] * 9,
        out_specs=[v] * 3,
        scratch_shapes=[
            pltpu.SMEM((8,), jnp.int32),
            pltpu.SMEM((2,), jnp.int32),
            pltpu.SMEM((16,), F32),
            pltpu.VMEM((32, 512), BF16),
            pltpu.VMEM((32, 256), BF16),
            pltpu.VMEM((9, 16, 16), BF16),
            pltpu.VMEM((9, 16, 16), BF16),
            pltpu.VMEM((16, 144), BF16),
            pltpu.VMEM((16, 144), BF16),
            pltpu.VMEM((16, 24), BF16),
            pltpu.VMEM((16, 32), BF16),
            pltpu.VMEM((ROWS, 512), BF16),
            pltpu.VMEM((BEHIND + 2, 16, LANES), F32),
            pltpu.VMEM((SLAB, OFF), BF16),
            pltpu.VMEM((16, OFF + LANES), F32),
            pltpu.VMEM((16, LANES), F32),
            pltpu.VMEM((SLAB, 16, LANES), F32),
            pltpu.VMEM((TILES, SLAB, LANES), jnp.int32),
            pltpu.VMEM((SLAB, TILES, 8, LANES), F32),
            pltpu.VMEM((SLAB + 2 * RIM + BATCH, 16, OFF), F32),
            pltpu.VMEM((5, SLAB, 16, OFF), BF16),
            pltpu.VMEM((5, SLAB, 16, OFF), BF16),
            pltpu.VMEM((SLAB, 16, OFF), BF16),
            pltpu.VMEM((ROWS, 16, OFF), F32),
            pltpu.VMEM((SLAB, TILES, 16, LANES), F32),
            pltpu.VMEM((3, TILES, ROWS * 16, LANES), F32),
            pltpu.VMEM((256, LANES), F32),
            pltpu.VMEM((ROWS, OFF), BF16),
            pltpu.VMEM((ROWS, OFF), BF16),
            pltpu.VMEM((REACH + 1, 16, LANES), F32),
            pltpu.VMEM((REACH + 1, 16, LANES), F32),
            pltpu.VMEM((32, LANES), BF16),
            pltpu.VMEM((32, LANES), BF16),
            pltpu.VMEM((GROUP, 16, LANES), F32),
            pltpu.VMEM((GROUP, 16, LANES), F32),
            pltpu.VMEM((PLANES, 16, LANES), F32),
            dma((9,)),
            dma((copies,)),
            dma((copies,)),
            dma((PLANES,)),
            dma((PLANES,)),
            dma((GROUP,)),
            dma((GROUP,)),
        ],
        compiler_params=pltpu.CompilerParams(
            collective_id=0, has_side_effects=True, vmem_limit_bytes=56 * 1024 * 1024
        ),
    )(*operands)


def output_kernel(
    head, fin, second_w, contacts_in, emb_grad_in,
    contacts, emb_grad, left_grad, right_grad, first_grad, second_grad, head_grad, wide,
):
    contacts[...] = contacts_in[...]
    emb_grad[...] = emb_grad_in[...]
    for j in range(GROUP):
        out = left_grad if j < 8 else right_grad
        r = 8 * ((j // 4) % 2)
        out[r : r + 8, cols(j % 4)] = fin[j, 0:8, :]
    wide[...] = jnp.zeros((LANES, 3 * LANES), F32)
    for j in range(4):
        r = 8 * (j // 2)
        wide[r : r + 8, cols(j % 2)] = fin[j, 8:16, :]
    wide[0:8, cols(2)] = fin[4, 8:16, :]
    wide[8:16, cols(2)] = fin[5, 8:16, :]
    turned = wide[...].T
    head_sum = wide[0:16, 154:155]
    head16 = head_column(head, 16)
    sums = jnp.zeros((16, 16), F32)
    for ab in range(9):
        a, b = ab // 3, ab % 3
        first_grad[ab] = turned[16 * ab : 16 * ab + 16, :16]
        row = 2 * LANES + 16 + 8 * a + (b - a + 2)
        moved = 0.5 * turned[row : row + 1, :16]
        second_grad[ab] = head16 * moved
        sums = sums + second_w[ab].astype(F32) * moved
    total = head_sum + jnp.sum(sums, axis=1, keepdims=True)
    head_grad[...] = diagonal(jnp.broadcast_to(total, (16, 16)), 16)


def output_call(head, fin, second_w, contacts, emb_grad):
    v = pl.BlockSpec(memory_space=pltpu.VMEM)
    m = pl.BlockSpec(memory_space=pltpu.SMEM)
    return pl.pallas_call(
        output_kernel,
        out_shape=(
            jax.ShapeDtypeStruct((ROWS, OFF), F32),
            jax.ShapeDtypeStruct((ROWS, 256), BF16),
            jax.ShapeDtypeStruct((16, 512), F32),
            jax.ShapeDtypeStruct((16, 512), F32),
            jax.ShapeDtypeStruct((9, 16, 16), F32),
            jax.ShapeDtypeStruct((9, 16, 16), F32),
            jax.ShapeDtypeStruct((1, 16), F32),
        ),
        in_specs=[m] + [v] * 4,
        out_specs=[v] * 7,
        scratch_shapes=[pltpu.VMEM((LANES, 3 * LANES), F32)],
    )(head, fin, second_w, contacts, emb_grad)


def on_device(
    embeddings,
    w_left,
    w_right,
    first_conv_weight,
    second_conv_weight,
    head_weight,
    cotangent,
    dilations,
    chrom_ends,
):
    bin_total = embeddings.shape[0] * lax.axis_size("chrom")
    scale = 1.0 / math.sqrt(bin_total * OFF)
    first_w = jnp.transpose(first_conv_weight, (1, 2, 0, 3)).reshape(9, 16, 16)
    second_w = jnp.transpose(second_conv_weight, (1, 2, 0, 3)).reshape(9, 16, 16)
    contacts, emb_grad, fin = band_call(
        scale, chrom_ends, dilations, head_weight, embeddings, w_left.T, w_right.T,
        first_w, second_w, cotangent,
    )
    contacts, emb_grad, left_grad, right_grad, first_grad, second_grad, head_grad = output_call(
        head_weight, fin, second_w, contacts, emb_grad
    )
    return (
        contacts,
        emb_grad,
        left_grad.T,
        right_grad.T,
        jnp.transpose(first_grad.reshape(3, 3, 16, 16), (2, 0, 1, 3)),
        jnp.transpose(second_grad.reshape(3, 3, 16, 16), (2, 0, 1, 3)),
        head_grad.reshape(16),
    )


def solution(mesh):
    in_specs = (
        P("chrom", "chan"),
        P(None, "chan"),
        P(None, "chan"),
        P("chan", None, None, None),
        P("chan", None, None, None),
        P("chan"),
        P("chrom", None),
        P(),
        P(),
    )
    out_specs = (
        P("chrom", None),
        P("chrom", "chan"),
        P(None, "chan"),
        P(None, "chan"),
        P("chan", None, None, None),
        P("chan", None, None, None),
        P("chan"),
    )
    return jax.shard_map(
        on_device, mesh=mesh, in_specs=in_specs, out_specs=out_specs, check_vma=False
    )
```
